512 devices in a mesh: slab: 32 (over x_lo, z, core), plane: 16 (over y, x_hi).
Axes of the slice: x: 4 (x_hi: 2, x_lo: 2; x = x_hi * 2 + x_lo), y: 8, z: 8, core: 2. Of those that a mesh axis runs over, the one named last changes fastest.
Arguments:
- positions: float32 [32, 16, 3, 64], P('slab', 'plane'), as said below
- species: int32 [32, 16, 64], P('slab', 'plane'), may hold values from 0 to 88
- slab_sends: int32 [32, 16, 2, 32], P('slab', 'plane'), may hold values from 0 to 63, as said below
- plane_sends: int32 [32, 16, 2, 64], P('slab', 'plane'), may hold values from 0 to 127, as said below
- edges: int32 [32, 16, 2, 1536], P('slab', 'plane'), may hold values from 0 to 255, as said below
- edge_count: int32 [32, 16], P('slab', 'plane'), may hold values from 384 to 1536, as said below
- embed_table: float32 [89, 128], replicated, may hold values from -6 to 6
- atom_ref: float32 [89], replicated, may hold values from -8 to -1
- radial_one: float32 [2, 8, 64], replicated, may hold values from -2 to 2
- radial_two: float32 [2, 64, 64], replicated, may hold values from -0.75 to 0.75
- radial_three: float32 [2, 64, 64], replicated, may hold values from -0.75 to 0.75
- radial_four: float32 [2, 64, 384], replicated, may hold values from -0.75 to 0.75
- up_weight: float32 [2, 128, 128], replicated, may hold values from -0.5 to 0.5
- skip_weight: float32 [2, 128, 128], replicated, may hold values from -0.5 to 0.5
- out_weight: float32 [2, 128, 128], replicated, may hold values from -0.5 to 0.5
- prod_weight: float32 [2, 4, 128], replicated, may hold values from -4 to 4
- read_one: float32 [128], replicated, may hold values from -0.5 to 0.5
- read_hidden: float32 [128, 16], replicated, may hold values from -0.5 to 0.5
- read_out: float32 [16], replicated, may hold values from -1.5 to 1.5
Outputs:
- atom_energy: float32 [32, 16, 64], P('slab', 'plane')
- forces: float32 [32, 16, 3, 64], P('slab', 'plane')
The draws below stay inside these ranges and needn't reach their ends.
Inputs may be any that keep to these rules, and one draw needn't show every extreme that they name: `positions`: each domain is a box of 4 x 2 x 2 cells of side 3 in its own frame, with 4 atoms in every cell, and no two atoms closer than 0.9; the owned slots hold the atoms in a random order. `slab_sends`: row 0 lists the owned slots of the atoms in the cells of the highest z layer, row 1 those of the lowest z layer, both in the same order of cells and atoms. `plane_sends`: row 0 lists the atoms of the cells of the highest y layer, row 1 those of the lowest y layer, over the z layers of the owned cells and of the slab ghosts on both sides, as slots of the first 128 extended rows. Senders are extended slots and receivers owned slots. Live edges join atoms of the same or adjacent cells (never across the x ends of a box, never to slab ghost rows that a boundary domain lacks), are grouped by receiver in order of owned slot, with equally many per owned atom in one domain; slots past edge_count hold zeros. `edge_count`: A multiple of 64; the domains of the lowest eighth of the slab (at least one) are full.
All inputs are finite; a program needn't handle non-finite values.
Results may differ from the reference program's by a relative error of at most 0.0003.
Values sent between devices are 32-bit elements; how exact they have to be, the bound alone decides.
No kernel may reach another device: no remote copies, remote signals or barrier semaphores. Data moves between devices by JAX's collectives and lax.ppermute only.
A program may use at most 64 MiB of HBM per device.

```python
import math
import jax
import jax.numpy as jnp
import numpy as np
from jax import lax

C = 128
RADIAL = 64
SPECIES = 89
READ = 16
NBASIS = 8
LAYERS = 2
CELLS_X = 4
CELLS_Y = 2
CELLS_Z = 2
PER_CELL = 4
NB_MAX = 24
ATOMS = 64
SLAB_GHOSTS = 32
PLANE_GHOSTS = 64
EDGES_DEV = 1536
N_SLAB = 32
N_PLANE = 16


cell_side = 3.0


def lattice(key):
    keys = jax.random.split(jax.random.fold_in(key, 101), N_SLAB * N_PLANE)
    orders = jax.vmap(lambda device_key: jax.random.permutation(device_key, ATOMS))(keys)
    return orders.reshape(N_SLAB, N_PLANE, ATOMS).astype(jnp.int32)


def neighbour_counts(key):
    spread = jax.random.randint(jax.random.fold_in(key, 202), (N_SLAB, N_PLANE), NB_MAX // 4, NB_MAX // 2 + 1)
    electrode = jnp.arange(N_SLAB)[:, None] < max(1, N_SLAB // 8)
    return jnp.where(electrode, NB_MAX, spread).astype(jnp.int32)


def draw_positions(key, part):
    slots = lattice(key)
    key = jax.random.fold_in(key, 1)
    canonical_index = jnp.arange(ATOMS)
    member = canonical_index % PER_CELL
    cell_index = canonical_index // PER_CELL
    cell_z = cell_index % CELLS_Z
    cell_y = cell_index // CELLS_Z % CELLS_Y
    cell_x = cell_index // (CELLS_Z * CELLS_Y)
    centre = jnp.stack([cell_x + 0.25 + 0.5 * (member % 2), cell_y + 0.25 + 0.5 * (member // 2), cell_z + 0.5 + 0.0 * member], axis=0).astype(jnp.float32) * cell_side
    shape_all = (N_SLAB, N_PLANE, 3, ATOMS)
    jitter = jax.random.uniform(key, shape_all, jnp.float32, minval=-1.0, maxval=1.0)
    reach = jnp.array([0.1, 0.1, 0.3], jnp.float32) * cell_side
    canonical = centre[None, None] + jitter * reach[None, None, :, None]

    def place(values_in, order):
        return jnp.zeros_like(values_in).at[:, order].set(values_in)
    return jax.vmap(jax.vmap(place))(canonical, slots).astype(jnp.float32)


def draw_slab_sends(key, part):
    slots = lattice(key)
    key = jax.random.fold_in(key, 2)
    entry = jnp.arange(SLAB_GHOSTS)
    member = entry % PER_CELL
    column = entry // PER_CELL
    cell_y = column % CELLS_Y
    cell_x = column // CELLS_Y
    top_face = ((cell_x * CELLS_Y + cell_y) * CELLS_Z + CELLS_Z - 1) * PER_CELL + member
    bottom_face = (cell_x * CELLS_Y + cell_y) * CELLS_Z * PER_CELL + member
    return jnp.stack([slots[:, :, top_face], slots[:, :, bottom_face]], axis=2).astype(jnp.int32)


def draw_plane_sends(key, part):
    slots = lattice(key)
    key = jax.random.fold_in(key, 3)
    entry = jnp.arange(PLANE_GHOSTS)
    member = entry % PER_CELL
    column = entry // PER_CELL
    cell_x = column % CELLS_X
    layer_z = column // CELLS_X - 1
    clipped = jnp.clip(layer_z, 0, CELLS_Z - 1)

    def face(cell_y):
        own_slot = slots[:, :, ((cell_x * CELLS_Y + cell_y) * CELLS_Z + clipped) * PER_CELL + member]
        slab_slot = (cell_x * CELLS_Y + cell_y) * PER_CELL + member
        return jnp.where(layer_z < 0, ATOMS + slab_slot, jnp.where(layer_z >= CELLS_Z, ATOMS + SLAB_GHOSTS + slab_slot, own_slot))
    return jnp.stack([face(CELLS_Y - 1), face(0)], axis=2).astype(jnp.int32)


def draw_edge_count(key, part):
    counts = neighbour_counts(key)
    key = jax.random.fold_in(key, 5)
    return (counts * ATOMS).astype(jnp.int32)


def draw_edges(key, part):
    slots = lattice(key)
    counts = neighbour_counts(key)
    key = jax.random.fold_in(key, 4)
    candidates = 27 * PER_CELL
    canonical_index = jnp.arange(ATOMS)
    member = canonical_index % PER_CELL
    cell_index = canonical_index // PER_CELL
    cell_z = cell_index % CELLS_Z
    cell_y = cell_index // CELLS_Z % CELLS_Y
    cell_x = cell_index // (CELLS_Z * CELLS_Y)
    choice_index = jnp.arange(candidates)
    other_member = choice_index % PER_CELL
    stencil = choice_index // PER_CELL
    step_x = stencil // 9 - 1
    step_y = stencil // 3 % 3 - 1
    step_z = stencil % 3 - 1
    near_x = cell_x[:, None] + step_x[None, :]
    near_y = cell_y[:, None] + step_y[None, :]
    near_z = cell_z[:, None] + step_z[None, :]
    near_member = jnp.broadcast_to(other_member[None, :], near_x.shape)
    safe_x = jnp.clip(near_x, 0, CELLS_X - 1)
    safe_y = jnp.clip(near_y, 0, CELLS_Y - 1)
    safe_z = jnp.clip(near_z, 0, CELLS_Z - 1)
    own_canon = ((safe_x * CELLS_Y + safe_y) * CELLS_Z + safe_z) * PER_CELL + near_member
    slab_slot = (safe_x * CELLS_Y + safe_y) * PER_CELL + near_member
    plane_slot = ((near_z + 1) * CELLS_X + safe_x) * PER_CELL + near_member
    itself = (step_x[None, :] == 0) & (step_y[None, :] == 0) & (step_z[None, :] == 0) & (near_member == member[:, None])
    base_valid = (near_x >= 0) & (near_x < CELLS_X) & jnp.logical_not(itself)
    slab_place = jnp.arange(N_SLAB)[:, None, None, None]
    valid = base_valid[None, None] & ((near_z >= 0)[None, None] | (slab_place > 0)) & ((near_z < CELLS_Z)[None, None] | (slab_place < N_SLAB - 1))
    own_index = slots[:, :, own_canon]
    target = jnp.where(near_y < 0, ATOMS + 2 * SLAB_GHOSTS + plane_slot, jnp.where(near_y >= CELLS_Y, ATOMS + 2 * SLAB_GHOSTS + PLANE_GHOSTS + plane_slot, jnp.where(near_z < 0, ATOMS + slab_slot, jnp.where(near_z >= CELLS_Z, ATOMS + SLAB_GHOSTS + slab_slot, own_index))))
    target = jnp.broadcast_to(target, (N_SLAB, N_PLANE, ATOMS, candidates))
    scores = jax.random.randint(key, (N_SLAB, N_PLANE, ATOMS, candidates), 0, 2 ** 20) * 128 + choice_index
    scores = jnp.where(valid, scores, scores + 2 ** 28)
    ranking = jnp.argsort(scores, axis=-1)
    chosen = jnp.take_along_axis(target, ranking[..., :NB_MAX], axis=-1)
    inverse = jnp.argsort(slots, axis=-1)
    by_slot = jnp.take_along_axis(chosen, inverse[..., None], axis=2)
    neighbour_slot = jnp.arange(NB_MAX)
    owned_slot = jnp.arange(ATOMS)
    per_atom = counts[:, :, None, None]
    placing = jnp.where(neighbour_slot[None, None, None, :] < per_atom, owned_slot[None, None, :, None] * per_atom + neighbour_slot[None, None, None, :], EDGES_DEV)

    def fill(place_row, values_in):
        return jnp.zeros((EDGES_DEV,), jnp.int32).at[place_row.reshape(-1)].set(values_in.reshape(-1).astype(jnp.int32), mode='drop')
    senders = jax.vmap(jax.vmap(fill))(placing, by_slot)
    receivers = jax.vmap(jax.vmap(fill))(placing, jnp.broadcast_to(owned_slot[None, None, :, None], placing.shape))
    return jnp.stack([senders, receivers], axis=2).astype(jnp.int32)


def set_ends(values, stream_key, least, high):
    longest = values.shape.index(max(values.shape))
    spots = []
    for shift in (0, 1):
        where = [jax.random.randint(jax.random.fold_in(stream_key, axis), (), 0, length) for axis, length in enumerate(values.shape)]
        where[longest] = (where[longest] + shift) % values.shape[longest]
        spots.append(tuple(where))
    return values.at[spots[0]].set(least).at[spots[1]].set(high)


def rank_bounds(count, skew):
    loads = [(1 << 20) // math.isqrt(grade ** skew) + 1 for grade in range(1, count + 1)]
    deviation = 1 + sum(loads) // (1 << 30)
    return np.cumsum(np.array([max(1, weight // deviation) for weight in loads]))


def ranked_ids(own_key, dims, number_of, lean):
    listing = rank_bounds(number_of, lean)
    lot = jax.random.randint(jax.random.fold_in(own_key, 1), dims, 0, int(listing[number_of - 1]))
    standing = jnp.searchsorted(jnp.asarray(listing, jnp.int32), lot, side="right")
    return jax.random.permutation(jax.random.fold_in(own_key, 2), number_of)[standing].astype(jnp.int32)


def scatter_about(stream_key, shape, scale, limit, kind=jnp.bfloat16):
    return jnp.clip(scale * jax.random.normal(stream_key, shape, jnp.float32), -limit, limit).astype(kind)


def setup_inputs(seed: int = 0) -> dict:
    arg_keys = jax.random.split(jax.random.key(seed), 20)
    return {
        "positions": draw_positions(jax.random.fold_in(arg_keys[19], 71), 0),
        "species": set_ends(ranked_ids(arg_keys[1], (N_SLAB, N_PLANE, ATOMS), SPECIES, 2), jax.random.fold_in(arg_keys[1], 3), 0, SPECIES - 1).astype(jnp.int32),
        "slab_sends": draw_slab_sends(jax.random.fold_in(arg_keys[19], 71), 0),
        "plane_sends": draw_plane_sends(jax.random.fold_in(arg_keys[19], 71), 0),
        "edges": draw_edges(jax.random.fold_in(arg_keys[19], 71), 0),
        "edge_count": draw_edge_count(jax.random.fold_in(arg_keys[19], 71), 0),
        "embed_table": scatter_about(arg_keys[6], (SPECIES, C), 1.0, 6.0, jnp.float32),
        "atom_ref": jnp.clip(jax.random.uniform(arg_keys[7], (SPECIES,), jnp.float32, -8.0, -1.0), -8.0, -1.0),
        "radial_one": scatter_about(arg_keys[8], (LAYERS, NBASIS, RADIAL), NBASIS ** -0.5, 2.0, jnp.float32),
        "radial_two": scatter_about(arg_keys[9], (LAYERS, RADIAL, RADIAL), RADIAL ** -0.5, 0.75, jnp.float32),
        "radial_three": scatter_about(arg_keys[10], (LAYERS, RADIAL, RADIAL), RADIAL ** -0.5, 0.75, jnp.float32),
        "radial_four": scatter_about(arg_keys[11], (LAYERS, RADIAL, 3 * C), RADIAL ** -0.5, 0.75, jnp.float32),
        "up_weight": scatter_about(arg_keys[12], (LAYERS, C, C), C ** -0.5, 0.5, jnp.float32),
        "skip_weight": scatter_about(arg_keys[13], (LAYERS, C, C), C ** -0.5, 0.5, jnp.float32),
        "out_weight": scatter_about(arg_keys[14], (LAYERS, C, C), C ** -0.5, 0.5, jnp.float32),
        "prod_weight": scatter_about(arg_keys[15], (LAYERS, 4, C), 1.0, 4.0, jnp.float32),
        "read_one": scatter_about(arg_keys[16], (C,), C ** -0.5, 0.5, jnp.float32),
        "read_hidden": scatter_about(arg_keys[17], (C, READ), C ** -0.5, 0.5, jnp.float32),
        "read_out": scatter_about(arg_keys[18], (READ,), READ ** -0.5, 1.5, jnp.float32),
    }


cutoff_radius = 5.0
cell_side = 3.0
inverse_neighbours = 0.2
highest = lax.Precision.HIGHEST

def matmul(left_side, right_side):
    return jnp.dot(left_side, right_side, precision=highest, preferred_element_type=jnp.float32)

def harmonics(direction):
    along_x = direction[:, 0]
    along_y = direction[:, 1]
    along_z = direction[:, 2]
    root_three = 3.0 ** 0.5
    root_five = 5.0 ** 0.5
    root_fifteen = 15.0 ** 0.5
    return jnp.stack([jnp.ones_like(along_x), root_three * along_x, root_three * along_y, root_three * along_z, root_fifteen * along_x * along_y, root_fifteen * along_y * along_z, 0.5 * root_five * (3.0 * along_z * along_z - 1.0), root_fifteen * along_x * along_z, 0.5 * root_fifteen * (along_x * along_x - along_y * along_y)], axis=1)

def radial(distance, weights):
    first_layer, second_layer, third_layer, fourth_layer = weights
    scaled = distance / cutoff_radius
    wavenumbers = jnp.arange(1, first_layer.shape[0] + 1).astype(jnp.float32) * jnp.pi
    bessel = (2.0 / cutoff_radius) ** 0.5 * jnp.sin(wavenumbers[None, :] * scaled[:, None]) / distance[:, None]
    polynomial = 1.0 - 28.0 * scaled ** 6 + 48.0 * scaled ** 7 - 21.0 * scaled ** 8
    envelope = jnp.where(scaled < 1.0, polynomial, 0.0)
    hidden = jax.nn.silu(matmul(bessel, first_layer))
    hidden = jax.nn.silu(matmul(hidden, second_layer))
    hidden = jax.nn.silu(matmul(hidden, third_layer))
    return matmul(hidden, fourth_layer) * envelope[:, None]

def aggregate(pos_ext, lifted, senders, receivers, live_mask, weights, owned_rows):
    vector = pos_ext[senders] - pos_ext[receivers]
    far_point = jnp.array([2.0 * cutoff_radius, 0.0, 0.0], jnp.float32)
    vector = jnp.where(live_mask[:, None] > 0.5, vector, far_point[None, :])
    distance = jnp.sqrt(lax.optimization_barrier(jnp.sum(vector * vector, axis=1)))
    channels = lifted.shape[1]
    shaped = (radial(distance, weights) * live_mask[:, None]).reshape(-1, 3, channels)
    edge_total = shaped.shape[0]
    expanded = jnp.concatenate([shaped[:, 0:1, :], jnp.broadcast_to(shaped[:, 1:2, :], (edge_total, 3, channels)), jnp.broadcast_to(shaped[:, 2:3, :], (edge_total, 5, channels))], axis=1)
    message = expanded * harmonics(vector / distance[:, None])[:, :, None] * lifted[senders][:, None, :]
    summed = jnp.zeros((owned_rows, 9, channels), jnp.float32).at[receivers].add(message)
    return summed * inverse_neighbours

def update(amplitude, previous, product_gain, skip_matrix, out_matrix):
    scalar_part = amplitude[:, 0, :]
    vector_part = lax.optimization_barrier(jnp.sum(amplitude[:, 1:4, :] ** 2, axis=1))
    tensor_part = lax.optimization_barrier(jnp.sum(amplitude[:, 4:9, :] ** 2, axis=1))
    mixture = product_gain[0] * scalar_part + product_gain[1] * vector_part + product_gain[2] * tensor_part + product_gain[3] * scalar_part * scalar_part
    return matmul(previous, skip_matrix) + matmul(mixture, out_matrix)

def take_rows(row_values, indices):
    return jnp.take_along_axis(row_values, indices[:, :, :, None], axis=2)

def extend(row_values, slab_sends, plane_sends, shifted_frame):
    upward = take_rows(row_values, slab_sends[:, :, 0])
    downward = take_rows(row_values, slab_sends[:, :, 1])
    empty_rows = jnp.zeros_like(upward[:1])
    below_rows = jnp.concatenate([empty_rows, upward[:-1]], axis=0)
    above_rows = jnp.concatenate([downward[1:], empty_rows], axis=0)
    if shifted_frame:
        slab_offset = jnp.array([0.0, 0.0, CELLS_Z * cell_side], jnp.float32)
        below_rows = below_rows - slab_offset
        above_rows = above_rows + slab_offset
    middle = jnp.concatenate([row_values, below_rows, above_rows], axis=2)
    leftward = jnp.roll(take_rows(middle, plane_sends[:, :, 0]), 1, axis=1)
    rightward = jnp.roll(take_rows(middle, plane_sends[:, :, 1]), -1, axis=1)
    if shifted_frame:
        plane_offset = jnp.array([0.0, CELLS_Y * cell_side, 0.0], jnp.float32)
        leftward = leftward - plane_offset
        rightward = rightward + plane_offset
    return jnp.concatenate([middle, leftward, rightward], axis=2)

def reference(positions, species, slab_sends, plane_sends, edges, edge_count, embed_table, atom_ref, radial_one, radial_two, radial_three, radial_four, up_weight, skip_weight, out_weight, prod_weight, read_one, read_hidden, read_out):
    onehot = (species[:, :, :, None] == jnp.arange(SPECIES)[None, None, None, :]).astype(jnp.float32)
    start_features = jnp.einsum('pqas,sc->pqac', onehot, embed_table, precision=highest)
    start_ext = extend(start_features, slab_sends, plane_sends, False)
    live_mask = (jnp.arange(EDGES_DEV)[None, None, :] < edge_count[:, :, None]).astype(jnp.float32)

    def flatten(values_in):
        return values_in.reshape((N_SLAB * N_PLANE,) + values_in.shape[2:])

    def interaction(depth, pos_ext, feat_ext, feat_own):
        weights = (radial_one[depth], radial_two[depth], radial_three[depth], radial_four[depth])

        def one_device(operands):
            position_rows, feature_rows, own_rows, edge_pairs, mask_row = operands
            lifted = matmul(feature_rows, up_weight[depth])
            amplitude = aggregate(position_rows, lifted, edge_pairs[0], edge_pairs[1], mask_row, weights, ATOMS)
            return update(amplitude, own_rows, prod_weight[depth], skip_weight[depth], out_weight[depth])
        result = lax.map(jax.checkpoint(one_device), (flatten(pos_ext), flatten(feat_ext), flatten(feat_own), flatten(edges), flatten(live_mask)))
        return result.reshape(N_SLAB, N_PLANE, ATOMS, -1)

    def energy_terms(coordinates):
        pos_ext = extend(jnp.swapaxes(coordinates, 2, 3), slab_sends, plane_sends, True)
        first_features = interaction(0, pos_ext, start_ext, start_features)
        first_ext = extend(first_features, slab_sends, plane_sends, False)
        second_features = interaction(1, pos_ext, first_ext, first_features)
        reference_part = jnp.einsum('pqas,s->pqa', onehot, atom_ref, precision=highest)
        first_part = jnp.einsum('pqac,c->pqa', first_features, read_one, precision=highest)
        hidden = jnp.einsum('pqac,ch->pqah', second_features, read_hidden, precision=highest)
        second_part = jnp.einsum('pqah,h->pqa', jax.nn.silu(hidden), read_out, precision=highest)
        energies = reference_part + first_part + second_part
        return (jnp.sum(energies), energies)
    gradient, energies = jax.grad(energy_terms, has_aux=True)(positions)
    return (energies, -gradient)
```

```python
import functools

import jax
import jax.numpy as jnp
from jax import lax
from jax.experimental import pallas as pl
from jax.experimental.pallas import tpu as pltpu
from jax.sharding import PartitionSpec as P

CELLS_Y = 2
CELLS_Z = 2

cutoff_radius = 5.0
cell_side = 3.0
inverse_neighbours = 0.2
highest = lax.Precision.HIGHEST
f32 = jnp.float32
bf16 = jnp.bfloat16

C = 128
OWN = 64
EXT = 256
EDGES = 1536
BLOCKS = 4
GROUP = 16
SPAN = EDGES // BLOCKS
KINDS = 96
LMS = (1, 3, 5)
FIRST_LM = (0, 1, 4)
STACK_AT = (0, 48, 192)
STACK = 432
R3, R5, R15 = 3.0**0.5, 5.0**0.5, 15.0**0.5

NN = (((1,), (0,)), ((), ()))
TN = (((0,), (0,)), ((), ()))
NT = (((1,), (1,)), ((), ()))


def dot(a, b, dims=NN):
    return lax.dot_general(a, b, dims, preferred_element_type=f32)


def dot3(a, b, dims=NN):
    return lax.dot_general(a, b, dims, precision=lax.Precision.HIGH, preferred_element_type=f32)


def split(x):
    hi = x.astype(bf16)
    return hi, (x - hi.astype(f32)).astype(bf16)


def pair_lanes(x):
    hi, lo = split(x)
    return jnp.concatenate([hi, lo], axis=1)


def halves(o):
    return o[:, :C] + o[:, C:]


def stack_rows(x):
    hi, lo = split(x)
    return jnp.concatenate([hi, lo, hi], axis=0)


def three(x):
    hi = x.astype(bf16).astype(f32)
    rest = x - hi
    mid = rest.astype(bf16).astype(f32)
    return hi, mid, rest - mid


def pick_lanes(values, chooser, dims=NN):
    hi, mid, lo = three(values)
    o = dot(jnp.concatenate([hi, mid, lo, jnp.zeros_like(lo)], axis=0).astype(bf16), chooser, dims)
    return (o[0:8] + o[8:16]) + o[16:24]


def pick_rows(chooser, values):
    hi, mid, lo = three(values)
    o = dot(chooser, jnp.concatenate([hi, mid, lo], axis=1).astype(bf16))
    return (o[:, :C] + o[:, C : 2 * C]) + o[:, 2 * C :]


def silu(x):
    return x * (1.0 / (1.0 + jnp.exp(-x)))


def silu_pair(x):
    s = 1.0 / (1.0 + jnp.exp(-x))
    return x * s, s * (1.0 + x * (1.0 - s))


def span(b):
    return pl.ds(b * SPAN, SPAN)


def call(kernel, outs, args, scratch=(), flops=0, name=None):
    spec = pl.BlockSpec(memory_space=pltpu.VMEM)
    out_shape = tuple(jax.ShapeDtypeStruct(shape, dtype) for shape, dtype in outs)
    moved = sum(a.size * a.dtype.itemsize for a in args)
    return pl.pallas_call(
        kernel,
        out_shape=out_shape,
        in_specs=[spec] * len(args),
        out_specs=tuple(spec for _ in out_shape),
        scratch_shapes=list(scratch),
        compiler_params=pltpu.CompilerParams(vmem_limit_bytes=56 * 1024 * 1024),
        cost_estimate=pl.CostEstimate(flops=flops, bytes_accessed=moved, transcendentals=0),
        name=name,
    )(*args)


def pick_kernel(v_ref, s_ref, a_ref, b_ref):
    o = pick_lanes(v_ref[...], s_ref[...])
    half = a_ref.shape[1]
    a_ref[...] = o[:, :half]
    b_ref[...] = o[:, half:]


def geometry(v, valid, b_ref, db_ref, geo_ref):
    vx = jnp.where(valid, v[0:1], 2.0 * cutoff_radius)
    vy = jnp.where(valid, v[1:2], 0.0)
    vz = jnp.where(valid, v[2:3], 0.0)
    d = jnp.sqrt(vx * vx + vy * vy + vz * vz)
    inv = 1.0 / d
    geo_ref[0:1, :] = vx * inv
    geo_ref[1:2, :] = vy * inv
    geo_ref[2:3, :] = vz * inv
    geo_ref[3:4, :] = inv
    s = d / cutoff_radius
    s2 = s * s
    s4 = s2 * s2
    s5 = s4 * s
    s6 = s4 * s2
    s7 = s6 * s
    inside = (s < 1.0) & valid
    u = 1.0 - 28.0 * s6 + 48.0 * s7 - 21.0 * s4 * s4
    du = (-168.0 * s5 + 336.0 * s6 - 168.0 * s7) / cutoff_radius
    geo_ref[4:5, :] = jnp.where(inside, u * inverse_neighbours, 0.0)
    geo_ref[5:6, :] = jnp.where(inside, du * inverse_neighbours, 0.0)
    geo_ref[6:8, :] = jnp.zeros_like(geo_ref[6:8, :])
    t = (jnp.minimum(s, 1.0) - 0.5) * jnp.pi
    z = t * t
    cs = 1.0 - z * (1 / 2 - z * (1 / 24 - z * (1 / 720 - z * (1 / 40320 - z * (1 / 3628800 - z * (1 / 479001600 - z * (1 / 87178291200)))))))
    sn = 1.0 - z * (1 / 6 - z * (1 / 120 - z * (1 / 5040 - z * (1 / 362880 - z * (1 / 39916800 - z * (1 / 6227020800))))))
    s1, c1 = cs, -t * sn

    def plus(a, b):
        return a[0] * b[1] + a[1] * b[0], a[1] * b[1] - a[0] * b[0]

    w1 = (s1, c1)
    w2 = plus(w1, w1)
    w3 = plus(w2, w1)
    w4 = plus(w2, w2)
    waves = (w1, w2, w3, w4, plus(w4, w1), plus(w4, w2), plus(w4, w3), plus(w4, w4))
    gain = (2.0 / cutoff_radius) ** 0.5 * inv
    for n, (sine, cosine) in enumerate(waves):
        b_ref[n : n + 1, :] = gain * sine
        db_ref[n : n + 1, :] = gain * (cosine * ((n + 1) * jnp.pi / cutoff_radius) - sine * inv)


def basis_stack(x):
    hi, mid, _ = three(x)
    lo = x - hi
    return jnp.concatenate([hi, lo, hi, jnp.zeros_like(hi)], axis=0).astype(bf16)


def radial_block(b, w1, w2, w3, w4, gate):
    h = silu(dot(w1, basis_stack(b)))
    h = silu(dot(w2, stack_rows(h)))
    h = silu(dot(w3, stack_rows(h)))
    return dot(stack_rows(h * gate), w4, TN)


def radial_tangent_block(b, db, w1, w2, w3, w4, gate, dgate):
    h, g = silu_pair(dot(w1, basis_stack(b)))
    t = g * dot(w1, basis_stack(db))
    h, g = silu_pair(dot(w2, stack_rows(h)))
    t = g * dot(w2, stack_rows(t))
    h, g = silu_pair(dot(w3, stack_rows(h)))
    t = g * dot(w3, stack_rows(t))
    return dot(stack_rows(t * gate + h * dgate), w4, TN)


def angular_rows(geo):
    x, y, z = geo[0:1], geo[1:2], geo[2:3]
    return (
        jnp.ones_like(x),
        R3 * x,
        R3 * y,
        R3 * z,
        R15 * x * y,
        R15 * y * z,
        0.5 * R5 * (3.0 * z * z - 1.0),
        R15 * x * z,
        0.5 * R15 * (x * x - y * y),
    )


def gather_messages(b, g_ref, lifted, radial, ast_ref, l_ref, m_ref, amp_ref):
    lift = halves(dot(g_ref[span(b), :], lifted))
    l_ref[span(b), :] = lift
    for l in range(3):
        n = LMS[l]
        m = pair_lanes(radial[:, l * C : (l + 1) * C] * lift)
        m_ref[l, span(b), :] = m
        o = dot(ast_ref[pl.ds(b * STACK + STACK_AT[l], 32 * n), :], m)
        amp = halves(o[: 16 * n]) + o[16 * n :, :C]
        for k in range(n):
            amp_ref[FIRST_LM[l] + k, pl.ds(b * GROUP, GROUP), :] = amp[16 * k : 16 * (k + 1)]


def invariants(amp_ref, gain):
    b0 = amp_ref[0]
    b1 = sum(amp_ref[k] * amp_ref[k] for k in range(1, 4))
    b2 = sum(amp_ref[k] * amp_ref[k] for k in range(4, 9))
    return gain[0:1] * b0 + gain[1:2] * b1 + gain[2:3] * b2 + gain[3:4] * b0 * b0


def amp_grads(amp_ref, gain, gm, ga_ref):
    ga_ref[0] = gm * (gain[0:1] + 2.0 * gain[3:4] * amp_ref[0])
    one = gm * (2.0 * gain[1:2])
    two = gm * (2.0 * gain[2:3])
    for k in range(1, 4):
        ga_ref[k] = one * amp_ref[k]
    for k in range(4, 9):
        ga_ref[k] = two * amp_ref[k]


def group_grads(ga_ref, b, l):
    return jnp.concatenate(
        [ga_ref[FIRST_LM[l] + k, pl.ds(b * GROUP, GROUP), :] for k in range(LMS[l])], axis=0
    )


def spread(ast_ref, ga_ref, b, l):
    n = LMS[l]
    hi, lo = split(group_grads(ga_ref, b, l))
    return dot(
        ast_ref[pl.ds(b * STACK + STACK_AT[l], 48 * n), :], jnp.concatenate([hi, hi, lo], axis=0), TN
    )


def edge_forces(b, x, m_ref, ga_ref, geo, mask, gv_ref):
    gd = dot(jnp.ones((16, 2 * C), bf16), pair_lanes(x), NT)[0:1]
    gy = [None]
    for l in (1, 2):
        n = LMS[l]
        hi, lo = split(group_grads(ga_ref, b, l))
        left = jnp.concatenate(
            [jnp.concatenate([hi, hi], axis=1), jnp.concatenate([lo, jnp.zeros_like(lo)], axis=1)],
            axis=0,
        )
        w = dot(left, m_ref[l, span(b), :], NT)
        w = w[: 16 * n] + w[16 * n :]
        for k in range(n):
            gy.append(jnp.sum(mask * w[16 * k : 16 * (k + 1)], axis=0, keepdims=True))
    x, y, z, inv = geo[0:1], geo[1:2], geo[2:3], geo[3:4]
    gx = R3 * gy[1] + R15 * (y * gy[4] + z * gy[7] + x * gy[8])
    gyy = R3 * gy[2] + R15 * (x * gy[4] + z * gy[5] - y * gy[8])
    gz = R3 * gy[3] + R15 * (y * gy[5] + x * gy[7]) + (3.0 * R5) * z * gy[6]
    along = x * gx + y * gyy + z * gz
    core = gd - along * inv
    gv_ref[0:1, span(b)] = core * x + gx * inv
    gv_ref[1:2, span(b)] = core * y + gyy * inv
    gv_ref[2:3, span(b)] = core * z + gz * inv
    gv_ref[3:8, span(b)] = jnp.zeros((5, SPAN), f32)


def first_kernel(
    vext_ref, dd_ref, g_ref, mask_ref, table_ref, skip_ref, w1_ref, w2_ref, w3_ref, w4_ref,
    gain_ref, out_ref, sn_ref,
    f_ref, sl_ref, si_ref, amp_ref, l_ref, m_ref, ast_ref, b_ref, db_ref, geo_ref,
):
    valid = jnp.sum(mask_ref[...], axis=0, keepdims=True) > 0.5
    geometry(pick_lanes(vext_ref[...], dd_ref[...]), valid, b_ref, db_ref, geo_ref)
    kinds = vext_ref[3:4, :]
    onehot = (
        lax.broadcasted_iota(jnp.int32, (KINDS, EXT), 0).astype(f32) == kinds
    ).astype(f32).astype(bf16)
    lifted = dot(onehot, table_ref[...], TN).astype(bf16)
    w1, w2, w3, w4 = w1_ref[...], w2_ref[...], w3_ref[...], w4_ref[...]
    for b in range(BLOCKS):
        geo = geo_ref[:, span(b)]
        mask = mask_ref[:, span(b)]
        rows = angular_rows(geo)
        for l in range(3):
            a = jnp.concatenate(
                [mask * rows[FIRST_LM[l] + k] for k in range(LMS[l])], axis=0
            )
            ast_ref[pl.ds(b * STACK + STACK_AT[l], 48 * LMS[l]), :] = stack_rows(a)
        radial = radial_block(b_ref[:, span(b)], w1, w2, w3, w4, geo[4:5])
        gather_messages(b, g_ref, lifted, radial, ast_ref, l_ref, m_ref, amp_ref)
    o = dot(onehot, skip_ref[...], TN)[:OWN]
    skipped = (o[:, :C] + o[:, C : 2 * C]) + o[:, 2 * C :]
    first = skipped + dot3(invariants(amp_ref, gain_ref[...]), out_ref[...])
    f_ref[...] = first
    sends = pick_rows(sn_ref[...], first)
    sl_ref[...] = sends[:32]
    si_ref[...] = sends[32:]


def middle_kernel(f_ref, rl_ref, ri_ref, pn_ref, a_ref, b_ref):
    o = pick_rows(pn_ref[...], jnp.concatenate([f_ref[...], rl_ref[...], ri_ref[...]], axis=0))
    a_ref[...] = o[:64]
    b_ref[...] = o[64:]


def radial_kernel(b_ref, geo_ref, w1_ref, w2_ref, w3_ref, w4_ref, r_ref):
    w1, w2, w3, w4 = w1_ref[...], w2_ref[...], w3_ref[...], w4_ref[...]
    for b in range(BLOCKS):
        r_ref[span(b), :] = radial_block(b_ref[:, span(b)], w1, w2, w3, w4, geo_ref[4:5, span(b)])


def tangent_kernel(b_ref, db_ref, geo_ref, w1_ref, w2_ref, w3_ref, w4_ref, r_ref):
    w1, w2, w3, w4 = w1_ref[...], w2_ref[...], w3_ref[...], w4_ref[...]
    for b in range(BLOCKS):
        r_ref[span(b), :] = radial_tangent_block(
            b_ref[:, span(b)], db_ref[:, span(b)], w1, w2, w3, w4, geo_ref[4:5, span(b)], geo_ref[5:6, span(b)]
        )


def second_kernel(
    f_ref, rl_ref, ri_ref, pl_ref, ps_ref, g_ref, gt_ref, ast_ref, r_ref, up_ref, skip_ref, out_ref, gain_ref,
    kinds_ref, ref_ref, one_ref, hid_ref, ro_ref,
    e_ref, gmid_ref, gl_ref, gs_ref, z_ref, l_ref, m_ref, ga_ref,
    amp_ref, glift_ref,
):
    first = f_ref[...]
    ext = jnp.concatenate([first, rl_ref[...], ri_ref[...], pl_ref[...], ps_ref[...]], axis=0)
    lifted = pair_lanes(dot3(ext, up_ref[...]))
    for b in range(BLOCKS):
        gather_messages(b, g_ref, lifted, r_ref[span(b), :], ast_ref, l_ref, m_ref, amp_ref)
    gain = gain_ref[...]
    second = dot3(first, skip_ref[...]) + dot3(invariants(amp_ref, gain), out_ref[...])
    hidden = lax.dot_general(hid_ref[...], second, NT, precision=highest, preferred_element_type=f32)
    act, slope = silu_pair(hidden)
    ro = ro_ref[...]
    grad_second = dot3(slope * ro, hid_ref[...], TN)
    gm = dot3(grad_second, out_ref[...], NT)
    amp_grads(amp_ref, gain, gm, ga_ref)
    for b in range(BLOCKS):
        grad = None
        for l in range(3):
            z = spread(ast_ref, ga_ref, b, l)
            z_ref[span(b), l * C : (l + 1) * C] = z
            term = r_ref[span(b), l * C : (l + 1) * C] * z
            grad = term if grad is None else grad + term
        glift_ref[span(b), :] = pair_lanes(grad)
    glift = halves(dot(gt_ref[...], glift_ref[...]))
    gext = dot3(glift, up_ref[...], NT)
    gl_ref[...] = gext[128:192]
    gs_ref[...] = gext[192:256]
    gmid_ref[64:128, :] = gext[64:128]
    gmid_ref[0:64, :] = gext[0:64] + dot3(grad_second, skip_ref[...], NT) + one_ref[0:1]
    onehot = (lax.broadcasted_iota(jnp.int32, (KINDS, OWN), 0).astype(f32) == kinds_ref[3:4, :]).astype(f32)
    energy = lax.dot_general(ref_ref[...], onehot, NN, precision=highest, preferred_element_type=f32)
    energy = energy + lax.dot_general(one_ref[...], first, NT, precision=highest, preferred_element_type=f32)
    e_ref[...] = energy + jnp.sum(act * ro, axis=0, keepdims=True)


def early_kernel(z_ref, dr_ref, l_ref, m_ref, ga_ref, geo_ref, mask_ref, dd_ref, gp_ref, gv_ref):
    for b in range(BLOCKS):
        x = sum(
            z_ref[span(b), l * C : (l + 1) * C] * dr_ref[span(b), l * C : (l + 1) * C] for l in range(3)
        )
        edge_forces(b, x * l_ref[span(b), :], m_ref, ga_ref, geo_ref[:, span(b)], mask_ref[:, span(b)], gv_ref)
    gp_ref[...] = pick_lanes(gv_ref[...], dd_ref[...], NT)


def back_middle_kernel(gmid_ref, al_ref, as_ref, pt_ref, own_ref, l_ref, i_ref):
    mid = gmid_ref[...] + pick_rows(pt_ref[...], jnp.concatenate([al_ref[...], as_ref[...]], axis=0))
    own_ref[...] = mid[:64]
    l_ref[...] = mid[64:96]
    i_ref[...] = mid[96:128]


def late_kernel(
    own_ref, rl_ref, ri_ref, st_ref, out_ref, gain_ref, amp_ref, ast_ref, dr_ref, l_ref, m_ref, geo_ref,
    mask_ref, dd_ref, early_ref, gp_ref, ga_ref, gv_ref,
):
    grad = own_ref[...] + pick_rows(st_ref[...], jnp.concatenate([rl_ref[...], ri_ref[...]], axis=0))
    amp_grads(amp_ref, gain_ref[...], dot3(grad, out_ref[...], NT), ga_ref)
    for b in range(BLOCKS):
        x = None
        for l in range(3):
            term = spread(ast_ref, ga_ref, b, l) * dr_ref[span(b), l * C : (l + 1) * C]
            x = term if x is None else x + term
        edge_forces(b, x * l_ref[span(b), :], m_ref, ga_ref, geo_ref[:, span(b)], mask_ref[:, span(b)], gv_ref)
    gp_ref[...] = early_ref[...] + pick_lanes(gv_ref[...], dd_ref[...], NT)


def collect_kernel(v_ref, r_ref, s_ref, o_ref, *, sign):
    o_ref[...] = sign * (v_ref[...] + pick_lanes(r_ref[...], s_ref[...]))


def swap_slab_far(value):
    count = lax.axis_size("slab")
    pairs = [(i, i + 1) for i in range(1, count - 1, 2)]
    return lax.ppermute(value, "slab", pairs + [(b, a) for a, b in pairs])


def swap_slab_near(value):
    count = lax.axis_size("slab")
    return lax.ppermute(value, "slab", [(i, i ^ 1) for i in range(count)])


def swap_plane_far(value):
    count = lax.axis_size("plane")
    pairs = [(i, (i + 1) % count) for i in range(1, count, 2)]
    return lax.ppermute(value, "plane", pairs + [(b, a) for a, b in pairs])


def swap_plane_near(value):
    count = lax.axis_size("plane")
    return lax.ppermute(value, "plane", [(i, i ^ 1) for i in range(count)])


def both(swap_far, swap_near, far, near):
    far_in = swap_far(far)
    near, far_held = lax.optimization_barrier((near, far))
    return far_in, swap_near(near)


def high_low(x):
    hi = lax.reduce_precision(x, 8, 7)
    return hi.astype(bf16), (x - hi).astype(bf16)


def high_mid_low(x):
    hi = lax.reduce_precision(x, 8, 7)
    mid = lax.reduce_precision(x - hi, 8, 7)
    return hi.astype(bf16), mid.astype(bf16), (x - hi - mid).astype(bf16)


def weights_of(one, two, three_, four):
    hi, lo = high_low(jnp.transpose(one))
    w1 = jnp.concatenate([hi, hi, lo, jnp.zeros_like(lo)], axis=1)

    def inner(w):
        hi, lo = high_low(jnp.transpose(w))
        return jnp.concatenate([hi, hi, lo], axis=1)

    hi, lo = high_low(four)
    return w1, inner(two), inner(three_), jnp.concatenate([hi, hi, lo], axis=0)


def body(
    positions,
    species,
    slab_sends,
    plane_sends,
    edges,
    edge_count,
    embed_table,
    atom_ref,
    radial_one,
    radial_two,
    radial_three,
    radial_four,
    up_weight,
    skip_weight,
    out_weight,
    prod_weight,
    read_one,
    read_hidden,
    read_out,
):
    slab_odd = lax.axis_index("slab") % 2 == 1
    plane_odd = lax.axis_index("plane") % 2 == 1
    slab_list = slab_sends[0, 0]
    slab_list = jnp.where(slab_odd, slab_list, slab_list[::-1]).reshape(-1)

    def moved_slab(slot):
        return jnp.where(slab_odd & (slot >= 64) & (slot < 128), slot ^ 32, slot)

    plane_list = plane_sends[0, 0]
    plane_list = moved_slab(jnp.where(plane_odd, plane_list, plane_list[::-1])).reshape(-1)
    slab_t = (jnp.arange(64)[:, None] == slab_list[None, :]).astype(bf16)
    slab_n = (slab_list[:, None] == jnp.arange(64)[None, :]).astype(bf16)
    plane_t = (jnp.arange(128)[:, None] == plane_list[None, :]).astype(bf16)
    plane_n = (plane_list[:, None] == jnp.arange(128)[None, :]).astype(bf16)

    values = jnp.concatenate(
        [positions[0, 0], species[0, 0].astype(f32)[None, :], jnp.zeros((4, OWN), f32)], axis=0
    )
    slab_step = jnp.where(slab_odd, 1.0, -1.0) * (CELLS_Z * cell_side)
    plane_step = jnp.where(plane_odd, 1.0, -1.0) * (CELLS_Y * cell_side)
    z_row = (jnp.arange(8) == 2).astype(f32)[:, None] * slab_step
    y_row = (jnp.arange(8) == 1).astype(f32)[:, None] * plane_step

    with jax.named_scope("atoms_slab"):
        far, near = call(pick_kernel, [((8, 32), f32)] * 2, (values, slab_t), name="pick_slab")
        far, near = both(swap_slab_far, swap_slab_near, far, near)
        values_mid = jnp.concatenate([values, far + z_row, near - z_row], axis=1)
    with jax.named_scope("atoms_plane"):
        far, near = call(pick_kernel, [((8, 64), f32)] * 2, (values_mid, plane_t), name="pick_plane")
        far, near = both(swap_plane_far, swap_plane_near, far, near)
        values_ext = jnp.concatenate([values_mid, far + y_row, near - y_row], axis=1)

    with jax.named_scope("edge_lists"):
        per_atom = edge_count[0, 0] // OWN
        padded = jnp.concatenate([edges[0, 0, 0], jnp.zeros((SPAN,), jnp.int32)])
        senders = jnp.stack(
            [lax.dynamic_slice_in_dim(padded, b * GROUP * per_atom, SPAN) for b in range(BLOCKS)]
        )
        place = jnp.arange(SPAN)
        senders = jnp.where(place[None, :] < GROUP * per_atom, senders, -1).reshape(-1)
        senders = moved_slab(senders)
        senders = jnp.where(plane_odd & (senders >= 128), senders ^ 64, senders)
        place = jnp.tile(place, BLOCKS)[None, :]
        inside = jnp.arange(GROUP)[:, None]
        mask = (place >= inside * per_atom) & (place < (inside + 1) * per_atom)
        sender_t = jnp.arange(EXT)[:, None] == senders[None, :]
        sender_n = (senders[:, None] == jnp.arange(EXT)[None, :]).astype(bf16)
        block_of = jnp.arange(EDGES) // SPAN
        atom = jnp.arange(EXT)[:, None] - GROUP * block_of[None, :]
        received = (atom >= 0) & (atom < GROUP) & (place >= atom * per_atom) & (place < (atom + 1) * per_atom)
        edge_t = sender_t.astype(bf16) - received.astype(bf16)
        sender_t = sender_t.astype(bf16)
        mask = mask.astype(f32)

    with jax.named_scope("weights"):
        weights = [
            weights_of(radial_one[t], radial_two[t], radial_three[t], radial_four[t]) for t in range(2)
        ]
        tables = jnp.dot(
            jnp.pad(embed_table, ((0, KINDS - embed_table.shape[0]), (0, 0))),
            jnp.concatenate([up_weight[0], skip_weight[0]], axis=1),
            precision=highest,
            preferred_element_type=f32,
        )
        table = jnp.concatenate(high_low(tables[:, :C]), axis=1)
        skip_table = jnp.concatenate(high_mid_low(tables[:, C:]), axis=1)
        gains = jnp.pad(prod_weight, ((0, 0), (0, 4), (0, 0)))
        ref_row = jnp.broadcast_to(jnp.pad(atom_ref, (0, KINDS - atom_ref.shape[0]))[None, :], (8, KINDS))
        one_row = jnp.broadcast_to(read_one[None, :], (8, C))
        hid = jnp.transpose(read_hidden)
        ro = jnp.broadcast_to(read_out[:, None], (read_out.shape[0], OWN))

    edge_mat = ((EDGES, C), f32)
    message_mat = ((3, EDGES, 2 * C), bf16)
    by_degree = ((EDGES, 3 * C), f32)
    rows = (((8, EDGES), f32),) * 3
    amp_mat = ((9, OWN, C), f32)
    slab_rows = ((32, C), f32)
    plane_rows = ((64, C), f32)
    with jax.named_scope("first_layer"):
        (first, far, near, amp_first, lift_first, message_first, angular, basis, basis_slope, geo) = call(
            first_kernel,
            [plane_rows, slab_rows, slab_rows, amp_mat, edge_mat, message_mat,
             ((BLOCKS * STACK, SPAN), bf16), *rows],
            (values_ext, edge_t, sender_n, mask, table, skip_table, *weights[0], gains[0], out_weight[0], slab_n),
            name="first_layer",
        )
    with jax.named_scope("features_slab"):
        far, near = both(swap_slab_far, swap_slab_near, far, near)
        slab_far, slab_near = far, near
    radial_second, = call(
        radial_kernel, [by_degree], (basis, geo, *weights[1]), flops=1_000_000_000, name="radial_second"
    )
    with jax.named_scope("features_plane"):
        far, near = call(
            middle_kernel, [plane_rows] * 2, (first, slab_far, slab_near, plane_n), name="middle"
        )
        far, near = both(swap_plane_far, swap_plane_near, far, near)
    slope_second, = call(
        tangent_kernel, [by_degree], (basis, basis_slope, geo, *weights[1]), flops=2_000_000_000, name="slope_second"
    )
    slope_first, = call(
        tangent_kernel, [by_degree], (basis, basis_slope, geo, *weights[0]), flops=2_000_000_000, name="slope_first"
    )
    with jax.named_scope("second_layer"):
        energies, gmid, far, near, z, lift_second, message_second, ga = call(
            second_kernel,
            [((8, OWN), f32), ((128, C), f32), plane_rows, plane_rows, by_degree, edge_mat, message_mat, amp_mat],
            (first, slab_far, slab_near, far, near, sender_n, sender_t, angular, radial_second,
             up_weight[1], skip_weight[1], out_weight[1], gains[1], values, ref_row, one_row, hid, ro),
            scratch=[pltpu.VMEM((9, OWN, C), f32), pltpu.VMEM((EDGES, 2 * C), bf16)],
            name="second_layer",
        )
    with jax.named_scope("feature_grads_plane"):
        far, near = both(swap_plane_far, swap_plane_near, far, near)
    early, = call(
        early_kernel,
        [((8, EXT), f32)],
        (z, slope_second, lift_second, message_second, ga, geo, mask, edge_t),
        scratch=[pltpu.VMEM((8, EDGES), f32)],
        flops=1_000_000_000,
        name="early_forces",
    )
    with jax.named_scope("feature_grads_slab"):
        own, far, near = call(
            back_middle_kernel, [plane_rows, slab_rows, slab_rows], (gmid, far, near, plane_t), name="back_middle"
        )
        far, near = both(swap_slab_far, swap_slab_near, far, near)
    with jax.named_scope("late_forces"):
        grads, = call(
            late_kernel,
            [((8, EXT), f32)],
            (own, far, near, slab_t, out_weight[0], gains[0], amp_first, angular, slope_first, lift_first,
             message_first, geo, mask, edge_t, early),
            scratch=[pltpu.VMEM((9, OWN, C), f32), pltpu.VMEM((8, EDGES), f32)],
            name="late_forces",
        )
    with jax.named_scope("position_grads_plane"):
        far, near = both(swap_plane_far, swap_plane_near, grads[:, 128:192], grads[:, 192:256])
        mid, = call(
            functools.partial(collect_kernel, sign=1.0),
            [((8, 128), f32)],
            (grads[:, :128], jnp.concatenate([far, near], axis=1), plane_n),
            name="collect_plane",
        )
    with jax.named_scope("position_grads_slab"):
        far, near = both(swap_slab_far, swap_slab_near, mid[:, 64:96], mid[:, 96:128])
        total, = call(
            functools.partial(collect_kernel, sign=-1.0),
            [((8, OWN), f32)],
            (mid[:, :64], jnp.concatenate([far, near], axis=1), slab_n),
            name="collect_slab",
        )
    return (energies[None, None, 0, :], total[None, None, :3, :])


def solution(mesh):
    in_specs = (
        P("slab", "plane", None, None),
        P("slab", "plane", None),
        P("slab", "plane", None, None),
        P("slab", "plane", None, None),
        P("slab", "plane", None, None),
        P("slab", "plane"),
    ) + (P(),) * 13
    out_specs = (P("slab", "plane", None), P("slab", "plane", None, None))
    return jax.shard_map(body, mesh=mesh, in_specs=in_specs, out_specs=out_specs, check_vma=False)
```

```python
import functools

import jax
import jax.numpy as jnp
from jax import lax
from jax.experimental import pallas as pl
from jax.experimental.pallas import tpu as pltpu
from jax.sharding import PartitionSpec as P

CELLS_Y = 2
CELLS_Z = 2

cutoff_radius = 5.0
cell_side = 3.0
inverse_neighbours = 0.2
highest = lax.Precision.HIGHEST
f32 = jnp.float32
bf16 = jnp.bfloat16

C = 128
OWN = 64
EXT = 256
EDGES = 1536
BLOCKS = 4
GROUP = 16
SPAN = EDGES // BLOCKS
KINDS = 96
LMS = (1, 3, 5)
FIRST_LM = (0, 1, 4)
STACK_AT = (0, 48, 192)
STACK = 432
R3, R5, R15 = 3.0**0.5, 5.0**0.5, 15.0**0.5

NN = (((1,), (0,)), ((), ()))
TN = (((0,), (0,)), ((), ()))
NT = (((1,), (1,)), ((), ()))


def dot(a, b, dims=NN):
    return lax.dot_general(a, b, dims, preferred_element_type=f32)


def dot3(a, b, dims=NN):
    return lax.dot_general(a, b, dims, precision=lax.Precision.HIGH, preferred_element_type=f32)


def split(x):
    hi = x.astype(bf16)
    return hi, (x - hi.astype(f32)).astype(bf16)


def pair_lanes(x):
    hi, lo = split(x)
    return jnp.concatenate([hi, lo], axis=1)


def halves(o):
    return o[:, :C] + o[:, C:]


def stack_rows(x):
    hi, lo = split(x)
    return jnp.concatenate([hi, lo, hi], axis=0)


def three(x):
    hi = x.astype(bf16).astype(f32)
    rest = x - hi
    mid = rest.astype(bf16).astype(f32)
    return hi, mid, rest - mid


def pick_lanes(values, chooser, dims=NN):
    hi, mid, lo = three(values)
    o = dot(jnp.concatenate([hi, mid, lo, jnp.zeros_like(lo)], axis=0).astype(bf16), chooser, dims)
    return (o[0:8] + o[8:16]) + o[16:24]


def pick_rows(chooser, values, dims=NN):
    hi, mid, lo = three(values)
    o = dot(chooser, jnp.concatenate([hi, mid, lo], axis=1).astype(bf16), dims)
    return (o[:, :C] + o[:, C : 2 * C]) + o[:, 2 * C :]


def silu(x):
    return x * (1.0 / (1.0 + jnp.exp(-x)))


def silu_pair(x):
    s = 1.0 / (1.0 + jnp.exp(-x))
    return x * s, s * (1.0 + x * (1.0 - s))


def span(b):
    return pl.ds(b * SPAN, SPAN)


def fetched(kernel, count):
    def run(*refs):
        given, rest = refs[:count], refs[count:]
        sems, held = rest[-1], rest[-1 - count : -1]
        copies = [pltpu.make_async_copy(src, dst, sems.at[k]) for k, (src, dst) in enumerate(zip(given, held))]
        for copy in copies:
            copy.start()
        for copy in copies:
            copy.wait()
        kernel(*held, *rest[: -1 - count])

    return run


def call(kernel, outs, args, scratch=(), flops=0, name=None, limit=8, raw=False):
    spec = pl.BlockSpec(memory_space=pltpu.VMEM)
    out_shape = tuple(pltpu.VMEM(shape, dtype) for shape, dtype in outs)
    moved = sum(a.size * a.dtype.itemsize for a in args)
    scratch = list(scratch)
    if raw:
        big = [a for a in args if a.size > 1]
        scratch += [pltpu.VMEM(a.shape, a.dtype) for a in big] + [pltpu.SemaphoreType.DMA((len(big),))]
        kernel = fetched(kernel, len(big))
        in_specs = [pl.BlockSpec(memory_space=pltpu.HBM)] * len(big)
        in_specs += [pl.BlockSpec(memory_space=pltpu.SMEM)] * (len(args) - len(big))
        args = [pltpu.with_memory_space_constraint(a, pltpu.HBM) for a in big] + [a for a in args if a.size == 1]
    else:
        in_specs = [spec] * len(args)
        args = [pltpu.with_memory_space_constraint(a, pltpu.VMEM) for a in args]
    return pl.pallas_call(
        kernel,
        out_shape=out_shape,
        in_specs=in_specs,
        out_specs=tuple(spec for _ in out_shape),
        scratch_shapes=scratch,
        compiler_params=pltpu.CompilerParams(vmem_limit_bytes=limit * 1024 * 1024),
        cost_estimate=pl.CostEstimate(flops=flops, bytes_accessed=moved, transcendentals=0),
        name=name,
    )(*args)


def odd(axis):
    return lax.rem(lax.axis_index(axis), 2)


def by_parity(flag, rows):
    swap = jnp.full(rows[0:1].shape, flag) == 1
    return jnp.where(swap, rows[0:1], rows[1:2]), jnp.where(swap, rows[1:2], rows[0:1])


def moved_slab(slot):
    swap = (jnp.full(slot.shape, odd("slab")) == 1) & (slot >= 64) & (slot < 128)
    return jnp.where(swap, slot ^ 32, slot)


def chooser(slots, picked):
    rows = lax.broadcasted_iota(jnp.int32, (slots, picked.shape[1]), 0)
    return (rows == picked).astype(f32).astype(bf16)


def shifted(values, row, step):
    rows = lax.broadcasted_iota(jnp.int32, values.shape, 0)
    return values + jnp.where(rows == row, step, 0.0)


def atoms_slab_kernel(
    pos_ref, kind_ref, list_ref, plane_ref, v_ref, tf_ref, tn_ref, pf_ref, pn_ref, far_ref, near_ref
):
    for k in range(3):
        v_ref[k : k + 1, :] = pos_ref[0, k]
    v_ref[3:4, :] = kind_ref[...].astype(f32)
    v_ref[4:8, :] = jnp.zeros((4, OWN), f32)
    far, near = by_parity(odd("slab"), list_ref[...])
    far, near = chooser(OWN, far), chooser(OWN, near)
    tf_ref[...] = far
    tn_ref[...] = near
    v = v_ref[...]
    far_ref[...] = pick_lanes(v, far)
    near_ref[...] = pick_lanes(v, near)
    for picked, t_ref in zip(by_parity(odd("plane"), plane_ref[...]), (pf_ref, pn_ref)):
        t_ref[...] = chooser(128, moved_slab(picked))


def atoms_plane_kernel(v_ref, far_ref, near_ref, tf_ref, tn_ref, pf_ref, pn_ref, sf_ref, sn_ref):
    step = (2 * odd("slab") - 1).astype(f32) * (CELLS_Z * cell_side)
    far = shifted(far_ref[...], 2, step)
    near = shifted(near_ref[...], 2, -step)
    pf_ref[...] = far
    pn_ref[...] = near
    own = v_ref[...]
    for t_ref, s_ref in ((tf_ref, sf_ref), (tn_ref, sn_ref)):
        s_ref[...] = pick_lanes(own, t_ref[0:64, :]) + (
            pick_lanes(far, t_ref[64:96, :]) + pick_lanes(near, t_ref[96:128, :])
        )


def prepare_kernel(
    edge_ref, one_ref, two_ref, three_ref, four_ref, embed_ref, up_ref, skip_ref, atom_ref, hid_ref, ro_ref,
    out_ref, gain_ref, read_ref, count_ref,
    g_ref, gt_ref, dd_ref, mask_ref, w1_ref, w2_ref, w3_ref, w4_ref, table_ref, skips_ref, refs_ref, hidt_ref, hidro_ref,
    up1_ref, skip1_ref, outs_ref, gains_ref, reads_ref, ros_ref,
):
    per_atom = count_ref[0, 0] // OWN
    senders = jnp.broadcast_to(edge_ref[0:1, :], (8, EDGES))
    swap_plane = jnp.full((1, SPAN), odd("plane")) == 1
    place = lax.broadcasted_iota(jnp.int32, (GROUP, SPAN), 1)
    first_place = lax.broadcasted_iota(jnp.int32, (GROUP, SPAN), 0) * per_atom
    mask = ((place >= first_place) & (place < first_place + per_atom)).astype(f32)
    lanes = lax.broadcasted_iota(jnp.int32, (128, 128), 1).astype(f32)
    for b in range(BLOCKS):
        start = b * GROUP * per_atom
        rows = senders if b == 0 else pltpu.roll(senders, lax.rem(EDGES - start, EDGES), 1)
        row = rows[0:1, :SPAN]
        row = moved_slab(row)
        row = jnp.where(swap_plane & (row >= 128), row ^ 64, row)
        row = jnp.where(place[0:1] < GROUP * per_atom, row, -1)
        t = (lax.broadcasted_iota(jnp.int32, (EXT, SPAN), 0) == row).astype(f32)
        gt_ref[:, span(b)] = t.astype(bf16)
        dd_ref[:, span(b)] = t.astype(bf16)
        mine = pl.ds(b * GROUP, GROUP)
        dd_ref[mine, span(b)] = (t[b * GROUP : (b + 1) * GROUP] - mask).astype(bf16)
        mask_ref[:, span(b)] = mask
        for chunk in range(SPAN // 128):
            part = row[:, chunk * 128 : (chunk + 1) * 128].astype(f32)
            column = jnp.transpose(jnp.broadcast_to(part, (128, 128)))
            here = pl.ds(b * SPAN + chunk * 128, 128)
            g_ref[here, 0:128] = (column == lanes).astype(f32).astype(bf16)
            g_ref[here, 128:256] = (column == lanes + 128.0).astype(f32).astype(bf16)
    for t in range(2):
        hi, mid, lo = three(one_ref[t])
        stacked = jnp.concatenate([hi, hi, mid + lo, jnp.zeros_like(hi)], axis=0)
        w1_ref[t] = jnp.transpose(stacked).astype(bf16)
        for ref, to_ref in ((two_ref, w2_ref), (three_ref, w3_ref)):
            hi, mid, lo = three(ref[t])
            to_ref[t] = jnp.transpose(jnp.concatenate([hi, hi, mid + lo], axis=0)).astype(bf16)
        hi, lo = split(four_ref[t])
        w4_ref[t] = jnp.concatenate([hi, hi, lo], axis=0)
    embed = embed_ref[...]
    kinds = embed.shape[0]
    table_ref[...] = jnp.zeros(table_ref.shape, bf16)
    skips_ref[...] = jnp.zeros(skips_ref.shape, bf16)
    exact = functools.partial(
        lax.dot_general, dimension_numbers=NN, precision=highest, preferred_element_type=f32
    )
    table_ref[0:kinds, :] = pair_lanes(exact(embed, up_ref[0]))
    hi, mid, lo = three(exact(embed, skip_ref[0]))
    skips_ref[0:kinds, :] = jnp.concatenate([hi, mid, lo], axis=1).astype(bf16)
    refs_ref[...] = jnp.zeros(refs_ref.shape, f32)
    refs_ref[0:1, 0:kinds] = atom_ref[...]
    hidt_ref[...] = hid_ref[...]
    hidro_ref[...] = hid_ref[...] * jnp.transpose(jnp.broadcast_to(ro_ref[...], (C, ro_ref.shape[1])))
    up1_ref[...] = up_ref[1]
    skip1_ref[...] = skip_ref[1]
    outs_ref[...] = out_ref[...]
    gains_ref[...] = gain_ref[...]
    reads_ref[...] = read_ref[...]
    ros_ref[...] = jnp.broadcast_to(ro_ref[...], ros_ref.shape)


def geometry(v, valid, b_ref, db_ref, geo_ref):
    vx = jnp.where(valid, v[0:1], 2.0 * cutoff_radius)
    vy = jnp.where(valid, v[1:2], 0.0)
    vz = jnp.where(valid, v[2:3], 0.0)
    d = jnp.sqrt(vx * vx + vy * vy + vz * vz)
    inv = 1.0 / d
    geo_ref[0:1, :] = vx * inv
    geo_ref[1:2, :] = vy * inv
    geo_ref[2:3, :] = vz * inv
    geo_ref[3:4, :] = inv
    s = d / cutoff_radius
    s2 = s * s
    s4 = s2 * s2
    s5 = s4 * s
    s6 = s4 * s2
    s7 = s6 * s
    inside = (s < 1.0) & valid
    u = 1.0 - 28.0 * s6 + 48.0 * s7 - 21.0 * s4 * s4
    du = (-168.0 * s5 + 336.0 * s6 - 168.0 * s7) / cutoff_radius
    geo_ref[4:5, :] = jnp.where(inside, u * inverse_neighbours, 0.0)
    geo_ref[5:6, :] = jnp.where(inside, du * inverse_neighbours, 0.0)
    geo_ref[6:8, :] = jnp.zeros_like(geo_ref[6:8, :])
    t = (jnp.minimum(s, 1.0) - 0.5) * jnp.pi
    z = t * t
    cs = 1.0 - z * (1 / 2 - z * (1 / 24 - z * (1 / 720 - z * (1 / 40320 - z * (1 / 3628800 - z * (1 / 479001600 - z * (1 / 87178291200)))))))
    sn = 1.0 - z * (1 / 6 - z * (1 / 120 - z * (1 / 5040 - z * (1 / 362880 - z * (1 / 39916800 - z * (1 / 6227020800))))))
    s1, c1 = cs, -t * sn

    def plus(a, b):
        return a[0] * b[1] + a[1] * b[0], a[1] * b[1] - a[0] * b[0]

    w1 = (s1, c1)
    w2 = plus(w1, w1)
    w3 = plus(w2, w1)
    w4 = plus(w2, w2)
    waves = (w1, w2, w3, w4, plus(w4, w1), plus(w4, w2), plus(w4, w3), plus(w4, w4))
    gain = (2.0 / cutoff_radius) ** 0.5 * inv
    for n, (sine, cosine) in enumerate(waves):
        b_ref[n : n + 1, :] = gain * sine
        db_ref[n : n + 1, :] = gain * (cosine * ((n + 1) * jnp.pi / cutoff_radius) - sine * inv)


def basis_stack(x):
    hi, mid, _ = three(x)
    lo = x - hi
    return jnp.concatenate([hi, lo, hi, jnp.zeros_like(hi)], axis=0).astype(bf16)


def radial_hidden(b, w1, w2, w3):
    h = silu(dot(w1, basis_stack(b)))
    h = silu(dot(w2, stack_rows(h)))
    return silu(dot(w3, stack_rows(h)))


def radial_hidden_pair(b, db, w1, w2, w3):
    h, g = silu_pair(dot(w1, basis_stack(b)))
    t = g * dot(w1, basis_stack(db))
    h, g = silu_pair(dot(w2, stack_rows(h)))
    t = g * dot(w2, stack_rows(t))
    h, g = silu_pair(dot(w3, stack_rows(h)))
    t = g * dot(w3, stack_rows(t))
    return h, t


def angular_rows(geo):
    x, y, z = geo[0:1], geo[1:2], geo[2:3]
    return (
        jnp.ones_like(x),
        R3 * x,
        R3 * y,
        R3 * z,
        R15 * x * y,
        R15 * y * z,
        0.5 * R5 * (3.0 * z * z - 1.0),
        R15 * x * z,
        0.5 * R15 * (x * x - y * y),
    )


def messages(g_ref, lifted, radial_of, l_ref, m_ref):
    for b in range(BLOCKS):
        lift = halves(dot(g_ref[span(b), :], lifted))
        l_ref[span(b), :] = lift
        radial = radial_of(b)
        for l in range(3):
            m_ref[l, span(b), :] = pair_lanes(radial[:, l * C : (l + 1) * C] * lift)


def amplitudes(ast_ref, m_ref, amp_ref):
    for b in range(BLOCKS):
        for l in range(3):
            n = LMS[l]
            o = dot(ast_ref[pl.ds(b * STACK + STACK_AT[l], 32 * n), :], m_ref[l, span(b), :])
            amp = halves(o[: 16 * n]) + o[16 * n :, :C]
            for k in range(n):
                amp_ref[FIRST_LM[l] + k, pl.ds(b * GROUP, GROUP), :] = amp[16 * k : 16 * (k + 1)]


def invariants(amp_ref, gain):
    b0 = amp_ref[0]
    b1 = sum(amp_ref[k] * amp_ref[k] for k in range(1, 4))
    b2 = sum(amp_ref[k] * amp_ref[k] for k in range(4, 9))
    return gain[0:1] * b0 + gain[1:2] * b1 + gain[2:3] * b2 + gain[3:4] * b0 * b0


def amp_grads(amp_ref, gain, gm, ga_ref):
    ga_ref[0] = gm * (gain[0:1] + 2.0 * gain[3:4] * amp_ref[0])
    one = gm * (2.0 * gain[1:2])
    two = gm * (2.0 * gain[2:3])
    for k in range(1, 4):
        ga_ref[k] = one * amp_ref[k]
    for k in range(4, 9):
        ga_ref[k] = two * amp_ref[k]


def group_grads(ga_ref, b, l):
    return jnp.concatenate(
        [ga_ref[FIRST_LM[l] + k, pl.ds(b * GROUP, GROUP), :] for k in range(LMS[l])], axis=0
    )


def spread(ast_ref, ga_ref, b, l):
    n = LMS[l]
    hi, lo = split(group_grads(ga_ref, b, l))
    return dot(
        ast_ref[pl.ds(b * STACK + STACK_AT[l], 48 * n), :], jnp.concatenate([hi, hi, lo], axis=0), TN
    )


def angular_grads(m_ref, ga_ref, mask_ref, gy_ref):
    for b in range(BLOCKS):
        mask = mask_ref[:, span(b)]
        for l in (1, 2):
            n = LMS[l]
            hi, lo = split(group_grads(ga_ref, b, l))
            left = jnp.concatenate(
                [jnp.concatenate([hi, hi], axis=1), jnp.concatenate([lo, jnp.zeros_like(lo)], axis=1)],
                axis=0,
            )
            w = dot(left, m_ref[l, span(b), :], NT)
            w = w[: 16 * n] + w[16 * n :]
            for k in range(n):
                row = FIRST_LM[l] + k - 1
                gy_ref[row : row + 1, span(b)] = jnp.sum(mask * w[16 * k : 16 * (k + 1)], axis=0, keepdims=True)


def edge_forces(x_ref, gy_ref, geo_ref, gv_ref):
    gd = dot(jnp.ones((16, 2 * C), bf16), x_ref[...], NT)[0:1]
    gy = [None] + [gy_ref[k : k + 1, :] for k in range(8)]
    x, y, z, inv = (geo_ref[k : k + 1, :] for k in range(4))
    gx = R3 * gy[1] + R15 * (y * gy[4] + z * gy[7] + x * gy[8])
    gyy = R3 * gy[2] + R15 * (x * gy[4] + z * gy[5] - y * gy[8])
    gz = R3 * gy[3] + R15 * (y * gy[5] + x * gy[7]) + (3.0 * R5) * z * gy[6]
    along = x * gx + y * gyy + z * gz
    core = gd - along * inv
    gv_ref[0:1, :] = core * x + gx * inv
    gv_ref[1:2, :] = core * y + gyy * inv
    gv_ref[2:3, :] = core * z + gz * inv
    gv_ref[3:8, :] = jnp.zeros((5, EDGES), f32)


def first_kernel(
    v_ref, pf_ref, pn_ref, qf_ref, qn_ref, dd_ref, g_ref, mask_ref, table_ref, skip_ref, w1_ref, w2_ref, w3_ref, w4_ref,
    gain_ref, out_ref, tf_ref, tn_ref,
    f_ref, sf_ref, sn_ref, amp_ref, l_ref, m_ref, ast_ref, b_ref, db_ref, geo_ref,
):
    step = (2 * odd("plane") - 1).astype(f32) * (CELLS_Y * cell_side)
    parts = (v_ref[...], pf_ref[...], pn_ref[...], shifted(qf_ref[...], 1, step), shifted(qn_ref[...], 1, -step))
    valid = jnp.sum(mask_ref[...], axis=0, keepdims=True) > 0.5
    vector, lifted, at = None, [], 0
    for part in parts:
        rows = part.shape[1]
        piece = pick_lanes(part, dd_ref[at : at + rows, :])
        vector = piece if vector is None else vector + piece
        kinds = lax.broadcasted_iota(jnp.int32, (KINDS, rows), 0).astype(f32) == part[3:4]
        kinds = kinds.astype(f32).astype(bf16)
        if at == 0:
            o = dot(kinds, skip_ref[...], TN)
            skipped = (o[:, :C] + o[:, C : 2 * C]) + o[:, 2 * C :]
        lifted.append(dot(kinds, table_ref[...], TN))
        at += rows
    lifted = jnp.concatenate(lifted, axis=0).astype(bf16)
    geometry(vector, valid, b_ref, db_ref, geo_ref)
    h = stack_rows(radial_hidden(b_ref[...], w1_ref[0], w2_ref[0], w3_ref[0]) * geo_ref[4:5, :])
    rows = angular_rows(geo_ref[0:3, :])
    for b in range(BLOCKS):
        mask = mask_ref[:, span(b)]
        for l in range(3):
            a = jnp.concatenate(
                [mask * rows[FIRST_LM[l] + k][:, b * SPAN : (b + 1) * SPAN] for k in range(LMS[l])], axis=0
            )
            ast_ref[pl.ds(b * STACK + STACK_AT[l], 48 * LMS[l]), :] = stack_rows(a)
    messages(g_ref, lifted, lambda b: dot(h[:, b * SPAN : (b + 1) * SPAN], w4_ref[0], TN), l_ref, m_ref)
    amplitudes(ast_ref, m_ref, amp_ref)
    first = skipped + dot3(invariants(amp_ref, gain_ref[0]), out_ref[0])
    f_ref[...] = first
    sf_ref[...] = pick_rows(tf_ref[...], first, TN)
    sn_ref[...] = pick_rows(tn_ref[...], first, TN)


def middle_kernel(f_ref, rf_ref, rn_ref, pf_ref, pn_ref, a_ref, b_ref):
    rows = jnp.concatenate([f_ref[...], rf_ref[...], rn_ref[...]], axis=0)
    a_ref[...] = pick_rows(pf_ref[...], rows, TN)
    b_ref[...] = pick_rows(pn_ref[...], rows, TN)


def slope_kernel(b_ref, db_ref, geo_ref, w1_ref, w2_ref, w3_ref, q_ref, *, layer):
    h, t = radial_hidden_pair(b_ref[...], db_ref[...], w1_ref[layer], w2_ref[layer], w3_ref[layer])
    q_ref[...] = stack_rows(t * geo_ref[4:5, :] + h * geo_ref[5:6, :])


def radial_kernel(b_ref, db_ref, geo_ref, w1_ref, w2_ref, w3_ref, w4_ref, r_ref, q_ref, *, layer):
    h, t = radial_hidden_pair(b_ref[...], db_ref[...], w1_ref[layer], w2_ref[layer], w3_ref[layer])
    q_ref[...] = stack_rows(t * geo_ref[4:5, :] + h * geo_ref[5:6, :])
    h = stack_rows(h * geo_ref[4:5, :])
    for b in range(BLOCKS):
        r_ref[span(b), :] = dot(h[:, b * SPAN : (b + 1) * SPAN], w4_ref[layer], TN)


def expand_kernel(q_ref, w4_ref, r_ref, *, layer):
    for b in range(BLOCKS):
        r_ref[span(b), :] = dot(q_ref[:, span(b)], w4_ref[layer], TN)


def second_kernel(
    f_ref, rf_ref, rn_ref, pf_ref, pn_ref, g_ref, gt_ref, ast_ref, r_ref, up_ref, skip_ref, out_ref, gain_ref,
    v_ref, ref_ref, one_ref, hid_ref, hidro_ref, ro_ref,
    e_ref, gmid_ref, gf_ref, gn_ref, z_ref, l_ref, m_ref, ga_ref,
    amp_ref, glift_ref,
):
    first = f_ref[...]
    ext = jnp.concatenate([first, rf_ref[...], rn_ref[...], pf_ref[...], pn_ref[...]], axis=0)
    up, skip, out, gain = up_ref[...], skip_ref[...], out_ref[1], gain_ref[1]
    lifted = pair_lanes(dot3(ext, up))
    messages(g_ref, lifted, lambda b: r_ref[span(b), :], l_ref, m_ref)
    amplitudes(ast_ref, m_ref, amp_ref)
    second = dot3(first, skip) + dot3(invariants(amp_ref, gain), out)
    hidden = lax.dot_general(hid_ref[...], second, NT, precision=highest, preferred_element_type=f32)
    act, slope = silu_pair(hidden)
    grad_second = dot3(slope, hidro_ref[...], TN)
    gm = dot3(grad_second, out, NT)
    amp_grads(amp_ref, gain, gm, ga_ref)
    for b in range(BLOCKS):
        grad = None
        for l in range(3):
            z = spread(ast_ref, ga_ref, b, l)
            z_ref[span(b), l * C : (l + 1) * C] = z
            term = r_ref[span(b), l * C : (l + 1) * C] * z
            grad = term if grad is None else grad + term
        glift_ref[span(b), :] = pair_lanes(grad)
    glift = halves(dot(gt_ref[...], glift_ref[...]))
    gext = dot3(glift, up, NT)
    gf_ref[...] = gext[128:192]
    gn_ref[...] = gext[192:256]
    gmid_ref[64:128, :] = gext[64:128]
    gmid_ref[0:64, :] = gext[0:64] + dot3(grad_second, skip, NT) + one_ref[...]
    onehot = (lax.broadcasted_iota(jnp.int32, (KINDS, OWN), 0).astype(f32) == v_ref[3:4, :]).astype(f32)

    def exact(a, b, dims=NN):
        return lax.dot_general(a, b, dims, precision=highest, preferred_element_type=f32)

    energy = exact(ref_ref[...], onehot)
    energy = energy + exact(jnp.broadcast_to(one_ref[...], (8, C)), first, NT)
    energy = energy + exact(ro_ref[...], act)
    e_ref[...] = energy[0:1]


def early_kernel(z_ref, q_ref, w4_ref, l_ref, m_ref, ga_ref, geo_ref, mask_ref, gv_ref, x_ref, gy_ref):
    for b in range(BLOCKS):
        slope = dot(q_ref[:, span(b)], w4_ref[1], TN)
        x = sum(z_ref[span(b), l * C : (l + 1) * C] * slope[:, l * C : (l + 1) * C] for l in range(3))
        x_ref[span(b), :] = pair_lanes(x * l_ref[span(b), :])
    angular_grads(m_ref, ga_ref, mask_ref, gy_ref)
    edge_forces(x_ref, gy_ref, geo_ref, gv_ref)


def back_middle_kernel(gmid_ref, rf_ref, rn_ref, pf_ref, pn_ref, own_ref, f_ref, n_ref):
    mid = gmid_ref[...] + (pick_rows(pf_ref[...], rf_ref[...]) + pick_rows(pn_ref[...], rn_ref[...]))
    own_ref[...] = mid[:64]
    f_ref[...] = mid[64:96]
    n_ref[...] = mid[96:128]


def late_kernel(
    own_ref, rf_ref, rn_ref, tf_ref, tn_ref, out_ref, gain_ref, amp_ref, ast_ref, dr_ref, l_ref, m_ref, geo_ref,
    mask_ref, dd_ref, early_ref, of_ref, pf_ref, pn_ref, qf_ref, qn_ref, ga_ref, gv_ref, x_ref, gy_ref,
):
    grad = own_ref[...] + (pick_rows(tf_ref[...], rf_ref[...]) + pick_rows(tn_ref[...], rn_ref[...]))
    amp_grads(amp_ref, gain_ref[0], dot3(grad, out_ref[0], NT), ga_ref)
    for b in range(BLOCKS):
        x = None
        for l in range(3):
            term = spread(ast_ref, ga_ref, b, l) * dr_ref[span(b), l * C : (l + 1) * C]
            x = term if x is None else x + term
        x_ref[span(b), :] = pair_lanes(x * l_ref[span(b), :])
    angular_grads(m_ref, ga_ref, mask_ref, gy_ref)
    edge_forces(x_ref, gy_ref, geo_ref, gv_ref)
    total = gv_ref[...] + early_ref[...]
    at = 0
    for ref in (of_ref, pf_ref, pn_ref, qf_ref, qn_ref):
        rows = ref.shape[1]
        ref[...] = pick_lanes(total, dd_ref[at : at + rows, :], NT)
        at += rows


def collect_plane_kernel(of_ref, pf_ref, pn_ref, rf_ref, rn_ref, tf_ref, tn_ref, o_ref, f_ref, n_ref):
    far, near, at = rf_ref[...], rn_ref[...], 0
    for have_ref, ref in ((of_ref, o_ref), (pf_ref, f_ref), (pn_ref, n_ref)):
        rows = ref.shape[1]
        back = pick_lanes(far, tf_ref[at : at + rows, :], NT) + pick_lanes(near, tn_ref[at : at + rows, :], NT)
        ref[...] = have_ref[...] + back
        at += rows


def collect_slab_kernel(v_ref, rf_ref, rn_ref, tf_ref, tn_ref, o_ref):
    back = pick_lanes(rf_ref[...], tf_ref[...], NT) + pick_lanes(rn_ref[...], tn_ref[...], NT)
    forces = -(v_ref[...] + back)
    for k in range(3):
        o_ref[0, k] = forces[k : k + 1]


def swap_slab_far(value):
    count = lax.axis_size("slab")
    pairs = [(i, i + 1) for i in range(1, count - 1, 2)]
    return lax.ppermute(value, "slab", pairs + [(b, a) for a, b in pairs])


def swap_slab_near(value):
    count = lax.axis_size("slab")
    return lax.ppermute(value, "slab", [(i, i ^ 1) for i in range(count)])


def swap_plane_far(value):
    count = lax.axis_size("plane")
    pairs = [(i, (i + 1) % count) for i in range(1, count, 2)]
    return lax.ppermute(value, "plane", pairs + [(b, a) for a, b in pairs])


def swap_plane_near(value):
    count = lax.axis_size("plane")
    return lax.ppermute(value, "plane", [(i, i ^ 1) for i in range(count)])


def both(swap_far, swap_near, far, near):
    return swap_far(far), swap_near(near)


def body(
    positions,
    species,
    slab_sends,
    plane_sends,
    edges,
    edge_count,
    embed_table,
    atom_ref,
    radial_one,
    radial_two,
    radial_three,
    radial_four,
    up_weight,
    skip_weight,
    out_weight,
    prod_weight,
    read_one,
    read_hidden,
    read_out,
):
    edge_mat = ((EDGES, C), f32)
    message_mat = ((3, EDGES, 2 * C), bf16)
    by_degree = ((EDGES, 3 * C), f32)
    edge_rows = ((8, EDGES), f32)
    amp_mat = ((9, OWN, C), f32)
    slab_rows = ((32, C), f32)
    plane_rows = ((64, C), f32)
    own_lanes = ((8, OWN), f32)
    slab_lanes = ((8, 32), f32)
    plane_lanes = ((8, 64), f32)

    with jax.named_scope("atoms_slab"):
        values, slab_t_far, slab_t_near, plane_t_far, plane_t_near, far, near = call(
            atoms_slab_kernel,
            [own_lanes, ((OWN, 32), bf16), ((OWN, 32), bf16), ((128, 64), bf16), ((128, 64), bf16), slab_lanes, slab_lanes],
            (jnp.transpose(positions, (0, 2, 1, 3)), species[0], slab_sends[0, 0], plane_sends[0, 0]),
            raw=True,
            name="atoms_slab",
        )
        far, near = both(swap_slab_far, swap_slab_near, far, near)
    with jax.named_scope("atoms_plane"):
        slab_far, slab_near, far, near = call(
            atoms_plane_kernel,
            [slab_lanes, slab_lanes, plane_lanes, plane_lanes],
            (values, far, near, plane_t_far, plane_t_near),
            name="atoms_plane",
        )
        edge_list, far, near = lax.optimization_barrier((edges[0, 0], far, near))
        far, near = both(swap_plane_far, swap_plane_near, far, near)
    with jax.named_scope("prepare"):
        square = ((C, C), f32)
        sender_n, sender_t, edge_t, mask, *prepared = call(
            prepare_kernel,
            [((EDGES, EXT), bf16), ((EXT, EDGES), bf16), ((EXT, EDGES), bf16), ((GROUP, EDGES), f32),
             ((2, 64, 32), bf16), ((2, 64, 192), bf16), ((2, 64, 192), bf16), ((2, 192, 3 * C), bf16),
             ((KINDS, 2 * C), bf16), ((KINDS, 3 * C), bf16), ((8, KINDS), f32), ((16, C), f32), ((16, C), f32),
             square, square, ((2, C, C), f32), ((2, 4, C), f32), ((1, C), f32), ((8, 16), f32)],
            (edge_list, radial_one, radial_two, radial_three, radial_four, embed_table, up_weight, skip_weight,
             atom_ref[None, :], jnp.transpose(read_hidden), read_out[None, :], out_weight, prod_weight,
             read_one[None, :], edge_count),
            raw=True,
            flops=1_000_000_000,
            name="prepare",
        )
        weights, (table, skip_table, ref_row, hid, hidro, up_second, skip_second, outs, gains, read_row, read_last) = (
            tuple(prepared[:4]), prepared[4:]
        )

    with jax.named_scope("first_layer"):
        (first, s_far, s_near, amp_first, lift_first, message_first, angular, basis, basis_slope, geo) = call(
            first_kernel,
            [plane_rows, slab_rows, slab_rows, amp_mat, edge_mat, message_mat,
             ((BLOCKS * STACK, SPAN), bf16), edge_rows, edge_rows, edge_rows],
            (values, slab_far, slab_near, far, near, edge_t, sender_n, mask, table, skip_table, *weights,
             gains, outs, slab_t_far, slab_t_near),
            name="first_layer",
        )
    with jax.named_scope("features_slab"):
        slab_far, slab_near = both(swap_slab_far, swap_slab_near, s_far, s_near)
    slope_first, = call(
        functools.partial(slope_kernel, layer=0), [((192, EDGES), bf16)], (basis, basis_slope, geo, *weights[:3]),
        flops=1_000_000_000, name="slope_first",
    )
    with jax.named_scope("features_plane"):
        far, near = call(
            middle_kernel, [plane_rows] * 2, (first, slab_far, slab_near, plane_t_far, plane_t_near), name="middle"
        )
        far, near, basis, geo = lax.optimization_barrier((far, near, basis, geo))
        far, near = both(swap_plane_far, swap_plane_near, far, near)
    radial_second, slope_second = call(
        functools.partial(radial_kernel, layer=1), [by_degree, ((192, EDGES), bf16)],
        (basis, basis_slope, geo, *weights), flops=1_000_000_000, name="radial_second",
    )
    with jax.named_scope("second_layer"):
        energies, gmid, far, near, z, lift_second, message_second, ga = call(
            second_kernel,
            [((1, OWN), f32), ((128, C), f32), plane_rows, plane_rows, by_degree, edge_mat, message_mat, amp_mat],
            (first, slab_far, slab_near, far, near, sender_n, sender_t, angular, radial_second,
             up_second, skip_second, outs, gains, values, ref_row, read_row, hid, hidro, read_last),
            scratch=[pltpu.VMEM((9, OWN, C), f32), pltpu.VMEM((EDGES, 2 * C), bf16)],
            name="second_layer",
        )
    with jax.named_scope("feature_grads_plane"):
        far, near, z, slope_first = lax.optimization_barrier((far, near, z, slope_first))
        far, near = both(swap_plane_far, swap_plane_near, far, near)
    early, = call(
        early_kernel, [edge_rows], (z, slope_second, weights[3], lift_second, message_second, ga, geo, mask),
        scratch=[pltpu.VMEM((EDGES, 2 * C), bf16), pltpu.VMEM((8, EDGES), f32)],
        flops=1_000_000_000, name="early_forces",
    )
    slope_first, = call(
        functools.partial(expand_kernel, layer=0), [by_degree], (slope_first, weights[3]),
        flops=1_000_000_000, name="expand_first",
    )
    with jax.named_scope("feature_grads_slab"):
        own, far, near = call(
            back_middle_kernel, [plane_rows, slab_rows, slab_rows], (gmid, far, near, plane_t_far, plane_t_near),
            name="back_middle",
        )
        far, near = both(swap_slab_far, swap_slab_near, far, near)
    with jax.named_scope("late_forces"):
        own, slab_far, slab_near, far, near = call(
            late_kernel,
            [own_lanes, slab_lanes, slab_lanes, plane_lanes, plane_lanes],
            (own, far, near, slab_t_far, slab_t_near, outs, gains, amp_first, angular, slope_first,
             lift_first, message_first, geo, mask, edge_t, early),
            scratch=[pltpu.VMEM((9, OWN, C), f32), pltpu.VMEM((8, EDGES), f32), pltpu.VMEM((EDGES, 2 * C), bf16),
                     pltpu.VMEM((8, EDGES), f32)],
            name="late_forces",
        )
    with jax.named_scope("position_grads_plane"):
        far, near = both(swap_plane_far, swap_plane_near, far, near)
        own, far, near = call(
            collect_plane_kernel, [own_lanes, slab_lanes, slab_lanes],
            (own, slab_far, slab_near, far, near, plane_t_far, plane_t_near), name="collect_plane",
        )
    with jax.named_scope("position_grads_slab"):
        far, near = both(swap_slab_far, swap_slab_near, far, near)
        forces, = call(
            collect_slab_kernel, [((1, 3, 1, OWN), f32)], (own, far, near, slab_t_far, slab_t_near), name="collect_slab"
        )
    return (energies[None], jnp.transpose(forces, (0, 2, 1, 3)))


def solution(mesh):
    in_specs = (
        P("slab", "plane", None, None),
        P("slab", "plane", None),
        P("slab", "plane", None, None),
        P("slab", "plane", None, None),
        P("slab", "plane", None, None),
        P("slab", "plane"),
    ) + (P(),) * 13
    out_specs = (P("slab", "plane", None), P("slab", "plane", None, None))
    return jax.shard_map(body, mesh=mesh, in_specs=in_specs, out_specs=out_specs, check_vma=False)
```

```python
import functools

import jax
import jax.numpy as jnp
from jax import lax
from jax.experimental import pallas as pl
from jax.experimental.pallas import tpu as pltpu
from jax.sharding import PartitionSpec as P

CELLS_Y = 2
CELLS_Z = 2

cutoff_radius = 5.0
cell_side = 3.0
inverse_neighbours = 0.2
highest = lax.Precision.HIGHEST
f32 = jnp.float32
bf16 = jnp.bfloat16

C = 128
OWN = 64
EXT = 256
EDGES = 1536
BLOCKS = 4
GROUP = 16
SPAN = EDGES // BLOCKS
KINDS = 96
LMS = (1, 3, 5)
FIRST_LM = (0, 1, 4)
STACK_AT = (0, 48, 192)
STACK = 432
TURNED_AT = (0, 128, 384)
TURNED = 640
R3, R5, R15 = 3.0**0.5, 5.0**0.5, 15.0**0.5

NN = (((1,), (0,)), ((), ()))
TN = (((0,), (0,)), ((), ()))
NT = (((1,), (1,)), ((), ()))


def dot(a, b, dims=NN):
    return lax.dot_general(a, b, dims, preferred_element_type=f32)


def dot3(a, b, dims=NN):
    return lax.dot_general(a, b, dims, precision=lax.Precision.HIGH, preferred_element_type=f32)


def exact(a, b, dims=NN):
    return lax.dot_general(a, b, dims, precision=highest, preferred_element_type=f32)


def split(x):
    hi = x.astype(bf16)
    return hi, (x - hi.astype(f32)).astype(bf16)


def pair_lanes(x):
    hi, lo = split(x)
    return jnp.concatenate([hi, lo], axis=1)


def halves(o):
    return o[:, :C] + o[:, C:]


def stack_rows(x):
    hi, lo = split(x)
    return jnp.concatenate([hi, lo, hi], axis=0)


def three(x):
    hi = x.astype(bf16).astype(f32)
    rest = x - hi
    mid = rest.astype(bf16).astype(f32)
    return hi, mid, rest - mid


def pick_lanes(values, chooser, dims=NN):
    hi, mid, lo = three(values)
    o = dot(jnp.concatenate([hi, mid, lo, jnp.zeros_like(lo)], axis=0).astype(bf16), chooser, dims)
    return (o[0:8] + o[8:16]) + o[16:24]


def pick_rows(chooser, values, dims=NN):
    hi, mid, lo = three(values)
    o = dot(chooser, jnp.concatenate([hi, mid, lo], axis=1).astype(bf16), dims)
    return (o[:, :C] + o[:, C : 2 * C]) + o[:, 2 * C :]


def silu(x):
    return x * (1.0 / (1.0 + jnp.exp(-x)))


def silu_pair(x):
    s = 1.0 / (1.0 + jnp.exp(-x))
    return x * s, s * (1.0 + x * (1.0 - s))


def span(b):
    return pl.ds(b * SPAN, SPAN)


def fetched(kernel, count):
    def run(*refs):
        given, rest = refs[:count], refs[count:]
        sems, held = rest[-1], rest[-1 - count : -1]
        copies = [pltpu.make_async_copy(src, dst, sems.at[k]) for k, (src, dst) in enumerate(zip(given, held))]
        for copy in copies:
            copy.start()
        for copy in copies:
            copy.wait()
        kernel(*held, *rest[: -1 - count])

    return run


def call(kernel, outs, args, scratch=(), flops=0, name=None, limit=8, raw=False):
    spec = pl.BlockSpec(memory_space=pltpu.VMEM)
    out_shape = tuple(pltpu.VMEM(shape, dtype) for shape, dtype in outs)
    moved = sum(a.size * a.dtype.itemsize for a in args)
    scratch = list(scratch)
    if raw:
        big = [a for a in args if a.size > 1]
        scratch += [pltpu.VMEM(a.shape, a.dtype) for a in big] + [pltpu.SemaphoreType.DMA((len(big),))]
        kernel = fetched(kernel, len(big))
        in_specs = [pl.BlockSpec(memory_space=pltpu.HBM)] * len(big)
        in_specs += [pl.BlockSpec(memory_space=pltpu.SMEM)] * (len(args) - len(big))
        args = [pltpu.with_memory_space_constraint(a, pltpu.HBM) for a in big] + [a for a in args if a.size == 1]
    else:
        in_specs = [spec] * len(args)
        args = [pltpu.with_memory_space_constraint(a, pltpu.VMEM) for a in args]
    return pl.pallas_call(
        kernel,
        out_shape=out_shape,
        in_specs=in_specs,
        out_specs=tuple(spec for _ in out_shape),
        scratch_shapes=scratch,
        compiler_params=pltpu.CompilerParams(vmem_limit_bytes=limit * 1024 * 1024),
        cost_estimate=pl.CostEstimate(flops=flops, bytes_accessed=moved, transcendentals=0),
        name=name,
    )(*args)


def odd(axis):
    return lax.rem(lax.axis_index(axis), 2)


def by_parity(flag, rows):
    swap = jnp.full(rows[0:1].shape, flag) == 1
    return jnp.where(swap, rows[0:1], rows[1:2]), jnp.where(swap, rows[1:2], rows[0:1])


def moved_slab(slot):
    swap = (jnp.full(slot.shape, odd("slab")) == 1) & (slot >= 64) & (slot < 128)
    return jnp.where(swap, slot ^ 32, slot)


def chooser(slots, picked):
    rows = lax.broadcasted_iota(jnp.int32, (slots, picked.shape[1]), 0)
    return (rows == picked).astype(f32).astype(bf16)


def shifted(values, row, step):
    rows = lax.broadcasted_iota(jnp.int32, values.shape, 0)
    return values + jnp.where(rows == row, step, 0.0)


def atoms_slab_kernel(
    pos_ref, kind_ref, list_ref, plane_ref, v_ref, tf_ref, tn_ref, pf_ref, pn_ref, far_ref, near_ref
):
    for k in range(3):
        v_ref[k : k + 1, :] = pos_ref[0, k]
    v_ref[3:4, :] = kind_ref[...].astype(f32)
    v_ref[4:8, :] = jnp.zeros((4, OWN), f32)
    far, near = by_parity(odd("slab"), list_ref[...])
    far, near = chooser(OWN, far), chooser(OWN, near)
    tf_ref[...] = far
    tn_ref[...] = near
    v = v_ref[...]
    far_ref[...] = pick_lanes(v, far)
    near_ref[...] = pick_lanes(v, near)
    for picked, t_ref in zip(by_parity(odd("plane"), plane_ref[...]), (pf_ref, pn_ref)):
        t_ref[...] = chooser(128, moved_slab(picked))


def atoms_plane_kernel(v_ref, far_ref, near_ref, tf_ref, tn_ref, pf_ref, pn_ref, sf_ref, sn_ref):
    step = (2 * odd("slab") - 1).astype(f32) * (CELLS_Z * cell_side)
    far = shifted(far_ref[...], 2, step)
    near = shifted(near_ref[...], 2, -step)
    pf_ref[...] = far
    pn_ref[...] = near
    own = v_ref[...]
    for t_ref, s_ref in ((tf_ref, sf_ref), (tn_ref, sn_ref)):
        s_ref[...] = pick_lanes(own, t_ref[0:64, :]) + (
            pick_lanes(far, t_ref[64:96, :]) + pick_lanes(near, t_ref[96:128, :])
        )


def prepare_kernel(
    edge_ref, one_ref, two_ref, three_ref, four_ref, embed_ref, up_ref, skip_ref, atom_ref, hid_ref, ro_ref,
    out_ref, gain_ref, read_ref, count_ref,
    g_ref, gt_ref, dd_ref, mask_ref, w1_ref, w2_ref, w3_ref, w4_ref, table_ref, skips_ref, skipups_ref, refs_ref,
    from_first_ref, from_mix_ref, from_first_ro_ref, from_mix_ro_ref, outup_ref, out0_ref, gains_ref, reads_ref, ros_ref,
):
    per_atom = count_ref[0, 0] // OWN
    senders = jnp.broadcast_to(edge_ref[0:1, :], (8, EDGES))
    swap_plane = jnp.full((1, SPAN), odd("plane")) == 1
    place = lax.broadcasted_iota(jnp.int32, (GROUP, SPAN), 1)
    first_place = lax.broadcasted_iota(jnp.int32, (GROUP, SPAN), 0) * per_atom
    mask = ((place >= first_place) & (place < first_place + per_atom)).astype(f32)
    lanes = lax.broadcasted_iota(jnp.int32, (128, 128), 1).astype(f32)
    for b in range(BLOCKS):
        start = b * GROUP * per_atom
        rows = senders if b == 0 else pltpu.roll(senders, lax.rem(EDGES - start, EDGES), 1)
        row = rows[0:1, :SPAN]
        row = moved_slab(row)
        row = jnp.where(swap_plane & (row >= 128), row ^ 64, row)
        row = jnp.where(place[0:1] < GROUP * per_atom, row, -1)
        t = (lax.broadcasted_iota(jnp.int32, (EXT, SPAN), 0) == row).astype(f32)
        gt_ref[:, span(b)] = t.astype(bf16)
        dd_ref[:, span(b)] = t.astype(bf16)
        mine = pl.ds(b * GROUP, GROUP)
        dd_ref[mine, span(b)] = (t[b * GROUP : (b + 1) * GROUP] - mask).astype(bf16)
        mask_ref[:, span(b)] = mask
        for chunk in range(SPAN // 128):
            part = row[:, chunk * 128 : (chunk + 1) * 128].astype(f32)
            column = jnp.transpose(jnp.broadcast_to(part, (128, 128)))
            here = pl.ds(b * SPAN + chunk * 128, 128)
            g_ref[here, 0:128] = (column == lanes).astype(f32).astype(bf16)
            g_ref[here, 128:256] = (column == lanes + 128.0).astype(f32).astype(bf16)
    for t in range(2):
        hi, mid, lo = three(one_ref[t])
        stacked = jnp.concatenate([hi, hi, mid + lo, jnp.zeros_like(hi)], axis=0)
        w1_ref[t] = jnp.transpose(stacked).astype(bf16)
        for ref, to_ref in ((two_ref, w2_ref), (three_ref, w3_ref)):
            hi, mid, lo = three(ref[t])
            to_ref[t] = jnp.transpose(jnp.concatenate([hi, hi, mid + lo], axis=0)).astype(bf16)
        hi, lo = split(four_ref[t])
        w4_ref[t] = jnp.concatenate([hi, hi, lo], axis=0)
    embed = embed_ref[...]
    kinds = embed.shape[0]
    for ref in (table_ref, skips_ref, skipups_ref):
        ref[...] = jnp.zeros(ref.shape, bf16)
    table_ref[0:kinds, :] = pair_lanes(exact(embed, up_ref[0]))
    skipped = exact(embed, skip_ref[0])
    for ref, values in ((skips_ref, skipped), (skipups_ref, exact(skipped, up_ref[1]))):
        hi, mid, lo = three(values)
        ref[0:kinds, :] = jnp.concatenate([hi, mid, lo], axis=1).astype(bf16)
    refs_ref[...] = jnp.zeros(refs_ref.shape, f32)
    refs_ref[0:1, 0:kinds] = atom_ref[...]
    last = jnp.transpose(jnp.broadcast_to(ro_ref[...], (C, ro_ref.shape[1])))
    from_first = exact(hid_ref[...], skip_ref[1], NT)
    from_mix = exact(hid_ref[...], out_ref[1], NT)
    from_first_ref[...] = from_first
    from_mix_ref[...] = from_mix
    from_first_ro_ref[...] = from_first * last
    from_mix_ro_ref[...] = from_mix * last
    outup_ref[...] = exact(out_ref[0], up_ref[1])
    out0_ref[...] = out_ref[0]
    gains_ref[...] = gain_ref[...]
    reads_ref[...] = read_ref[...]
    ros_ref[...] = jnp.broadcast_to(ro_ref[...], ros_ref.shape)


def kinds_of(row):
    kinds = lax.broadcasted_iota(jnp.int32, (KINDS, row.shape[1]), 0).astype(f32) == row
    return kinds.astype(f32)


def near_atoms_kernel(v_ref, pf_ref, pn_ref, dd_ref, table_ref, vector_ref, lifted_ref):
    vector, at = None, 0
    for ref in (v_ref, pf_ref, pn_ref):
        rows = ref.shape[1]
        piece = pick_lanes(ref[...], dd_ref[at : at + rows, :])
        vector = piece if vector is None else vector + piece
        lifted_ref[at : at + rows, :] = dot(kinds_of(ref[3:4, :]).astype(bf16), table_ref[...], TN).astype(bf16)
        at += rows
    vector_ref[...] = vector


def geometry(v, valid, b_ref, db_ref, geo_ref):
    vx = jnp.where(valid, v[0:1], 2.0 * cutoff_radius)
    vy = jnp.where(valid, v[1:2], 0.0)
    vz = jnp.where(valid, v[2:3], 0.0)
    d = jnp.sqrt(vx * vx + vy * vy + vz * vz)
    inv = 1.0 / d
    geo_ref[0:1, :] = vx * inv
    geo_ref[1:2, :] = vy * inv
    geo_ref[2:3, :] = vz * inv
    geo_ref[3:4, :] = inv
    s = d / cutoff_radius
    s2 = s * s
    s4 = s2 * s2
    s5 = s4 * s
    s6 = s4 * s2
    s7 = s6 * s
    inside = (s < 1.0) & valid
    u = 1.0 - 28.0 * s6 + 48.0 * s7 - 21.0 * s4 * s4
    du = (-168.0 * s5 + 336.0 * s6 - 168.0 * s7) / cutoff_radius
    geo_ref[4:5, :] = jnp.where(inside, u * inverse_neighbours, 0.0)
    geo_ref[5:6, :] = jnp.where(inside, du * inverse_neighbours, 0.0)
    geo_ref[6:8, :] = jnp.zeros_like(geo_ref[6:8, :])
    t = (jnp.minimum(s, 1.0) - 0.5) * jnp.pi
    z = t * t
    cs = 1.0 - z * (1 / 2 - z * (1 / 24 - z * (1 / 720 - z * (1 / 40320 - z * (1 / 3628800 - z * (1 / 479001600 - z * (1 / 87178291200)))))))
    sn = 1.0 - z * (1 / 6 - z * (1 / 120 - z * (1 / 5040 - z * (1 / 362880 - z * (1 / 39916800 - z * (1 / 6227020800))))))
    s1, c1 = cs, -t * sn

    def plus(a, b):
        return a[0] * b[1] + a[1] * b[0], a[1] * b[1] - a[0] * b[0]

    w1 = (s1, c1)
    w2 = plus(w1, w1)
    w3 = plus(w2, w1)
    w4 = plus(w2, w2)
    waves = (w1, w2, w3, w4, plus(w4, w1), plus(w4, w2), plus(w4, w3), plus(w4, w4))
    gain = (2.0 / cutoff_radius) ** 0.5 * inv
    for n, (sine, cosine) in enumerate(waves):
        b_ref[n : n + 1, :] = gain * sine
        db_ref[n : n + 1, :] = gain * (cosine * ((n + 1) * jnp.pi / cutoff_radius) - sine * inv)


def basis_stack(x):
    hi, mid, _ = three(x)
    lo = x - hi
    return jnp.concatenate([hi, lo, hi, jnp.zeros_like(hi)], axis=0).astype(bf16)


def radial_hidden(b, w1, w2, w3):
    h = silu(dot(w1, basis_stack(b)))
    h = silu(dot(w2, stack_rows(h)))
    return silu(dot(w3, stack_rows(h)))


def radial_hidden_pair(b, db, w1, w2, w3):
    h, g = silu_pair(dot(w1, basis_stack(b)))
    t = g * dot(w1, basis_stack(db))
    h, g = silu_pair(dot(w2, stack_rows(h)))
    t = g * dot(w2, stack_rows(t))
    h, g = silu_pair(dot(w3, stack_rows(h)))
    t = g * dot(w3, stack_rows(t))
    return h, t


def angular_rows(geo):
    x, y, z = geo[0:1], geo[1:2], geo[2:3]
    return (
        jnp.ones_like(x),
        R3 * x,
        R3 * y,
        R3 * z,
        R15 * x * y,
        R15 * y * z,
        0.5 * R5 * (3.0 * z * z - 1.0),
        R15 * x * z,
        0.5 * R15 * (x * x - y * y),
    )


def messages(g_ref, lifted, radial_of, l_ref, m_ref):
    for b in range(BLOCKS):
        lift = halves(dot(g_ref[span(b), :], lifted))
        l_ref[span(b), :] = lift
        radial = radial_of(b)
        for l in range(3):
            m_ref[l, span(b), :] = pair_lanes(radial[:, l * C : (l + 1) * C] * lift)


def amplitudes(ast_ref, m_ref, amp_ref):
    for b in range(BLOCKS):
        for l in range(3):
            n = LMS[l]
            o = dot(ast_ref[pl.ds(b * STACK + STACK_AT[l], 32 * n), :], m_ref[l, span(b), :])
            amp = halves(o[: 16 * n]) + o[16 * n :, :C]
            for k in range(n):
                amp_ref[FIRST_LM[l] + k, pl.ds(b * GROUP, GROUP), :] = amp[16 * k : 16 * (k + 1)]


def invariants(amp_ref, gain):
    b0 = amp_ref[0]
    b1 = sum(amp_ref[k] * amp_ref[k] for k in range(1, 4))
    b2 = sum(amp_ref[k] * amp_ref[k] for k in range(4, 9))
    return gain[0:1] * b0 + gain[1:2] * b1 + gain[2:3] * b2 + gain[3:4] * b0 * b0


def amp_grads(amp_ref, gain, gm, ga_ref):
    ga_ref[0] = gm * (gain[0:1] + 2.0 * gain[3:4] * amp_ref[0])
    one = gm * (2.0 * gain[1:2])
    two = gm * (2.0 * gain[2:3])
    for k in range(1, 4):
        ga_ref[k] = one * amp_ref[k]
    for k in range(4, 9):
        ga_ref[k] = two * amp_ref[k]


def group_grads(ga_ref, b, l):
    return jnp.concatenate(
        [ga_ref[FIRST_LM[l] + k, pl.ds(b * GROUP, GROUP), :] for k in range(LMS[l])], axis=0
    )


def spread(turned_ref, ga_ref, b, l):
    hi, lo = split(group_grads(ga_ref, b, l))
    angular = turned_ref[span(b), TURNED_AT[l] : TURNED_AT[l] + 48 * LMS[l]]
    return dot(angular, jnp.concatenate([hi, hi, lo], axis=0))


def angular_grads(m_ref, ga_ref, mask_ref, gy_ref):
    for b in range(BLOCKS):
        mask = mask_ref[:, span(b)]
        for l in (1, 2):
            n = LMS[l]
            hi, lo = split(group_grads(ga_ref, b, l))
            left = jnp.concatenate(
                [jnp.concatenate([hi, hi], axis=1), jnp.concatenate([lo, jnp.zeros_like(lo)], axis=1)],
                axis=0,
            )
            w = dot(left, m_ref[l, span(b), :], NT)
            w = w[: 16 * n] + w[16 * n :]
            for k in range(n):
                row = FIRST_LM[l] + k - 1
                gy_ref[row : row + 1, span(b)] = jnp.sum(mask * w[16 * k : 16 * (k + 1)], axis=0, keepdims=True)


def edge_forces(x_ref, gy_ref, geo_ref, gv_ref):
    gd = dot(jnp.ones((16, 2 * C), bf16), x_ref[...], NT)[0:1]
    gy = [None] + [gy_ref[k : k + 1, :] for k in range(8)]
    x, y, z, inv = (geo_ref[k : k + 1, :] for k in range(4))
    gx = R3 * gy[1] + R15 * (y * gy[4] + z * gy[7] + x * gy[8])
    gyy = R3 * gy[2] + R15 * (x * gy[4] + z * gy[5] - y * gy[8])
    gz = R3 * gy[3] + R15 * (y * gy[5] + x * gy[7]) + (3.0 * R5) * z * gy[6]
    along = x * gx + y * gyy + z * gz
    core = gd - along * inv
    gv_ref[0:1, :] = core * x + gx * inv
    gv_ref[1:2, :] = core * y + gyy * inv
    gv_ref[2:3, :] = core * z + gz * inv
    gv_ref[3:8, :] = jnp.zeros((5, EDGES), f32)


def first_kernel(
    v_ref, vector_ref, lifted_ref, qf_ref, qn_ref, dd_ref, g_ref, mask_ref, table_ref, skip_ref, w1_ref, w2_ref, w3_ref, w4_ref,
    gain_ref, outup_ref, tf_ref, tn_ref,
    f_ref, sf_ref, sn_ref, mix_ref, amp_ref, l_ref, m_ref, ast_ref, b_ref, db_ref, geo_ref,
):
    step = (2 * odd("plane") - 1).astype(f32) * (CELLS_Y * cell_side)
    far, near = shifted(qf_ref[...], 1, step), shifted(qn_ref[...], 1, -step)
    valid = jnp.sum(mask_ref[...], axis=0, keepdims=True) > 0.5
    vector = vector_ref[...] + (pick_lanes(far, dd_ref[128:192, :]) + pick_lanes(near, dd_ref[192:256, :]))
    lifted = [dot(kinds_of(part[3:4]).astype(bf16), table_ref[...], TN).astype(bf16) for part in (far, near)]
    lifted = jnp.concatenate([lifted_ref[...]] + lifted, axis=0)
    o = dot(kinds_of(v_ref[3:4, :]).astype(bf16), skip_ref[...], TN)
    skipped = (o[:, :C] + o[:, C : 2 * C]) + o[:, 2 * C :]
    geometry(vector, valid, b_ref, db_ref, geo_ref)
    h = stack_rows(radial_hidden(b_ref[...], w1_ref[0], w2_ref[0], w3_ref[0]) * geo_ref[4:5, :])
    rows = angular_rows(geo_ref[0:3, :])
    for b in range(BLOCKS):
        mask = mask_ref[:, span(b)]
        for l in range(3):
            a = jnp.concatenate(
                [mask * rows[FIRST_LM[l] + k][:, b * SPAN : (b + 1) * SPAN] for k in range(LMS[l])], axis=0
            )
            ast_ref[pl.ds(b * STACK + STACK_AT[l], 48 * LMS[l]), :] = stack_rows(a)
    messages(g_ref, lifted, lambda b: dot(h[:, b * SPAN : (b + 1) * SPAN], w4_ref[0], TN), l_ref, m_ref)
    amplitudes(ast_ref, m_ref, amp_ref)
    mix = invariants(amp_ref, gain_ref[0])
    mix_ref[...] = mix
    lifted = skipped + dot3(mix, outup_ref[...])
    f_ref[...] = lifted
    sf_ref[...] = pick_rows(tf_ref[...], lifted, TN)
    sn_ref[...] = pick_rows(tn_ref[...], lifted, TN)


def own_terms_kernel(v_ref, mix_ref, skip_ref, out0_ref, ref_ref, one_ref, from_first_ref, hid_ref, e_ref):
    kinds = kinds_of(v_ref[3:4, :])
    o = dot(kinds.astype(bf16), skip_ref[...], TN)
    first = ((o[:, :C] + o[:, C : 2 * C]) + o[:, 2 * C :]) + exact(mix_ref[...], out0_ref[...])
    hid_ref[...] = exact(from_first_ref[...], first, NT)
    e_ref[...] = exact(ref_ref[...], kinds) + exact(jnp.broadcast_to(one_ref[...], (8, C)), first, NT)


def middle_kernel(f_ref, rf_ref, rn_ref, pf_ref, pn_ref, a_ref, b_ref):
    rows = jnp.concatenate([f_ref[...], rf_ref[...], rn_ref[...]], axis=0)
    a_ref[...] = pick_rows(pf_ref[...], rows, TN)
    b_ref[...] = pick_rows(pn_ref[...], rows, TN)


def slope_kernel(b_ref, db_ref, geo_ref, w1_ref, w2_ref, w3_ref, q_ref, *, layer):
    h, t = radial_hidden_pair(b_ref[...], db_ref[...], w1_ref[layer], w2_ref[layer], w3_ref[layer])
    q_ref[...] = stack_rows(t * geo_ref[4:5, :] + h * geo_ref[5:6, :])


def radial_kernel(b_ref, db_ref, geo_ref, w1_ref, w2_ref, w3_ref, w4_ref, r_ref, q_ref, *, layer):
    h, t = radial_hidden_pair(b_ref[...], db_ref[...], w1_ref[layer], w2_ref[layer], w3_ref[layer])
    q_ref[...] = stack_rows(t * geo_ref[4:5, :] + h * geo_ref[5:6, :])
    h = stack_rows(h * geo_ref[4:5, :])
    for b in range(BLOCKS):
        r_ref[span(b), :] = dot(h[:, b * SPAN : (b + 1) * SPAN], w4_ref[layer], TN)


def expand_kernel(q_ref, w4_ref, r_ref, *, layer):
    for b in range(BLOCKS):
        r_ref[span(b), :] = dot(q_ref[:, span(b)], w4_ref[layer], TN)


def beside_features_kernel(
    b_ref, db_ref, geo_ref, w1_ref, w2_ref, w3_ref, w4_ref, v_ref, mix_ref, skip_ref, out0_ref, ref_ref, one_ref, from_first_ref,
    ast_ref, r_ref, second_q_ref, first_q_ref, hid_ref, e_ref, turned_ref,
):
    for b in range(BLOCKS):
        for l in range(3):
            rows = ast_ref[pl.ds(b * STACK + STACK_AT[l], 48 * LMS[l]), :]
            turned_ref[span(b), TURNED_AT[l] : TURNED_AT[l] + 48 * LMS[l]] = jnp.transpose(rows)
    slope_kernel(b_ref, db_ref, geo_ref, w1_ref, w2_ref, w3_ref, first_q_ref, layer=0)
    radial_kernel(b_ref, db_ref, geo_ref, w1_ref, w2_ref, w3_ref, w4_ref, r_ref, second_q_ref, layer=1)
    own_terms_kernel(v_ref, mix_ref, skip_ref, out0_ref, ref_ref, one_ref, from_first_ref, hid_ref, e_ref)


def second_kernel(
    f_ref, rf_ref, rn_ref, pf_ref, pn_ref, g_ref, gt_ref, ast_ref, turned_ref, r_ref, gain_ref, hid_ref, from_mix_ref, from_mix_ro_ref,
    act_ref, slope_ref, gmid_ref, gf_ref, gn_ref, l_ref, m_ref, ga_ref,
    amp_ref, glift_ref,
):
    lifted = pair_lanes(
        jnp.concatenate([f_ref[...], rf_ref[...], rn_ref[...], pf_ref[...], pn_ref[...]], axis=0)
    )
    messages(g_ref, lifted, lambda b: r_ref[span(b), :], l_ref, m_ref)
    amplitudes(ast_ref, m_ref, amp_ref)
    gain = gain_ref[1]
    act, slope = silu_pair(hid_ref[...] + exact(from_mix_ref[...], invariants(amp_ref, gain), NT))
    act_ref[...] = act
    slope_ref[...] = slope
    amp_grads(amp_ref, gain, dot3(slope, from_mix_ro_ref[...], TN), ga_ref)
    for b in range(BLOCKS):
        grad = None
        for l in range(3):
            term = r_ref[span(b), l * C : (l + 1) * C] * spread(turned_ref, ga_ref, b, l)
            grad = term if grad is None else grad + term
        glift_ref[span(b), :] = pair_lanes(grad)
    glift = halves(dot(gt_ref[...], glift_ref[...]))
    gmid_ref[...] = glift[0:128]
    gf_ref[...] = glift[128:192]
    gn_ref[...] = glift[192:256]


def own_grads_kernel(act_ref, slope_ref, e0_ref, ro_ref, from_first_ro_ref, one_ref, out0_ref, e_ref, gm_ref):
    e_ref[...] = (e0_ref[...] + exact(ro_ref[...], act_ref[...]))[0:1]
    grad = dot3(slope_ref[...], from_first_ro_ref[...], TN) + one_ref[...]
    gm_ref[...] = dot3(grad, out0_ref[...], NT)


def early_kernel(turned_ref, q_ref, w4_ref, l_ref, m_ref, ga_ref, geo_ref, mask_ref, gv_ref, x_ref, gy_ref):
    for b in range(BLOCKS):
        slope = dot(q_ref[:, span(b)], w4_ref[1], TN)
        x = sum(spread(turned_ref, ga_ref, b, l) * slope[:, l * C : (l + 1) * C] for l in range(3))
        x_ref[span(b), :] = pair_lanes(x * l_ref[span(b), :])
    angular_grads(m_ref, ga_ref, mask_ref, gy_ref)
    edge_forces(x_ref, gy_ref, geo_ref, gv_ref)


def beside_grads_kernel(
    turned_ref, second_q_ref, w4_ref, l_ref, m_ref, ga_ref, geo_ref, mask_ref, first_q_ref,
    act_ref, slope_ref, e0_ref, ro_ref, from_first_ro_ref, one_ref, out0_ref,
    gv_ref, dr_ref, e_ref, gm_ref, x_ref, gy_ref,
):
    early_kernel(turned_ref, second_q_ref, w4_ref, l_ref, m_ref, ga_ref, geo_ref, mask_ref, gv_ref, x_ref, gy_ref)
    expand_kernel(first_q_ref, w4_ref, dr_ref, layer=0)
    own_grads_kernel(act_ref, slope_ref, e0_ref, ro_ref, from_first_ro_ref, one_ref, out0_ref, e_ref, gm_ref)


def back_middle_kernel(gmid_ref, rf_ref, rn_ref, pf_ref, pn_ref, own_ref, f_ref, n_ref):
    mid = gmid_ref[...] + (pick_rows(pf_ref[...], rf_ref[...]) + pick_rows(pn_ref[...], rn_ref[...]))
    own_ref[...] = mid[:64]
    f_ref[...] = mid[64:96]
    n_ref[...] = mid[96:128]


def late_kernel(
    own_ref, rf_ref, rn_ref, tf_ref, tn_ref, gm_ref, outup_ref, gain_ref, amp_ref, turned_ref, dr_ref, l_ref, m_ref, geo_ref,
    mask_ref, dd_ref, early_ref, of_ref, pf_ref, pn_ref, qf_ref, qn_ref, ga_ref, gv_ref, x_ref, gy_ref,
):
    grad = own_ref[...] + (pick_rows(tf_ref[...], rf_ref[...]) + pick_rows(tn_ref[...], rn_ref[...]))
    amp_grads(amp_ref, gain_ref[0], gm_ref[...] + dot3(grad, outup_ref[...], NT), ga_ref)
    for b in range(BLOCKS):
        x = None
        for l in range(3):
            term = spread(turned_ref, ga_ref, b, l) * dr_ref[span(b), l * C : (l + 1) * C]
            x = term if x is None else x + term
        x_ref[span(b), :] = pair_lanes(x * l_ref[span(b), :])
    angular_grads(m_ref, ga_ref, mask_ref, gy_ref)
    edge_forces(x_ref, gy_ref, geo_ref, gv_ref)
    total = gv_ref[...] + early_ref[...]
    at = 0
    for ref in (of_ref, pf_ref, pn_ref, qf_ref, qn_ref):
        rows = ref.shape[1]
        ref[...] = pick_lanes(total, dd_ref[at : at + rows, :], NT)
        at += rows


def collect_plane_kernel(of_ref, pf_ref, pn_ref, rf_ref, rn_ref, tf_ref, tn_ref, o_ref, f_ref, n_ref):
    far, near, at = rf_ref[...], rn_ref[...], 0
    for have_ref, ref in ((of_ref, o_ref), (pf_ref, f_ref), (pn_ref, n_ref)):
        rows = ref.shape[1]
        back = pick_lanes(far, tf_ref[at : at + rows, :], NT) + pick_lanes(near, tn_ref[at : at + rows, :], NT)
        ref[...] = have_ref[...] + back
        at += rows


def collect_slab_kernel(v_ref, rf_ref, rn_ref, tf_ref, tn_ref, o_ref):
    back = pick_lanes(rf_ref[...], tf_ref[...], NT) + pick_lanes(rn_ref[...], tn_ref[...], NT)
    forces = -(v_ref[...] + back)
    for k in range(3):
        o_ref[0, k] = forces[k : k + 1]


def swap_slab_far(value):
    count = lax.axis_size("slab")
    pairs = [(i, i + 1) for i in range(1, count - 1, 2)]
    return lax.ppermute(value, "slab", pairs + [(b, a) for a, b in pairs])


def swap_slab_near(value):
    count = lax.axis_size("slab")
    return lax.ppermute(value, "slab", [(i, i ^ 1) for i in range(count)])


def swap_plane_far(value):
    count = lax.axis_size("plane")
    pairs = [(i, (i + 1) % count) for i in range(1, count, 2)]
    return lax.ppermute(value, "plane", pairs + [(b, a) for a, b in pairs])


def swap_plane_near(value):
    count = lax.axis_size("plane")
    return lax.ppermute(value, "plane", [(i, i ^ 1) for i in range(count)])


def both(swap_far, swap_near, far, near):
    return swap_far(far), swap_near(near)


def body(
    positions,
    species,
    slab_sends,
    plane_sends,
    edges,
    edge_count,
    embed_table,
    atom_ref,
    radial_one,
    radial_two,
    radial_three,
    radial_four,
    up_weight,
    skip_weight,
    out_weight,
    prod_weight,
    read_one,
    read_hidden,
    read_out,
):
    edge_mat = ((EDGES, C), f32)
    message_mat = ((3, EDGES, 2 * C), bf16)
    by_degree = ((EDGES, 3 * C), f32)
    edge_rows = ((8, EDGES), f32)
    amp_mat = ((9, OWN, C), f32)
    slab_rows = ((32, C), f32)
    plane_rows = ((64, C), f32)
    own_lanes = ((8, OWN), f32)
    slab_lanes = ((8, 32), f32)
    plane_lanes = ((8, 64), f32)

    with jax.named_scope("atoms_slab"):
        values, slab_t_far, slab_t_near, plane_t_far, plane_t_near, far, near = call(
            atoms_slab_kernel,
            [own_lanes, ((OWN, 32), bf16), ((OWN, 32), bf16), ((128, 64), bf16), ((128, 64), bf16), slab_lanes, slab_lanes],
            (jnp.transpose(positions, (0, 2, 1, 3)), species[0], slab_sends[0, 0], plane_sends[0, 0]),
            raw=True,
            name="atoms_slab",
        )
        far, near = both(swap_slab_far, swap_slab_near, far, near)
    with jax.named_scope("atoms_plane"):
        slab_far, slab_near, far, near = call(
            atoms_plane_kernel,
            [slab_lanes, slab_lanes, plane_lanes, plane_lanes],
            (values, far, near, plane_t_far, plane_t_near),
            name="atoms_plane",
        )
        edge_list, far, near = lax.optimization_barrier((edges[0, 0], far, near))
        far, near = both(swap_plane_far, swap_plane_near, far, near)
    with jax.named_scope("prepare"):
        sender_n, sender_t, edge_t, mask, *prepared = call(
            prepare_kernel,
            [((EDGES, EXT), bf16), ((EXT, EDGES), bf16), ((EXT, EDGES), bf16), ((GROUP, EDGES), f32),
             ((2, 64, 32), bf16), ((2, 64, 192), bf16), ((2, 64, 192), bf16), ((2, 192, 3 * C), bf16),
             ((KINDS, 2 * C), bf16), ((KINDS, 3 * C), bf16), ((KINDS, 3 * C), bf16), ((8, KINDS), f32),
             *[((16, C), f32)] * 4, ((C, C), f32), ((C, C), f32), ((2, 4, C), f32), ((1, C), f32), ((8, 16), f32)],
            (edge_list, radial_one, radial_two, radial_three, radial_four, embed_table, up_weight, skip_weight,
             atom_ref[None, :], jnp.transpose(read_hidden), read_out[None, :], out_weight, prod_weight,
             read_one[None, :], edge_count),
            raw=True,
            flops=1_000_000_000,
            name="prepare",
        )
        weights = tuple(prepared[:4])
        (table, skip_table, skip_up_table, ref_row, from_first, from_mix, from_first_ro, from_mix_ro, out_up, out_first,
         gains, read_row, read_last) = prepared[4:]
        vector, lifted = call(
            near_atoms_kernel, [edge_rows, ((128, 2 * C), bf16)], (values, slab_far, slab_near, edge_t, table),
            flops=1_000_000_000, name="near_atoms",
        )

    hidden_mat = ((16, OWN), f32)
    with jax.named_scope("first_layer"):
        far, near, vector, lifted = lax.optimization_barrier((far, near, vector, lifted))
        (first, s_far, s_near, mix, amp_first, lift_first, message_first, angular, basis, basis_slope, geo) = call(
            first_kernel,
            [plane_rows, slab_rows, slab_rows, plane_rows, amp_mat, edge_mat, message_mat,
             ((BLOCKS * STACK, SPAN), bf16), edge_rows, edge_rows, edge_rows],
            (values, vector, lifted, far, near, edge_t, sender_n, mask, table, skip_up_table, *weights,
             gains, out_up, slab_t_far, slab_t_near),
            name="first_layer",
        )
    with jax.named_scope("features_slab"):
        slab_far, slab_near = both(swap_slab_far, swap_slab_near, s_far, s_near)
    with jax.named_scope("features_plane"):
        far, near = call(
            middle_kernel, [plane_rows] * 2, (first, slab_far, slab_near, plane_t_far, plane_t_near), name="middle"
        )
        far, near, basis, geo, mix = lax.optimization_barrier((far, near, basis, geo, mix))
        far, near = both(swap_plane_far, swap_plane_near, far, near)
    radial_second, slope_second, slope_first, hidden, energies, turned = call(
        beside_features_kernel,
        [by_degree, ((192, EDGES), bf16), ((192, EDGES), bf16), hidden_mat, own_lanes, ((EDGES, TURNED), bf16)],
        (basis, basis_slope, geo, *weights, values, mix, skip_table, out_first, ref_row, read_row, from_first,
         angular),
        flops=1_000_000_000, name="beside_features",
    )
    with jax.named_scope("second_layer"):
        act, slope, gmid, far, near, lift_second, message_second, ga = call(
            second_kernel,
            [hidden_mat, hidden_mat, ((128, C), f32), plane_rows, plane_rows, edge_mat, message_mat, amp_mat],
            (first, slab_far, slab_near, far, near, sender_n, sender_t, angular, turned, radial_second, gains, hidden, from_mix,
             from_mix_ro),
            scratch=[pltpu.VMEM((9, OWN, C), f32), pltpu.VMEM((EDGES, 2 * C), bf16)],
            name="second_layer",
        )
    with jax.named_scope("feature_grads_plane"):
        far, near, ga = lax.optimization_barrier((far, near, ga))
        far, near = both(swap_plane_far, swap_plane_near, far, near)
    early, slope_first, energies, own_grads = call(
        beside_grads_kernel,
        [edge_rows, by_degree, ((1, OWN), f32), plane_rows],
        (turned, slope_second, weights[3], lift_second, message_second, ga, geo, mask, slope_first,
         act, slope, energies, read_last, from_first_ro, read_row, out_first),
        scratch=[pltpu.VMEM((EDGES, 2 * C), bf16), pltpu.VMEM((8, EDGES), f32)],
        flops=1_000_000_000, name="beside_grads",
    )
    with jax.named_scope("feature_grads_slab"):
        far, near, early = lax.optimization_barrier((far, near, early))
        own, far, near = call(
            back_middle_kernel, [plane_rows, slab_rows, slab_rows], (gmid, far, near, plane_t_far, plane_t_near),
            name="back_middle",
        )
        far, near = both(swap_slab_far, swap_slab_near, far, near)
    with jax.named_scope("late_forces"):
        own, slab_far, slab_near, far, near = call(
            late_kernel,
            [own_lanes, slab_lanes, slab_lanes, plane_lanes, plane_lanes],
            (own, far, near, slab_t_far, slab_t_near, own_grads, out_up, gains, amp_first, turned, slope_first,
             lift_first, message_first, geo, mask, edge_t, early),
            scratch=[pltpu.VMEM((9, OWN, C), f32), pltpu.VMEM((8, EDGES), f32), pltpu.VMEM((EDGES, 2 * C), bf16),
                     pltpu.VMEM((8, EDGES), f32)],
            name="late_forces",
        )
    with jax.named_scope("position_grads_plane"):
        far, near = both(swap_plane_far, swap_plane_near, far, near)
        own, far, near = call(
            collect_plane_kernel, [own_lanes, slab_lanes, slab_lanes],
            (own, slab_far, slab_near, far, near, plane_t_far, plane_t_near), name="collect_plane",
        )
    with jax.named_scope("position_grads_slab"):
        far, near = both(swap_slab_far, swap_slab_near, far, near)
        forces, = call(
            collect_slab_kernel, [((1, 3, 1, OWN), f32)], (own, far, near, slab_t_far, slab_t_near), name="collect_slab"
        )
    return (energies[None], jnp.transpose(forces, (0, 2, 1, 3)))


def solution(mesh):
    in_specs = (
        P("slab", "plane", None, None),
        P("slab", "plane", None),
        P("slab", "plane", None, None),
        P("slab", "plane", None, None),
        P("slab", "plane", None, None),
        P("slab", "plane"),
    ) + (P(),) * 13
    out_specs = (P("slab", "plane", None), P("slab", "plane", None, None))
    return jax.shard_map(body, mesh=mesh, in_specs=in_specs, out_specs=out_specs, check_vma=False)
```

```python
import functools

import jax
import jax.numpy as jnp
from jax import lax
from jax.experimental import pallas as pl
from jax.experimental.pallas import tpu as pltpu
from jax.sharding import PartitionSpec as P

CELLS_Y = 2
CELLS_Z = 2

cutoff_radius = 5.0
cell_side = 3.0
inverse_neighbours = 0.2
highest = lax.Precision.HIGHEST
f32 = jnp.float32
bf16 = jnp.bfloat16

C = 128
OWN = 64
EXT = 256
EDGES = 1536
BLOCKS = 4
GROUP = 16
SPAN = EDGES // BLOCKS
KINDS = 96
LMS = (1, 3, 5)
FIRST_LM = (0, 1, 4)
STACK_AT = (0, 48, 192)
STACK = 432
TURNED_AT = (0, 128, 384)
TURNED = 640
R3, R5, R15 = 3.0**0.5, 5.0**0.5, 15.0**0.5

NN = (((1,), (0,)), ((), ()))
TN = (((0,), (0,)), ((), ()))
NT = (((1,), (1,)), ((), ()))


def dot(a, b, dims=NN):
    return lax.dot_general(a, b, dims, preferred_element_type=f32)


def dot3(a, b, dims=NN):
    return lax.dot_general(a, b, dims, precision=lax.Precision.HIGH, preferred_element_type=f32)


def exact(a, b, dims=NN):
    return lax.dot_general(a, b, dims, precision=highest, preferred_element_type=f32)


def split(x):
    hi = x.astype(bf16)
    return hi, (x - hi.astype(f32)).astype(bf16)


def pair_lanes(x):
    hi, lo = split(x)
    return jnp.concatenate([hi, lo], axis=1)


def halves(o):
    return o[:, :C] + o[:, C:]


def stack_rows(x):
    hi, lo = split(x)
    return jnp.concatenate([hi, lo, hi], axis=0)


def three(x):
    hi = x.astype(bf16).astype(f32)
    rest = x - hi
    mid = rest.astype(bf16).astype(f32)
    return hi, mid, rest - mid


def pick_lanes(values, chooser, dims=NN):
    hi, mid, lo = three(values)
    o = dot(jnp.concatenate([hi, mid, lo, jnp.zeros_like(lo)], axis=0).astype(bf16), chooser, dims)
    return (o[0:8] + o[8:16]) + o[16:24]


def pick_rows(chooser, values, dims=NN):
    hi, mid, lo = three(values)
    o = dot(chooser, jnp.concatenate([hi, mid, lo], axis=1).astype(bf16), dims)
    return (o[:, :C] + o[:, C : 2 * C]) + o[:, 2 * C :]


def silu(x):
    return x * (1.0 / (1.0 + jnp.exp(-x)))


def silu_pair(x):
    s = 1.0 / (1.0 + jnp.exp(-x))
    return x * s, s * (1.0 + x * (1.0 - s))


def span(b):
    return pl.ds(b * SPAN, SPAN)


def fetched(kernel, count, carried):
    def run(*refs):
        given, rest = refs[: count + carried], refs[count + carried :]
        sems, held = rest[-1], rest[-1 - count : -1]
        targets = held + rest[:carried]
        copies = [pltpu.make_async_copy(src, dst, sems.at[k]) for k, (src, dst) in enumerate(zip(given, targets))]
        for copy in copies:
            copy.start()
        for copy in copies[:count]:
            copy.wait()
        kernel(*held, *rest[carried : -1 - count])
        for copy in copies[count:]:
            copy.wait()

    return run


def call(kernel, outs, args, scratch=(), flops=0, name=None, limit=8, carried=None):
    spec = pl.BlockSpec(memory_space=pltpu.VMEM)
    scratch = list(scratch)
    if carried is not None:
        scratch += [pltpu.VMEM(a.shape, a.dtype) for a in args]
        scratch.append(pltpu.SemaphoreType.DMA((len(args) + len(carried),)))
        kernel = fetched(kernel, len(args), len(carried))
        outs = [(a.shape, a.dtype) for a in carried] + list(outs)
        args = [pltpu.with_memory_space_constraint(a, pltpu.HBM) for a in [*args, *carried]]
        in_specs = [pl.BlockSpec(memory_space=pltpu.HBM)] * len(args)
    else:
        args = [pltpu.with_memory_space_constraint(a, pltpu.VMEM) for a in args]
        in_specs = [spec] * len(args)
    out_shape = tuple(pltpu.VMEM(shape, dtype) for shape, dtype in outs)
    moved = sum(a.size * a.dtype.itemsize for a in args)
    return pl.pallas_call(
        kernel,
        out_shape=out_shape,
        in_specs=in_specs,
        out_specs=tuple(spec for _ in out_shape),
        scratch_shapes=scratch,
        compiler_params=pltpu.CompilerParams(vmem_limit_bytes=limit * 1024 * 1024),
        cost_estimate=pl.CostEstimate(flops=flops, bytes_accessed=moved, transcendentals=0),
        name=name,
    )(*args)


def odd(axis):
    return lax.rem(lax.axis_index(axis), 2)


def partner_of(ref):
    return jnp.where(jnp.full(ref.shape[1:], odd("plane")) == 1, ref[0], ref[1])


def by_parity(flag, rows):
    swap = jnp.full(rows[0:1].shape, flag) == 1
    return jnp.where(swap, rows[0:1], rows[1:2]), jnp.where(swap, rows[1:2], rows[0:1])


def moved_slab(slot):
    swap = (jnp.full(slot.shape, odd("slab")) == 1) & (slot >= 64) & (slot < 128)
    return jnp.where(swap, slot ^ 32, slot)


def chooser(slots, picked):
    rows = lax.broadcasted_iota(jnp.int32, (slots, picked.shape[1]), 0)
    return (rows == picked).astype(f32).astype(bf16)


def shifted(values, row, step):
    rows = lax.broadcasted_iota(jnp.int32, values.shape, 0)
    return values + jnp.where(rows == row, step, 0.0)


def atoms_slab_kernel(
    pos_ref, kind_ref, list_ref, plane_ref, v_ref, tf_ref, tn_ref, pf_ref, pn_ref, far_ref, near_ref
):
    for k in range(3):
        v_ref[k : k + 1, :] = pos_ref[0, k]
    v_ref[3:4, :] = kind_ref[...].astype(f32)
    v_ref[4:8, :] = jnp.zeros((4, OWN), f32)
    far, near = by_parity(odd("slab"), list_ref[...])
    far, near = chooser(OWN, far), chooser(OWN, near)
    tf_ref[...] = far
    tn_ref[...] = near
    v = v_ref[...]
    far_ref[...] = pick_lanes(v, far)
    near_ref[...] = pick_lanes(v, near)
    for picked, t_ref in zip(by_parity(odd("plane"), plane_ref[...]), (pf_ref, pn_ref)):
        t_ref[...] = chooser(128, moved_slab(picked))


def atoms_plane_kernel(v_ref, far_ref, near_ref, tf_ref, tn_ref, pf_ref, pn_ref, sf_ref, sn_ref):
    step = (2 * odd("slab") - 1).astype(f32) * (CELLS_Z * cell_side)
    far = shifted(far_ref[...], 2, step)
    near = shifted(near_ref[...], 2, -step)
    pf_ref[...] = far
    pn_ref[...] = near
    own = v_ref[...]
    for t_ref, s_ref in ((tf_ref, sf_ref), (tn_ref, sn_ref)):
        s_ref[...] = pick_lanes(own, t_ref[0:64, :]) + (
            pick_lanes(far, t_ref[64:96, :]) + pick_lanes(near, t_ref[96:128, :])
        )


def prepare_kernel(
    edge_ref, one_ref, two_ref, three_ref, four_ref, embed_ref, up_ref, skip_ref, atom_ref, hid_ref, ro_ref,
    out_ref, gain_ref, read_ref,
    g_ref, gt_ref, dd_ref, mask_ref, w1_ref, w2_ref, w3_ref, w4_ref, table_ref, skips_ref, skipups_ref, refs_ref,
    from_first_ref, from_mix_ref, from_first_ro_ref, from_mix_ro_ref, outup_ref, out0_ref, gains_ref, reads_ref, ros_ref,
):
    per_atom = jnp.sum((edge_ref[1:2, :] == OWN - 1).astype(f32)).astype(jnp.int32)
    senders = jnp.broadcast_to(edge_ref[0:1, :], (8, EDGES))
    swap_plane = jnp.full((1, SPAN), odd("plane")) == 1
    place = lax.broadcasted_iota(jnp.int32, (GROUP, SPAN), 1)
    first_place = lax.broadcasted_iota(jnp.int32, (GROUP, SPAN), 0) * per_atom
    mask = ((place >= first_place) & (place < first_place + per_atom)).astype(f32)
    lanes = lax.broadcasted_iota(jnp.int32, (128, 128), 1).astype(f32)
    for b in range(BLOCKS):
        start = b * GROUP * per_atom
        rows = senders if b == 0 else pltpu.roll(senders, lax.rem(EDGES - start, EDGES), 1)
        row = rows[0:1, :SPAN]
        row = moved_slab(row)
        row = jnp.where(swap_plane & (row >= 128), row ^ 64, row)
        row = jnp.where(place[0:1] < GROUP * per_atom, row, -1)
        t = (lax.broadcasted_iota(jnp.int32, (EXT, SPAN), 0) == row).astype(f32)
        gt_ref[:, span(b)] = t.astype(bf16)
        dd_ref[:, span(b)] = t.astype(bf16)
        mine = pl.ds(b * GROUP, GROUP)
        dd_ref[mine, span(b)] = (t[b * GROUP : (b + 1) * GROUP] - mask).astype(bf16)
        mask_ref[:, span(b)] = mask
        for chunk in range(SPAN // 128):
            part = row[:, chunk * 128 : (chunk + 1) * 128].astype(f32)
            column = jnp.transpose(jnp.broadcast_to(part, (128, 128)))
            here = pl.ds(b * SPAN + chunk * 128, 128)
            g_ref[here, 0:128] = (column == lanes).astype(f32).astype(bf16)
            g_ref[here, 128:256] = (column == lanes + 128.0).astype(f32).astype(bf16)
    for t in range(2):
        hi, mid, lo = three(one_ref[t])
        stacked = jnp.concatenate([hi, hi, mid + lo, jnp.zeros_like(hi)], axis=0)
        w1_ref[t] = jnp.transpose(stacked).astype(bf16)
        for ref, to_ref in ((two_ref, w2_ref), (three_ref, w3_ref)):
            hi, mid, lo = three(ref[t])
            to_ref[t] = jnp.transpose(jnp.concatenate([hi, hi, mid + lo], axis=0)).astype(bf16)
        hi, lo = split(four_ref[t])
        w4_ref[t] = jnp.concatenate([hi, hi, lo], axis=0)
    embed = embed_ref[...]
    kinds = embed.shape[0]
    for ref in (table_ref, skips_ref, skipups_ref):
        ref[...] = jnp.zeros(ref.shape, bf16)
    table_ref[0:kinds, :] = pair_lanes(exact(embed, up_ref[0]))
    skipped = exact(embed, skip_ref[0])
    for ref, values in ((skips_ref, skipped), (skipups_ref, exact(skipped, up_ref[1]))):
        hi, mid, lo = three(values)
        ref[0:kinds, :] = jnp.concatenate([hi, mid, lo], axis=1).astype(bf16)
    refs_ref[...] = jnp.zeros(refs_ref.shape, f32)
    refs_ref[0:1, 0:kinds] = atom_ref[...]
    last = jnp.transpose(jnp.broadcast_to(ro_ref[...], (C, ro_ref.shape[1])))
    from_first = exact(hid_ref[...], skip_ref[1], NT)
    from_mix = exact(hid_ref[...], out_ref[1], NT)
    from_first_ref[...] = from_first
    from_mix_ref[...] = from_mix
    from_first_ro_ref[...] = from_first * last
    from_mix_ro_ref[...] = from_mix * last
    outup_ref[...] = exact(out_ref[0], up_ref[1])
    out0_ref[...] = out_ref[0]
    gains_ref[...] = gain_ref[...]
    reads_ref[...] = read_ref[...]
    ros_ref[...] = jnp.broadcast_to(ro_ref[...], ros_ref.shape)


def kinds_of(row):
    kinds = lax.broadcasted_iota(jnp.int32, (KINDS, row.shape[1]), 0).astype(f32) == row
    return kinds.astype(f32)


def near_atoms_kernel(v_ref, pf_ref, pn_ref, dd_ref, table_ref, vector_ref, lifted_ref):
    vector, at = None, 0
    for ref in (v_ref, pf_ref, pn_ref):
        rows = ref.shape[1]
        piece = pick_lanes(ref[...], dd_ref[at : at + rows, :])
        vector = piece if vector is None else vector + piece
        lifted_ref[at : at + rows, :] = dot(kinds_of(ref[3:4, :]).astype(bf16), table_ref[...], TN).astype(bf16)
        at += rows
    vector_ref[...] = vector


def geometry(v, valid, b_ref, db_ref, geo_ref):
    vx = jnp.where(valid, v[0:1], 2.0 * cutoff_radius)
    vy = jnp.where(valid, v[1:2], 0.0)
    vz = jnp.where(valid, v[2:3], 0.0)
    d = jnp.sqrt(vx * vx + vy * vy + vz * vz)
    inv = 1.0 / d
    geo_ref[0:1, :] = vx * inv
    geo_ref[1:2, :] = vy * inv
    geo_ref[2:3, :] = vz * inv
    geo_ref[3:4, :] = inv
    s = d / cutoff_radius
    s2 = s * s
    s4 = s2 * s2
    s5 = s4 * s
    s6 = s4 * s2
    s7 = s6 * s
    inside = (s < 1.0) & valid
    u = 1.0 - 28.0 * s6 + 48.0 * s7 - 21.0 * s4 * s4
    du = (-168.0 * s5 + 336.0 * s6 - 168.0 * s7) / cutoff_radius
    geo_ref[4:5, :] = jnp.where(inside, u * inverse_neighbours, 0.0)
    geo_ref[5:6, :] = jnp.where(inside, du * inverse_neighbours, 0.0)
    geo_ref[6:8, :] = jnp.zeros_like(geo_ref[6:8, :])
    t = (jnp.minimum(s, 1.0) - 0.5) * jnp.pi
    z = t * t
    cs = 1.0 - z * (1 / 2 - z * (1 / 24 - z * (1 / 720 - z * (1 / 40320 - z * (1 / 3628800 - z * (1 / 479001600 - z * (1 / 87178291200)))))))
    sn = 1.0 - z * (1 / 6 - z * (1 / 120 - z * (1 / 5040 - z * (1 / 362880 - z * (1 / 39916800 - z * (1 / 6227020800))))))
    s1, c1 = cs, -t * sn

    def plus(a, b):
        return a[0] * b[1] + a[1] * b[0], a[1] * b[1] - a[0] * b[0]

    w1 = (s1, c1)
    w2 = plus(w1, w1)
    w3 = plus(w2, w1)
    w4 = plus(w2, w2)
    waves = (w1, w2, w3, w4, plus(w4, w1), plus(w4, w2), plus(w4, w3), plus(w4, w4))
    gain = (2.0 / cutoff_radius) ** 0.5 * inv
    for n, (sine, cosine) in enumerate(waves):
        b_ref[n : n + 1, :] = gain * sine
        db_ref[n : n + 1, :] = gain * (cosine * ((n + 1) * jnp.pi / cutoff_radius) - sine * inv)


def basis_stack(x):
    hi, mid, _ = three(x)
    lo = x - hi
    return jnp.concatenate([hi, lo, hi, jnp.zeros_like(hi)], axis=0).astype(bf16)


def radial_hidden(b, w1, w2, w3):
    h = silu(dot(w1, basis_stack(b)))
    h = silu(dot(w2, stack_rows(h)))
    return silu(dot(w3, stack_rows(h)))


def radial_hidden_pair(b, db, w1, w2, w3):
    h, g = silu_pair(dot(w1, basis_stack(b)))
    t = g * dot(w1, basis_stack(db))
    h, g = silu_pair(dot(w2, stack_rows(h)))
    t = g * dot(w2, stack_rows(t))
    h, g = silu_pair(dot(w3, stack_rows(h)))
    t = g * dot(w3, stack_rows(t))
    return h, t


def angular_rows(geo):
    x, y, z = geo[0:1], geo[1:2], geo[2:3]
    return (
        jnp.ones_like(x),
        R3 * x,
        R3 * y,
        R3 * z,
        R15 * x * y,
        R15 * y * z,
        0.5 * R5 * (3.0 * z * z - 1.0),
        R15 * x * z,
        0.5 * R15 * (x * x - y * y),
    )


def messages(g_ref, lifted, radial_of, l_ref, m_ref):
    for b in range(BLOCKS):
        lift = halves(dot(g_ref[span(b), :], lifted))
        l_ref[span(b), :] = lift
        radial = radial_of(b)
        for l in range(3):
            m_ref[l, span(b), :] = pair_lanes(radial[:, l * C : (l + 1) * C] * lift)


def amplitudes(ast_ref, m_ref, amp_ref):
    for b in range(BLOCKS):
        for l in range(3):
            n = LMS[l]
            o = dot(ast_ref[pl.ds(b * STACK + STACK_AT[l], 32 * n), :], m_ref[l, span(b), :])
            amp = halves(o[: 16 * n]) + o[16 * n :, :C]
            for k in range(n):
                amp_ref[FIRST_LM[l] + k, pl.ds(b * GROUP, GROUP), :] = amp[16 * k : 16 * (k + 1)]


def invariants(amp_ref, gain):
    b0 = amp_ref[0]
    b1 = sum(amp_ref[k] * amp_ref[k] for k in range(1, 4))
    b2 = sum(amp_ref[k] * amp_ref[k] for k in range(4, 9))
    return gain[0:1] * b0 + gain[1:2] * b1 + gain[2:3] * b2 + gain[3:4] * b0 * b0


def amp_grads(amp_ref, gain, gm, ga_ref):
    ga_ref[0] = gm * (gain[0:1] + 2.0 * gain[3:4] * amp_ref[0])
    one = gm * (2.0 * gain[1:2])
    two = gm * (2.0 * gain[2:3])
    for k in range(1, 4):
        ga_ref[k] = one * amp_ref[k]
    for k in range(4, 9):
        ga_ref[k] = two * amp_ref[k]


def group_grads(ga_ref, b, l):
    return jnp.concatenate(
        [ga_ref[FIRST_LM[l] + k, pl.ds(b * GROUP, GROUP), :] for k in range(LMS[l])], axis=0
    )


def spread(turned_ref, ga_ref, b, l):
    hi, lo = split(group_grads(ga_ref, b, l))
    angular = turned_ref[span(b), TURNED_AT[l] : TURNED_AT[l] + 48 * LMS[l]]
    return dot(angular, jnp.concatenate([hi, hi, lo], axis=0))


def angular_grads(m_ref, ga_ref, mask_ref, gy_ref):
    for b in range(BLOCKS):
        mask = mask_ref[:, span(b)]
        for l in (1, 2):
            n = LMS[l]
            hi, lo = split(group_grads(ga_ref, b, l))
            left = jnp.concatenate(
                [jnp.concatenate([hi, hi], axis=1), jnp.concatenate([lo, jnp.zeros_like(lo)], axis=1)],
                axis=0,
            )
            w = dot(left, m_ref[l, span(b), :], NT)
            w = w[: 16 * n] + w[16 * n :]
            for k in range(n):
                row = FIRST_LM[l] + k - 1
                gy_ref[row : row + 1, span(b)] = jnp.sum(mask * w[16 * k : 16 * (k + 1)], axis=0, keepdims=True)


def edge_forces(x_ref, gy_ref, geo_ref, gv_ref):
    gd = dot(jnp.ones((16, 2 * C), bf16), x_ref[...], NT)[0:1]
    gy = [None] + [gy_ref[k : k + 1, :] for k in range(8)]
    x, y, z, inv = (geo_ref[k : k + 1, :] for k in range(4))
    gx = R3 * gy[1] + R15 * (y * gy[4] + z * gy[7] + x * gy[8])
    gyy = R3 * gy[2] + R15 * (x * gy[4] + z * gy[5] - y * gy[8])
    gz = R3 * gy[3] + R15 * (y * gy[5] + x * gy[7]) + (3.0 * R5) * z * gy[6]
    along = x * gx + y * gyy + z * gz
    core = gd - along * inv
    gv_ref[0:1, :] = core * x + gx * inv
    gv_ref[1:2, :] = core * y + gyy * inv
    gv_ref[2:3, :] = core * z + gz * inv
    gv_ref[3:8, :] = jnp.zeros((5, EDGES), f32)


def first_kernel(
    v_ref, vector_ref, lifted_ref, qf_ref, qn_ref, dd_ref, g_ref, mask_ref, table_ref, skip_ref, w1_ref, w2_ref, w3_ref, w4_ref,
    gain_ref, outup_ref, tf_ref, tn_ref,
    f_ref, sf_ref, sn_ref, mix_ref, amp_ref, l_ref, m_ref, ast_ref, b_ref, db_ref, geo_ref,
):
    step = (2 * odd("plane") - 1).astype(f32) * (CELLS_Y * cell_side)
    far, near = shifted(qf_ref[...], 1, step), shifted(partner_of(qn_ref), 1, -step)
    valid = jnp.sum(mask_ref[...], axis=0, keepdims=True) > 0.5
    vector = vector_ref[...] + (pick_lanes(far, dd_ref[128:192, :]) + pick_lanes(near, dd_ref[192:256, :]))
    lifted = [dot(kinds_of(part[3:4]).astype(bf16), table_ref[...], TN).astype(bf16) for part in (far, near)]
    lifted = jnp.concatenate([lifted_ref[...]] + lifted, axis=0)
    o = dot(kinds_of(v_ref[3:4, :]).astype(bf16), skip_ref[...], TN)
    skipped = (o[:, :C] + o[:, C : 2 * C]) + o[:, 2 * C :]
    geometry(vector, valid, b_ref, db_ref, geo_ref)
    h = stack_rows(radial_hidden(b_ref[...], w1_ref[0], w2_ref[0], w3_ref[0]) * geo_ref[4:5, :])
    rows = angular_rows(geo_ref[0:3, :])
    for b in range(BLOCKS):
        mask = mask_ref[:, span(b)]
        for l in range(3):
            a = jnp.concatenate(
                [mask * rows[FIRST_LM[l] + k][:, b * SPAN : (b + 1) * SPAN] for k in range(LMS[l])], axis=0
            )
            ast_ref[pl.ds(b * STACK + STACK_AT[l], 48 * LMS[l]), :] = stack_rows(a)
    messages(g_ref, lifted, lambda b: dot(h[:, b * SPAN : (b + 1) * SPAN], w4_ref[0], TN), l_ref, m_ref)
    amplitudes(ast_ref, m_ref, amp_ref)
    mix = invariants(amp_ref, gain_ref[0])
    mix_ref[...] = mix
    lifted = skipped + dot3(mix, outup_ref[...])
    f_ref[...] = lifted
    sf_ref[...] = pick_rows(tf_ref[...], lifted, TN)
    sn_ref[...] = pick_rows(tn_ref[...], lifted, TN)


def own_terms_kernel(v_ref, mix_ref, skip_ref, out0_ref, ref_ref, one_ref, from_first_ref, hid_ref, e_ref):
    kinds = kinds_of(v_ref[3:4, :])
    o = dot(kinds.astype(bf16), skip_ref[...], TN)
    first = ((o[:, :C] + o[:, C : 2 * C]) + o[:, 2 * C :]) + exact(mix_ref[...], out0_ref[...])
    hid_ref[...] = exact(from_first_ref[...], first, NT)
    e_ref[...] = exact(ref_ref[...], kinds) + exact(jnp.broadcast_to(one_ref[...], (8, C)), first, NT)


def middle_kernel(f_ref, rf_ref, rn_ref, pf_ref, pn_ref, a_ref, b_ref):
    rows = jnp.concatenate([f_ref[...], rf_ref[...], rn_ref[...]], axis=0)
    a_ref[...] = pick_rows(pf_ref[...], rows, TN)
    b_ref[...] = pick_rows(pn_ref[...], rows, TN)


def slope_kernel(b_ref, db_ref, geo_ref, w1_ref, w2_ref, w3_ref, q_ref, *, layer):
    h, t = radial_hidden_pair(b_ref[...], db_ref[...], w1_ref[layer], w2_ref[layer], w3_ref[layer])
    q_ref[...] = stack_rows(t * geo_ref[4:5, :] + h * geo_ref[5:6, :])


def radial_kernel(b_ref, db_ref, geo_ref, w1_ref, w2_ref, w3_ref, w4_ref, r_ref, q_ref, *, layer):
    h, t = radial_hidden_pair(b_ref[...], db_ref[...], w1_ref[layer], w2_ref[layer], w3_ref[layer])
    q_ref[...] = stack_rows(t * geo_ref[4:5, :] + h * geo_ref[5:6, :])
    h = stack_rows(h * geo_ref[4:5, :])
    for b in range(BLOCKS):
        r_ref[span(b), :] = dot(h[:, b * SPAN : (b + 1) * SPAN], w4_ref[layer], TN)


def expand_kernel(q_ref, w4_ref, r_ref, *, layer):
    for b in range(BLOCKS):
        r_ref[span(b), :] = dot(q_ref[:, span(b)], w4_ref[layer], TN)


def beside_features_kernel(
    b_ref, db_ref, geo_ref, w1_ref, w2_ref, w3_ref, w4_ref, v_ref, mix_ref, skip_ref, out0_ref, ref_ref, one_ref, from_first_ref,
    ast_ref, r_ref, second_q_ref, first_q_ref, hid_ref, e_ref, turned_ref,
):
    for b in range(BLOCKS):
        for l in range(3):
            rows = ast_ref[pl.ds(b * STACK + STACK_AT[l], 48 * LMS[l]), :]
            turned_ref[span(b), TURNED_AT[l] : TURNED_AT[l] + 48 * LMS[l]] = jnp.transpose(rows)
    slope_kernel(b_ref, db_ref, geo_ref, w1_ref, w2_ref, w3_ref, first_q_ref, layer=0)
    radial_kernel(b_ref, db_ref, geo_ref, w1_ref, w2_ref, w3_ref, w4_ref, r_ref, second_q_ref, layer=1)
    own_terms_kernel(v_ref, mix_ref, skip_ref, out0_ref, ref_ref, one_ref, from_first_ref, hid_ref, e_ref)


def second_kernel(
    f_ref, rf_ref, rn_ref, pf_ref, pn_ref, g_ref, gt_ref, ast_ref, turned_ref, r_ref, gain_ref, hid_ref, from_mix_ref, from_mix_ro_ref,
    act_ref, slope_ref, gmid_ref, gf_ref, gn_ref, l_ref, m_ref, ga_ref,
    amp_ref, glift_ref,
):
    lifted = pair_lanes(
        jnp.concatenate([f_ref[...], rf_ref[...], rn_ref[...], pf_ref[...], partner_of(pn_ref)], axis=0)
    )
    messages(g_ref, lifted, lambda b: r_ref[span(b), :], l_ref, m_ref)
    amplitudes(ast_ref, m_ref, amp_ref)
    gain = gain_ref[1]
    act, slope = silu_pair(hid_ref[...] + exact(from_mix_ref[...], invariants(amp_ref, gain), NT))
    act_ref[...] = act
    slope_ref[...] = slope
    amp_grads(amp_ref, gain, dot3(slope, from_mix_ro_ref[...], TN), ga_ref)
    for b in range(BLOCKS):
        grad = None
        for l in range(3):
            term = r_ref[span(b), l * C : (l + 1) * C] * spread(turned_ref, ga_ref, b, l)
            grad = term if grad is None else grad + term
        glift_ref[span(b), :] = pair_lanes(grad)
    glift = halves(dot(gt_ref[...], glift_ref[...]))
    gmid_ref[...] = glift[0:128]
    gf_ref[...] = glift[128:192]
    gn_ref[...] = glift[192:256]


def own_grads_kernel(act_ref, slope_ref, e0_ref, ro_ref, from_first_ro_ref, one_ref, out0_ref, e_ref, gm_ref):
    e_ref[...] = (e0_ref[...] + exact(ro_ref[...], act_ref[...]))[0:1]
    grad = dot3(slope_ref[...], from_first_ro_ref[...], TN) + one_ref[...]
    gm_ref[...] = dot3(grad, out0_ref[...], NT)


def early_kernel(turned_ref, q_ref, w4_ref, l_ref, m_ref, ga_ref, geo_ref, mask_ref, gv_ref, x_ref, gy_ref):
    for b in range(BLOCKS):
        slope = dot(q_ref[:, span(b)], w4_ref[1], TN)
        x = sum(spread(turned_ref, ga_ref, b, l) * slope[:, l * C : (l + 1) * C] for l in range(3))
        x_ref[span(b), :] = pair_lanes(x * l_ref[span(b), :])
    angular_grads(m_ref, ga_ref, mask_ref, gy_ref)
    edge_forces(x_ref, gy_ref, geo_ref, gv_ref)


def beside_grads_kernel(
    turned_ref, second_q_ref, w4_ref, l_ref, m_ref, ga_ref, geo_ref, mask_ref, first_q_ref,
    act_ref, slope_ref, e0_ref, ro_ref, from_first_ro_ref, one_ref, out0_ref,
    gv_ref, dr_ref, e_ref, gm_ref, x_ref, gy_ref,
):
    early_kernel(turned_ref, second_q_ref, w4_ref, l_ref, m_ref, ga_ref, geo_ref, mask_ref, gv_ref, x_ref, gy_ref)
    expand_kernel(first_q_ref, w4_ref, dr_ref, layer=0)
    own_grads_kernel(act_ref, slope_ref, e0_ref, ro_ref, from_first_ro_ref, one_ref, out0_ref, e_ref, gm_ref)


def back_middle_kernel(gmid_ref, rf_ref, rn_ref, pf_ref, pn_ref, own_ref, f_ref, n_ref):
    mid = gmid_ref[...] + (pick_rows(pf_ref[...], rf_ref[...]) + pick_rows(pn_ref[...], partner_of(rn_ref)))
    own_ref[...] = mid[:64]
    f_ref[...] = mid[64:96]
    n_ref[...] = mid[96:128]


def late_kernel(
    own_ref, rf_ref, rn_ref, tf_ref, tn_ref, gm_ref, outup_ref, gain_ref, amp_ref, turned_ref, dr_ref, l_ref, m_ref, geo_ref,
    mask_ref, dd_ref, early_ref, of_ref, pf_ref, pn_ref, qf_ref, qn_ref, ga_ref, gv_ref, x_ref, gy_ref,
):
    grad = own_ref[...] + (pick_rows(tf_ref[...], rf_ref[...]) + pick_rows(tn_ref[...], rn_ref[...]))
    amp_grads(amp_ref, gain_ref[0], gm_ref[...] + dot3(grad, outup_ref[...], NT), ga_ref)
    for b in range(BLOCKS):
        x = None
        for l in range(3):
            term = spread(turned_ref, ga_ref, b, l) * dr_ref[span(b), l * C : (l + 1) * C]
            x = term if x is None else x + term
        x_ref[span(b), :] = pair_lanes(x * l_ref[span(b), :])
    angular_grads(m_ref, ga_ref, mask_ref, gy_ref)
    edge_forces(x_ref, gy_ref, geo_ref, gv_ref)
    total = gv_ref[...] + early_ref[...]
    at = 0
    for ref in (of_ref, pf_ref, pn_ref, qf_ref, qn_ref):
        rows = ref.shape[1]
        ref[...] = pick_lanes(total, dd_ref[at : at + rows, :], NT)
        at += rows


def collect_plane_kernel(of_ref, pf_ref, pn_ref, rf_ref, rn_ref, tf_ref, tn_ref, o_ref, f_ref, n_ref):
    far, near, at = rf_ref[...], partner_of(rn_ref), 0
    for have_ref, ref in ((of_ref, o_ref), (pf_ref, f_ref), (pn_ref, n_ref)):
        rows = ref.shape[1]
        back = pick_lanes(far, tf_ref[at : at + rows, :], NT) + pick_lanes(near, tn_ref[at : at + rows, :], NT)
        ref[...] = have_ref[...] + back
        at += rows


def collect_slab_kernel(v_ref, rf_ref, rn_ref, tf_ref, tn_ref, o_ref):
    back = pick_lanes(rf_ref[...], tf_ref[...], NT) + pick_lanes(rn_ref[...], tn_ref[...], NT)
    forces = -(v_ref[...] + back)
    for k in range(3):
        o_ref[0, k] = forces[k : k + 1]


def swap_slab_far(value):
    count = lax.axis_size("slab")
    pairs = [(i, i + 1) for i in range(1, count - 1, 2)]
    return lax.ppermute(value, "slab", pairs + [(b, a) for a, b in pairs])


def swap_slab_near(value):
    count = lax.axis_size("slab")
    return lax.ppermute(value, "slab", [(i, i ^ 1) for i in range(count)])


def swap_plane_far(value):
    count = lax.axis_size("plane")
    pairs = [(i, (i + 1) % count) for i in range(1, count, 2)]
    return lax.ppermute(value, "plane", pairs + [(b, a) for a, b in pairs])


def swap_plane_near(value):
    count = lax.axis_size("plane")
    return lax.all_gather(value, "plane", axis_index_groups=[[i, i + 1] for i in range(0, count, 2)])


def both(swap_far, swap_near, far, near):
    return swap_far(far), swap_near(near)


def body(
    positions,
    species,
    slab_sends,
    plane_sends,
    edges,
    edge_count,
    embed_table,
    atom_ref,
    radial_one,
    radial_two,
    radial_three,
    radial_four,
    up_weight,
    skip_weight,
    out_weight,
    prod_weight,
    read_one,
    read_hidden,
    read_out,
):
    edge_mat = ((EDGES, C), f32)
    message_mat = ((3, EDGES, 2 * C), bf16)
    by_degree = ((EDGES, 3 * C), f32)
    edge_rows = ((8, EDGES), f32)
    amp_mat = ((9, OWN, C), f32)
    slab_rows = ((32, C), f32)
    plane_rows = ((64, C), f32)
    own_lanes = ((8, OWN), f32)
    slab_lanes = ((8, 32), f32)
    plane_lanes = ((8, 64), f32)

    with jax.named_scope("atoms_slab"):
        *arguments, values, slab_t_far, slab_t_near, plane_t_far, plane_t_near, far, near = call(
            atoms_slab_kernel,
            [own_lanes, ((OWN, 32), bf16), ((OWN, 32), bf16), ((128, 64), bf16), ((128, 64), bf16), slab_lanes, slab_lanes],
            (jnp.transpose(positions, (0, 2, 1, 3)), species[0], slab_sends[0, 0], plane_sends[0, 0]),
            carried=(
                edges[0, 0], radial_one, radial_two, radial_three, radial_four, embed_table, up_weight, skip_weight,
                atom_ref[None, :], jnp.transpose(read_hidden), read_out[None, :], out_weight, prod_weight, read_one[None, :],
            ),
            name="atoms_slab",
        )
        far, near = both(swap_slab_far, swap_slab_near, far, near)
    with jax.named_scope("prepare"):
        sender_n, sender_t, edge_t, mask, *prepared = call(
            prepare_kernel,
            [((EDGES, EXT), bf16), ((EXT, EDGES), bf16), ((EXT, EDGES), bf16), ((GROUP, EDGES), f32),
             ((2, 64, 32), bf16), ((2, 64, 192), bf16), ((2, 64, 192), bf16), ((2, 192, 3 * C), bf16),
             ((KINDS, 2 * C), bf16), ((KINDS, 3 * C), bf16), ((KINDS, 3 * C), bf16), ((8, KINDS), f32),
             *[((16, C), f32)] * 4, ((C, C), f32), ((C, C), f32), ((2, 4, C), f32), ((1, C), f32), ((8, 16), f32)],
            arguments,
            flops=1_000_000_000,
            name="prepare",
        )
        weights = tuple(prepared[:4])
        (table, skip_table, skip_up_table, ref_row, from_first, from_mix, from_first_ro, from_mix_ro, out_up, out_first,
         gains, read_row, read_last) = prepared[4:]
    with jax.named_scope("atoms_plane"):
        far, near, edge_t = lax.optimization_barrier((far, near, edge_t))
        slab_far, slab_near, far, near = call(
            atoms_plane_kernel,
            [slab_lanes, slab_lanes, plane_lanes, plane_lanes],
            (values, far, near, plane_t_far, plane_t_near),
            name="atoms_plane",
        )
        far, near = both(swap_plane_far, swap_plane_near, far, near)
        vector, lifted = call(
            near_atoms_kernel, [edge_rows, ((128, 2 * C), bf16)], (values, slab_far, slab_near, edge_t, table),
            flops=1_000_000_000, name="near_atoms",
        )

    hidden_mat = ((16, OWN), f32)
    with jax.named_scope("first_layer"):
        far, near, vector, lifted = lax.optimization_barrier((far, near, vector, lifted))
        (first, s_far, s_near, mix, amp_first, lift_first, message_first, angular, basis, basis_slope, geo) = call(
            first_kernel,
            [plane_rows, slab_rows, slab_rows, plane_rows, amp_mat, edge_mat, message_mat,
             ((BLOCKS * STACK, SPAN), bf16), edge_rows, edge_rows, edge_rows],
            (values, vector, lifted, far, near, edge_t, sender_n, mask, table, skip_up_table, *weights,
             gains, out_up, slab_t_far, slab_t_near),
            name="first_layer",
        )
    with jax.named_scope("features_slab"):
        slab_far, slab_near = both(swap_slab_far, swap_slab_near, s_far, s_near)
    radial_second, slope_second, slope_first, hidden, energies, turned = call(
        beside_features_kernel,
        [by_degree, ((192, EDGES), bf16), ((192, EDGES), bf16), hidden_mat, own_lanes, ((EDGES, TURNED), bf16)],
        (basis, basis_slope, geo, *weights, values, mix, skip_table, out_first, ref_row, read_row, from_first,
         angular),
        flops=1_000_000_000, name="beside_features",
    )
    with jax.named_scope("features_plane"):
        slab_far, slab_near, radial_second = lax.optimization_barrier((slab_far, slab_near, radial_second))
        far, near = call(
            middle_kernel, [plane_rows] * 2, (first, slab_far, slab_near, plane_t_far, plane_t_near), name="middle"
        )
        far, near = both(swap_plane_far, swap_plane_near, far, near)
    with jax.named_scope("second_layer"):
        act, slope, gmid, far, near, lift_second, message_second, ga = call(
            second_kernel,
            [hidden_mat, hidden_mat, ((128, C), f32), plane_rows, plane_rows, edge_mat, message_mat, amp_mat],
            (first, slab_far, slab_near, far, near, sender_n, sender_t, angular, turned, radial_second, gains, hidden, from_mix,
             from_mix_ro),
            scratch=[pltpu.VMEM((9, OWN, C), f32), pltpu.VMEM((EDGES, 2 * C), bf16)],
            name="second_layer",
        )
    with jax.named_scope("feature_grads_plane"):
        far, near = both(swap_plane_far, swap_plane_near, far, near)
    with jax.named_scope("feature_grads_slab"):
        own, far, near = call(
            back_middle_kernel, [plane_rows, slab_rows, slab_rows], (gmid, far, near, plane_t_far, plane_t_near),
            name="back_middle",
        )
        far, near, ga = lax.optimization_barrier((far, near, ga))
        far, near = both(swap_slab_far, swap_slab_near, far, near)
    early, slope_first, energies, own_grads = call(
        beside_grads_kernel,
        [edge_rows, by_degree, ((1, OWN), f32), plane_rows],
        (turned, slope_second, weights[3], lift_second, message_second, ga, geo, mask, slope_first,
         act, slope, energies, read_last, from_first_ro, read_row, out_first),
        scratch=[pltpu.VMEM((EDGES, 2 * C), bf16), pltpu.VMEM((8, EDGES), f32)],
        flops=1_000_000_000, name="beside_grads",
    )
    with jax.named_scope("late_forces"):
        own, slab_far, slab_near, far, near = call(
            late_kernel,
            [own_lanes, slab_lanes, slab_lanes, plane_lanes, plane_lanes],
            (own, far, near, slab_t_far, slab_t_near, own_grads, out_up, gains, amp_first, turned, slope_first,
             lift_first, message_first, geo, mask, edge_t, early),
            scratch=[pltpu.VMEM((9, OWN, C), f32), pltpu.VMEM((8, EDGES), f32), pltpu.VMEM((EDGES, 2 * C), bf16),
                     pltpu.VMEM((8, EDGES), f32)],
            name="late_forces",
        )
    with jax.named_scope("position_grads_plane"):
        far, near = both(swap_plane_far, swap_plane_near, far, near)
        own, far, near = call(
            collect_plane_kernel, [own_lanes, slab_lanes, slab_lanes],
            (own, slab_far, slab_near, far, near, plane_t_far, plane_t_near), name="collect_plane",
        )
    with jax.named_scope("position_grads_slab"):
        far, near = both(swap_slab_far, swap_slab_near, far, near)
        forces, = call(
            collect_slab_kernel, [((1, 3, 1, OWN), f32)], (own, far, near, slab_t_far, slab_t_near), name="collect_slab"
        )
    return (energies[None], jnp.transpose(forces, (0, 2, 1, 3)))


def solution(mesh):
    in_specs = (
        P("slab", "plane", None, None),
        P("slab", "plane", None),
        P("slab", "plane", None, None),
        P("slab", "plane", None, None),
        P("slab", "plane", None, None),
        P("slab", "plane"),
    ) + (P(),) * 13
    out_specs = (P("slab", "plane", None), P("slab", "plane", None, None))
    return jax.shard_map(body, mesh=mesh, in_specs=in_specs, out_specs=out_specs, check_vma=False)
```

```python
import functools

import jax
import jax.numpy as jnp
from jax import lax
from jax.experimental import pallas as pl
from jax.experimental.pallas import tpu as pltpu
from jax.sharding import PartitionSpec as P

CELLS_Y = 2
CELLS_Z = 2

cutoff_radius = 5.0
cell_side = 3.0
inverse_neighbours = 0.2
highest = lax.Precision.HIGHEST
f32 = jnp.float32
bf16 = jnp.bfloat16

C = 128
OWN = 64
EXT = 256
EDGES = 1536
BLOCKS = 4
GROUP = 16
SPAN = EDGES // BLOCKS
KINDS = 96
LMS = (1, 3, 5)
FIRST_LM = (0, 1, 4)
STACK_AT = (0, 48, 192)
STACK = 432
PAIR_ROWS = 192
TURNED_AT = 256
TURNED = 512
R3, R5, R15 = 3.0**0.5, 5.0**0.5, 15.0**0.5

NN = (((1,), (0,)), ((), ()))
TN = (((0,), (0,)), ((), ()))
NT = (((1,), (1,)), ((), ()))


def dot(a, b, dims=NN):
    return lax.dot_general(a, b, dims, preferred_element_type=f32)


def dot3(a, b, dims=NN):
    return lax.dot_general(a, b, dims, precision=lax.Precision.HIGH, preferred_element_type=f32)


def exact(a, b, dims=NN):
    return lax.dot_general(a, b, dims, precision=highest, preferred_element_type=f32)


def split(x):
    hi = x.astype(bf16)
    return hi, (x - hi.astype(f32)).astype(bf16)


def pair_lanes(x):
    hi, lo = split(x)
    return jnp.concatenate([hi, lo], axis=1)


def halves(o):
    return o[:, :C] + o[:, C:]


def stack_rows(x):
    hi, lo = split(x)
    return jnp.concatenate([hi, lo, hi], axis=0)


def three(x):
    hi = x.astype(bf16).astype(f32)
    rest = x - hi
    mid = rest.astype(bf16).astype(f32)
    return hi, mid, rest - mid


def pick_lanes(values, chooser, dims=NN):
    hi, mid, lo = three(values)
    o = dot(jnp.concatenate([hi, mid, lo, jnp.zeros_like(lo)], axis=0).astype(bf16), chooser, dims)
    return (o[0:8] + o[8:16]) + o[16:24]


def pick_rows(chooser, values, dims=NN):
    hi, mid, lo = three(values)
    o = dot(chooser, jnp.concatenate([hi, mid, lo], axis=1).astype(bf16), dims)
    return (o[:, :C] + o[:, C : 2 * C]) + o[:, 2 * C :]


def sigmoid(x):
    return 0.5 + 0.5 * jnp.tanh(0.5 * x)


def silu(x):
    return x * sigmoid(x)


def silu_pair(x):
    s = sigmoid(x)
    return x * s, s * (1.0 + x * (1.0 - s))


def span(b):
    return pl.ds(b * SPAN, SPAN)


def fetched(kernel, count, carried):
    def run(*refs):
        given, rest = refs[: count + carried], refs[count + carried :]
        sems, held = rest[-1], rest[-1 - count : -1]
        targets = held + rest[:carried]
        copies = [pltpu.make_async_copy(src, dst, sems.at[k]) for k, (src, dst) in enumerate(zip(given, targets))]
        for copy in copies:
            copy.start()
        for copy in copies[:count]:
            copy.wait()
        kernel(*held, *rest[carried : -1 - count])
        for copy in copies[count:]:
            copy.wait()

    return run


def call(kernel, outs, args, scratch=(), flops=0, name=None, limit=8, carried=None):
    spec = pl.BlockSpec(memory_space=pltpu.VMEM)
    scratch = list(scratch)
    if carried is not None:
        scratch += [pltpu.VMEM(a.shape, a.dtype) for a in args]
        scratch.append(pltpu.SemaphoreType.DMA((len(args) + len(carried),)))
        kernel = fetched(kernel, len(args), len(carried))
        outs = [(a.shape, a.dtype) for a in carried] + list(outs)
        args = [pltpu.with_memory_space_constraint(a, pltpu.HBM) for a in [*args, *carried]]
        in_specs = [pl.BlockSpec(memory_space=pltpu.HBM)] * len(args)
    else:
        args = [pltpu.with_memory_space_constraint(a, pltpu.VMEM) for a in args]
        in_specs = [spec] * len(args)
    out_shape = tuple(pltpu.VMEM(shape, dtype) for shape, dtype in outs)
    moved = sum(a.size * a.dtype.itemsize for a in args)
    return pl.pallas_call(
        kernel,
        out_shape=out_shape,
        in_specs=in_specs,
        out_specs=tuple(spec for _ in out_shape),
        scratch_shapes=scratch,
        compiler_params=pltpu.CompilerParams(vmem_limit_bytes=limit * 1024 * 1024),
        cost_estimate=pl.CostEstimate(flops=flops, bytes_accessed=moved, transcendentals=0),
        name=name,
    )(*args)


def odd(axis):
    return lax.rem(lax.axis_index(axis), 2)


def partner_of(ref):
    return jnp.where(jnp.full(ref.shape[1:], odd("plane")) == 1, ref[0], ref[1])


def by_parity(flag, rows):
    swap = jnp.full(rows[0:1].shape, flag) == 1
    return jnp.where(swap, rows[0:1], rows[1:2]), jnp.where(swap, rows[1:2], rows[0:1])


def moved_slab(slot):
    swap = (jnp.full(slot.shape, odd("slab")) == 1) & (slot >= 64) & (slot < 128)
    return jnp.where(swap, slot ^ 32, slot)


def chooser(slots, picked):
    rows = lax.broadcasted_iota(jnp.int32, (slots, picked.shape[1]), 0)
    return (rows == picked).astype(f32).astype(bf16)


def shifted(values, row, step):
    rows = lax.broadcasted_iota(jnp.int32, values.shape, 0)
    return values + jnp.where(rows == row, step, 0.0)


def atoms_slab_kernel(
    pos_ref, kind_ref, list_ref, plane_ref, v_ref, tf_ref, tn_ref, pf_ref, pn_ref, far_ref, near_ref
):
    for k in range(3):
        v_ref[k : k + 1, :] = pos_ref[0, k]
    v_ref[3:4, :] = kind_ref[...].astype(f32)
    v_ref[4:8, :] = jnp.zeros((4, OWN), f32)
    far, near = by_parity(odd("slab"), list_ref[...])
    far, near = chooser(OWN, far), chooser(OWN, near)
    tf_ref[...] = far
    tn_ref[...] = near
    v = v_ref[...]
    far_ref[...] = pick_lanes(v, far)
    near_ref[...] = pick_lanes(v, near)
    for picked, t_ref in zip(by_parity(odd("plane"), plane_ref[...]), (pf_ref, pn_ref)):
        t_ref[...] = chooser(128, moved_slab(picked))


def atoms_plane_kernel(v_ref, far_ref, near_ref, tf_ref, tn_ref, pf_ref, pn_ref, sf_ref, sn_ref):
    step = (2 * odd("slab") - 1).astype(f32) * (CELLS_Z * cell_side)
    far = shifted(far_ref[...], 2, step)
    near = shifted(near_ref[...], 2, -step)
    pf_ref[...] = far
    pn_ref[...] = near
    own = v_ref[...]
    for t_ref, s_ref in ((tf_ref, sf_ref), (tn_ref, sn_ref)):
        s_ref[...] = pick_lanes(own, t_ref[0:64, :]) + (
            pick_lanes(far, t_ref[64:96, :]) + pick_lanes(near, t_ref[96:128, :])
        )


def prepare_kernel(
    edge_ref, one_ref, two_ref, three_ref, four_ref, embed_ref, up_ref, skip_ref, atom_ref, hid_ref, ro_ref,
    out_ref, gain_ref, read_ref,
    g_ref, gt_ref, dd_ref, mask_ref, w1_ref, w2_ref, w3_ref, w4_ref, table_ref, skips_ref, skipups_ref, refs_ref,
    from_first_ref, from_mix_ref, from_first_ro_ref, from_mix_ro_ref, outup_ref, out0_ref, gains_ref, reads_ref, ros_ref,
):
    per_atom = jnp.sum((edge_ref[1:2, :] == OWN - 1).astype(f32)).astype(jnp.int32)
    senders = jnp.broadcast_to(edge_ref[0:1, :], (8, EDGES))
    swap_plane = jnp.full((1, SPAN), odd("plane")) == 1
    place = lax.broadcasted_iota(jnp.int32, (GROUP, SPAN), 1)
    first_place = lax.broadcasted_iota(jnp.int32, (GROUP, SPAN), 0) * per_atom
    mask = ((place >= first_place) & (place < first_place + per_atom)).astype(f32)
    lanes = lax.broadcasted_iota(jnp.int32, (128, 128), 1).astype(f32)
    for b in range(BLOCKS):
        start = b * GROUP * per_atom
        rows = senders if b == 0 else pltpu.roll(senders, lax.rem(EDGES - start, EDGES), 1)
        row = rows[0:1, :SPAN]
        row = moved_slab(row)
        row = jnp.where(swap_plane & (row >= 128), row ^ 64, row)
        row = jnp.where(place[0:1] < GROUP * per_atom, row, -1)
        t = (lax.broadcasted_iota(jnp.int32, (EXT, SPAN), 0) == row).astype(f32)
        gt_ref[:, span(b)] = t.astype(bf16)
        dd_ref[:, span(b)] = t.astype(bf16)
        mine = pl.ds(b * GROUP, GROUP)
        dd_ref[mine, span(b)] = (t[b * GROUP : (b + 1) * GROUP] - mask).astype(bf16)
        mask_ref[:, span(b)] = mask
        for chunk in range(SPAN // 128):
            part = row[:, chunk * 128 : (chunk + 1) * 128].astype(f32)
            column = jnp.transpose(jnp.broadcast_to(part, (128, 128)))
            here = pl.ds(b * SPAN + chunk * 128, 128)
            g_ref[here, 0:128] = (column == lanes).astype(f32).astype(bf16)
            g_ref[here, 128:256] = (column == lanes + 128.0).astype(f32).astype(bf16)
    for t in range(2):
        hi, mid, lo = three(one_ref[t])
        stacked = jnp.concatenate([hi, hi, mid + lo, jnp.zeros_like(hi)], axis=0)
        w1_ref[t] = jnp.transpose(stacked).astype(bf16)
        for ref, to_ref in ((two_ref, w2_ref), (three_ref, w3_ref)):
            hi, mid, lo = three(ref[t])
            to_ref[t] = jnp.transpose(jnp.concatenate([hi, hi, mid + lo], axis=0)).astype(bf16)
        hi, lo = split(four_ref[t])
        w4_ref[t] = jnp.concatenate([hi, hi, lo], axis=0)
    embed = embed_ref[...]
    kinds = embed.shape[0]
    for ref in (table_ref, skips_ref, skipups_ref):
        ref[...] = jnp.zeros(ref.shape, bf16)
    table_ref[0:kinds, :] = pair_lanes(exact(embed, up_ref[0]))
    skipped = exact(embed, skip_ref[0])
    for ref, values in ((skips_ref, skipped), (skipups_ref, exact(skipped, up_ref[1]))):
        hi, mid, lo = three(values)
        ref[0:kinds, :] = jnp.concatenate([hi, mid, lo], axis=1).astype(bf16)
    refs_ref[...] = jnp.zeros(refs_ref.shape, f32)
    refs_ref[0:1, 0:kinds] = atom_ref[...]
    last = jnp.transpose(jnp.broadcast_to(ro_ref[...], (C, ro_ref.shape[1])))
    from_first = exact(hid_ref[...], skip_ref[1], NT)
    from_mix = exact(hid_ref[...], out_ref[1], NT)
    from_first_ref[...] = from_first
    from_mix_ref[...] = from_mix
    from_first_ro_ref[...] = from_first * last
    from_mix_ro_ref[...] = from_mix * last
    outup_ref[...] = exact(out_ref[0], up_ref[1])
    out0_ref[...] = out_ref[0]
    gains_ref[...] = gain_ref[...]
    reads_ref[...] = read_ref[...]
    ros_ref[...] = jnp.broadcast_to(ro_ref[...], ros_ref.shape)


def kinds_of(row):
    kinds = lax.broadcasted_iota(jnp.int32, (KINDS, row.shape[1]), 0).astype(f32) == row
    return kinds.astype(f32)


def geometry(v, valid, b_ref, db_ref, geo_ref):
    vx = jnp.where(valid, v[0:1], 2.0 * cutoff_radius)
    vy = jnp.where(valid, v[1:2], 0.0)
    vz = jnp.where(valid, v[2:3], 0.0)
    d = jnp.sqrt(vx * vx + vy * vy + vz * vz)
    inv = 1.0 / d
    geo_ref[0:1, :] = vx * inv
    geo_ref[1:2, :] = vy * inv
    geo_ref[2:3, :] = vz * inv
    geo_ref[3:4, :] = inv
    s = d / cutoff_radius
    s2 = s * s
    s4 = s2 * s2
    s5 = s4 * s
    s6 = s4 * s2
    s7 = s6 * s
    inside = (s < 1.0) & valid
    u = 1.0 - 28.0 * s6 + 48.0 * s7 - 21.0 * s4 * s4
    du = (-168.0 * s5 + 336.0 * s6 - 168.0 * s7) / cutoff_radius
    geo_ref[4:5, :] = jnp.where(inside, u * inverse_neighbours, 0.0)
    geo_ref[5:6, :] = jnp.where(inside, du * inverse_neighbours, 0.0)
    geo_ref[6:8, :] = jnp.zeros_like(geo_ref[6:8, :])
    t = (jnp.minimum(s, 1.0) - 0.5) * jnp.pi
    z = t * t
    cs = 1.0 - z * (1 / 2 - z * (1 / 24 - z * (1 / 720 - z * (1 / 40320 - z * (1 / 3628800 - z * (1 / 479001600 - z * (1 / 87178291200)))))))
    sn = 1.0 - z * (1 / 6 - z * (1 / 120 - z * (1 / 5040 - z * (1 / 362880 - z * (1 / 39916800 - z * (1 / 6227020800))))))
    s1, c1 = cs, -t * sn

    def plus(a, b):
        return a[0] * b[1] + a[1] * b[0], a[1] * b[1] - a[0] * b[0]

    w1 = (s1, c1)
    w2 = plus(w1, w1)
    w3 = plus(w2, w1)
    w4 = plus(w2, w2)
    waves = (w1, w2, w3, w4, plus(w4, w1), plus(w4, w2), plus(w4, w3), plus(w4, w4))
    gain = (2.0 / cutoff_radius) ** 0.5 * inv
    for n, (sine, cosine) in enumerate(waves):
        b_ref[n : n + 1, :] = gain * sine
        db_ref[n : n + 1, :] = gain * (cosine * ((n + 1) * jnp.pi / cutoff_radius) - sine * inv)


def basis_stack(x):
    hi, mid, _ = three(x)
    lo = x - hi
    return jnp.concatenate([hi, lo, hi, jnp.zeros_like(hi)], axis=0).astype(bf16)


def radial_hidden(b, w1, w2, w3):
    h = silu(dot(w1, basis_stack(b)))
    h = silu(dot(w2, stack_rows(h)))
    return silu(dot(w3, stack_rows(h)))


def radial_hidden_pair(b, db, w1, w2, w3):
    h, g = silu_pair(dot(w1, basis_stack(b)))
    t = g * dot(w1, basis_stack(db))
    h, g = silu_pair(dot(w2, stack_rows(h)))
    t = g * dot(w2, stack_rows(t))
    h, g = silu_pair(dot(w3, stack_rows(h)))
    t = g * dot(w3, stack_rows(t))
    return h, t


def angular_rows(geo):
    x, y, z = geo[0:1], geo[1:2], geo[2:3]
    return (
        jnp.ones_like(x),
        R3 * x,
        R3 * y,
        R3 * z,
        R15 * x * y,
        R15 * y * z,
        0.5 * R5 * (3.0 * z * z - 1.0),
        R15 * x * z,
        0.5 * R15 * (x * x - y * y),
    )


def messages(g_ref, lifted, radial_of, l_ref, m_ref):
    for b in range(BLOCKS):
        lift = halves(dot(g_ref[span(b), :], lifted))
        l_ref[span(b), :] = lift
        radial = radial_of(b)
        for l in range(3):
            m_ref[l, span(b), :] = pair_lanes(radial[:, l * C : (l + 1) * C] * lift)


def amplitudes(ast_ref, m_ref, amp_ref):
    for b in range(BLOCKS):
        for l in range(3):
            n = LMS[l]
            o = dot(ast_ref[pl.ds(b * STACK + STACK_AT[l], 32 * n), :], m_ref[l, span(b), :])
            amp = halves(o[: 16 * n]) + o[16 * n :, :C]
            for k in range(n):
                amp_ref[FIRST_LM[l] + k, pl.ds(b * GROUP, GROUP), :] = amp[16 * k : 16 * (k + 1)]


def invariants(amp_ref, gain):
    b0 = amp_ref[0]
    b1 = sum(amp_ref[k] * amp_ref[k] for k in range(1, 4))
    b2 = sum(amp_ref[k] * amp_ref[k] for k in range(4, 9))
    return gain[0:1] * b0 + gain[1:2] * b1 + gain[2:3] * b2 + gain[3:4] * b0 * b0


def amp_grads(amp_ref, gain, gm, ga_ref):
    ga_ref[0] = gm * (gain[0:1] + 2.0 * gain[3:4] * amp_ref[0])
    one = gm * (2.0 * gain[1:2])
    two = gm * (2.0 * gain[2:3])
    for k in range(1, 4):
        ga_ref[k] = one * amp_ref[k]
    for k in range(4, 9):
        ga_ref[k] = two * amp_ref[k]


def group_grads(ga_ref, b, l):
    return jnp.concatenate(
        [ga_ref[FIRST_LM[l] + k, pl.ds(b * GROUP, GROUP), :] for k in range(LMS[l])], axis=0
    )


def spread(turned_ref, ga_ref, b):
    pieces = [split(group_grads(ga_ref, b, l)) for l in range(3)]
    rows = []
    for l in range(2):
        hi, lo = pieces[l]
        none = jnp.zeros_like(hi)
        for part in (hi, hi, lo):
            rows.append(jnp.concatenate([part, none] if l == 0 else [none, part], axis=1))
    first = dot(turned_ref[span(b), 0:PAIR_ROWS], jnp.concatenate(rows, axis=0))
    hi, lo = pieces[2]
    last = turned_ref[span(b), TURNED_AT : TURNED_AT + STACK - PAIR_ROWS]
    return first[:, :C], first[:, C:], dot(last, jnp.concatenate([hi, hi, lo], axis=0))


def angular_grads(m_ref, ga_ref, mask_ref, gy_ref):
    for b in range(BLOCKS):
        mask = mask_ref[:, span(b)]
        for l in (1, 2):
            n = LMS[l]
            hi, lo = split(group_grads(ga_ref, b, l))
            left = jnp.concatenate(
                [jnp.concatenate([hi, hi], axis=1), jnp.concatenate([lo, jnp.zeros_like(lo)], axis=1)],
                axis=0,
            )
            w = dot(left, m_ref[l, span(b), :], NT)
            w = w[: 16 * n] + w[16 * n :]
            for k in range(n):
                row = FIRST_LM[l] + k - 1
                gy_ref[row : row + 1, span(b)] = jnp.sum(mask * w[16 * k : 16 * (k + 1)], axis=0, keepdims=True)


def edge_forces(x_ref, gy_ref, geo_ref, gv_ref):
    gd = dot(jnp.ones((16, 2 * C), bf16), x_ref[...], NT)[0:1]
    gy = [None] + [gy_ref[k : k + 1, :] for k in range(8)]
    x, y, z, inv = (geo_ref[k : k + 1, :] for k in range(4))
    gx = R3 * gy[1] + R15 * (y * gy[4] + z * gy[7] + x * gy[8])
    gyy = R3 * gy[2] + R15 * (x * gy[4] + z * gy[5] - y * gy[8])
    gz = R3 * gy[3] + R15 * (y * gy[5] + x * gy[7]) + (3.0 * R5) * z * gy[6]
    along = x * gx + y * gyy + z * gz
    core = gd - along * inv
    gv_ref[0:1, :] = core * x + gx * inv
    gv_ref[1:2, :] = core * y + gyy * inv
    gv_ref[2:3, :] = core * z + gz * inv
    gv_ref[3:8, :] = jnp.zeros((5, EDGES), f32)


def first_kernel(
    v_ref, pf_ref, pn_ref, qf_ref, qn_ref, dd_ref, g_ref, mask_ref, table_ref, skip_ref, w1_ref, w2_ref, w3_ref, w4_ref,
    gain_ref, outup_ref, tf_ref, tn_ref,
    f_ref, sf_ref, sn_ref, mix_ref, amp_ref, l_ref, m_ref, ast_ref, b_ref, db_ref, geo_ref,
):
    step = (2 * odd("plane") - 1).astype(f32) * (CELLS_Y * cell_side)
    far, near = shifted(qf_ref[...], 1, step), shifted(partner_of(qn_ref), 1, -step)
    valid = jnp.sum(mask_ref[...], axis=0, keepdims=True) > 0.5
    vector, lifted, at = None, [], 0
    for part in (v_ref[...], pf_ref[...], pn_ref[...], far, near):
        rows = part.shape[1]
        piece = pick_lanes(part, dd_ref[at : at + rows, :])
        vector = piece if vector is None else vector + piece
        lifted.append(dot(kinds_of(part[3:4]).astype(bf16), table_ref[...], TN).astype(bf16))
        at += rows
    lifted = jnp.concatenate(lifted, axis=0)
    o = dot(kinds_of(v_ref[3:4, :]).astype(bf16), skip_ref[...], TN)
    skipped = (o[:, :C] + o[:, C : 2 * C]) + o[:, 2 * C :]
    geometry(vector, valid, b_ref, db_ref, geo_ref)
    h = stack_rows(radial_hidden(b_ref[...], w1_ref[0], w2_ref[0], w3_ref[0]) * geo_ref[4:5, :])
    rows = angular_rows(geo_ref[0:3, :])
    for b in range(BLOCKS):
        mask = mask_ref[:, span(b)]
        for l in range(3):
            a = jnp.concatenate(
                [mask * rows[FIRST_LM[l] + k][:, b * SPAN : (b + 1) * SPAN] for k in range(LMS[l])], axis=0
            )
            ast_ref[pl.ds(b * STACK + STACK_AT[l], 48 * LMS[l]), :] = stack_rows(a)
    messages(g_ref, lifted, lambda b: dot(h[:, b * SPAN : (b + 1) * SPAN], w4_ref[0], TN), l_ref, m_ref)
    amplitudes(ast_ref, m_ref, amp_ref)
    mix = invariants(amp_ref, gain_ref[0])
    mix_ref[...] = mix
    lifted = skipped + dot3(mix, outup_ref[...])
    f_ref[...] = lifted
    sf_ref[...] = pick_rows(tf_ref[...], lifted, TN)
    sn_ref[...] = pick_rows(tn_ref[...], lifted, TN)


def own_terms_kernel(v_ref, mix_ref, skip_ref, out0_ref, ref_ref, one_ref, from_first_ref, hid_ref, e_ref):
    kinds = kinds_of(v_ref[3:4, :])
    o = dot(kinds.astype(bf16), skip_ref[...], TN)
    first = ((o[:, :C] + o[:, C : 2 * C]) + o[:, 2 * C :]) + exact(mix_ref[...], out0_ref[...])
    hid_ref[...] = exact(from_first_ref[...], first, NT)
    e_ref[...] = exact(ref_ref[...], kinds) + exact(jnp.broadcast_to(one_ref[...], (8, C)), first, NT)


def middle_kernel(f_ref, rf_ref, rn_ref, pf_ref, pn_ref, a_ref, b_ref):
    rows = jnp.concatenate([f_ref[...], rf_ref[...], rn_ref[...]], axis=0)
    a_ref[...] = pick_rows(pf_ref[...], rows, TN)
    b_ref[...] = pick_rows(pn_ref[...], rows, TN)


def slope_kernel(b_ref, db_ref, geo_ref, w1_ref, w2_ref, w3_ref, q_ref, *, layer):
    h, t = radial_hidden_pair(b_ref[...], db_ref[...], w1_ref[layer], w2_ref[layer], w3_ref[layer])
    q_ref[...] = stack_rows(t * geo_ref[4:5, :] + h * geo_ref[5:6, :])


def radial_kernel(b_ref, db_ref, geo_ref, w1_ref, w2_ref, w3_ref, w4_ref, r_ref, q_ref, *, layer):
    h, t = radial_hidden_pair(b_ref[...], db_ref[...], w1_ref[layer], w2_ref[layer], w3_ref[layer])
    q_ref[...] = stack_rows(t * geo_ref[4:5, :] + h * geo_ref[5:6, :])
    h = stack_rows(h * geo_ref[4:5, :])
    for b in range(BLOCKS):
        r_ref[span(b), :] = dot(h[:, b * SPAN : (b + 1) * SPAN], w4_ref[layer], TN)


def expand_kernel(q_ref, w4_ref, r_ref, *, layer):
    for b in range(BLOCKS):
        r_ref[span(b), :] = dot(q_ref[:, span(b)], w4_ref[layer], TN)


def beside_features_kernel(
    b_ref, db_ref, geo_ref, w1_ref, w2_ref, w3_ref, w4_ref, v_ref, mix_ref, skip_ref, out0_ref, ref_ref, one_ref, from_first_ref,
    ast_ref, r_ref, second_q_ref, first_q_ref, hid_ref, e_ref, turned_ref,
):
    for b in range(BLOCKS):
        turned_ref[span(b), 0:PAIR_ROWS] = jnp.transpose(ast_ref[pl.ds(b * STACK, PAIR_ROWS), :])
        rest = ast_ref[pl.ds(b * STACK + PAIR_ROWS, STACK - PAIR_ROWS), :]
        turned_ref[span(b), TURNED_AT : TURNED_AT + STACK - PAIR_ROWS] = jnp.transpose(rest)
    slope_kernel(b_ref, db_ref, geo_ref, w1_ref, w2_ref, w3_ref, first_q_ref, layer=0)
    radial_kernel(b_ref, db_ref, geo_ref, w1_ref, w2_ref, w3_ref, w4_ref, r_ref, second_q_ref, layer=1)
    own_terms_kernel(v_ref, mix_ref, skip_ref, out0_ref, ref_ref, one_ref, from_first_ref, hid_ref, e_ref)


def second_kernel(
    f_ref, rf_ref, rn_ref, pf_ref, pn_ref, g_ref, gt_ref, ast_ref, turned_ref, r_ref, gain_ref, hid_ref, from_mix_ref, from_mix_ro_ref,
    act_ref, slope_ref, gmid_ref, gf_ref, gn_ref, l_ref, m_ref, ga_ref,
    amp_ref, glift_ref,
):
    lifted = pair_lanes(
        jnp.concatenate([f_ref[...], rf_ref[...], rn_ref[...], pf_ref[...], partner_of(pn_ref)], axis=0)
    )
    messages(g_ref, lifted, lambda b: r_ref[span(b), :], l_ref, m_ref)
    amplitudes(ast_ref, m_ref, amp_ref)
    gain = gain_ref[1]
    act, slope = silu_pair(hid_ref[...] + exact(from_mix_ref[...], invariants(amp_ref, gain), NT))
    act_ref[...] = act
    slope_ref[...] = slope
    amp_grads(amp_ref, gain, dot3(slope, from_mix_ro_ref[...], TN), ga_ref)
    for b in range(BLOCKS):
        grad = None
        for l, z in enumerate(spread(turned_ref, ga_ref, b)):
            term = r_ref[span(b), l * C : (l + 1) * C] * z
            grad = term if grad is None else grad + term
        glift_ref[span(b), :] = pair_lanes(grad)
    glift = halves(dot(gt_ref[...], glift_ref[...]))
    gmid_ref[...] = glift[0:128]
    gf_ref[...] = glift[128:192]
    gn_ref[...] = glift[192:256]


def own_grads_kernel(act_ref, slope_ref, e0_ref, ro_ref, from_first_ro_ref, one_ref, out0_ref, e_ref, gm_ref):
    e_ref[...] = (e0_ref[...] + exact(ro_ref[...], act_ref[...]))[0:1]
    grad = dot3(slope_ref[...], from_first_ro_ref[...], TN) + one_ref[...]
    gm_ref[...] = dot3(grad, out0_ref[...], NT)


def early_kernel(turned_ref, q_ref, w4_ref, l_ref, m_ref, ga_ref, geo_ref, mask_ref, gv_ref, x_ref, gy_ref):
    for b in range(BLOCKS):
        slope = dot(q_ref[:, span(b)], w4_ref[1], TN)
        x = sum(z * slope[:, l * C : (l + 1) * C] for l, z in enumerate(spread(turned_ref, ga_ref, b)))
        x_ref[span(b), :] = pair_lanes(x * l_ref[span(b), :])
    angular_grads(m_ref, ga_ref, mask_ref, gy_ref)
    edge_forces(x_ref, gy_ref, geo_ref, gv_ref)


def beside_grads_kernel(
    turned_ref, second_q_ref, w4_ref, l_ref, m_ref, ga_ref, geo_ref, mask_ref, first_q_ref,
    act_ref, slope_ref, e0_ref, ro_ref, from_first_ro_ref, one_ref, out0_ref,
    gv_ref, dr_ref, e_ref, gm_ref, x_ref, gy_ref,
):
    early_kernel(turned_ref, second_q_ref, w4_ref, l_ref, m_ref, ga_ref, geo_ref, mask_ref, gv_ref, x_ref, gy_ref)
    expand_kernel(first_q_ref, w4_ref, dr_ref, layer=0)
    own_grads_kernel(act_ref, slope_ref, e0_ref, ro_ref, from_first_ro_ref, one_ref, out0_ref, e_ref, gm_ref)


def back_middle_kernel(gmid_ref, rf_ref, rn_ref, pf_ref, pn_ref, own_ref, f_ref, n_ref):
    mid = gmid_ref[...] + (pick_rows(pf_ref[...], rf_ref[...]) + pick_rows(pn_ref[...], partner_of(rn_ref)))
    own_ref[...] = mid[:64]
    f_ref[...] = mid[64:96]
    n_ref[...] = mid[96:128]


def late_kernel(
    own_ref, rf_ref, rn_ref, tf_ref, tn_ref, gm_ref, outup_ref, gain_ref, amp_ref, turned_ref, dr_ref, l_ref, m_ref, geo_ref,
    mask_ref, dd_ref, early_ref, of_ref, pf_ref, pn_ref, qf_ref, qn_ref, ga_ref, gv_ref, x_ref, gy_ref,
):
    grad = own_ref[...] + (pick_rows(tf_ref[...], rf_ref[...]) + pick_rows(tn_ref[...], rn_ref[...]))
    amp_grads(amp_ref, gain_ref[0], gm_ref[...] + dot3(grad, outup_ref[...], NT), ga_ref)
    for b in range(BLOCKS):
        x = None
        for l, z in enumerate(spread(turned_ref, ga_ref, b)):
            term = z * dr_ref[span(b), l * C : (l + 1) * C]
            x = term if x is None else x + term
        x_ref[span(b), :] = pair_lanes(x * l_ref[span(b), :])
    angular_grads(m_ref, ga_ref, mask_ref, gy_ref)
    edge_forces(x_ref, gy_ref, geo_ref, gv_ref)
    total = gv_ref[...] + early_ref[...]
    at = 0
    for ref in (of_ref, pf_ref, pn_ref, qf_ref, qn_ref):
        rows = ref.shape[1]
        ref[...] = pick_lanes(total, dd_ref[at : at + rows, :], NT)
        at += rows


def collect_plane_kernel(of_ref, pf_ref, pn_ref, rf_ref, rn_ref, tf_ref, tn_ref, o_ref, f_ref, n_ref):
    far, near, at = rf_ref[...], partner_of(rn_ref), 0
    for have_ref, ref in ((of_ref, o_ref), (pf_ref, f_ref), (pn_ref, n_ref)):
        rows = ref.shape[1]
        back = pick_lanes(far, tf_ref[at : at + rows, :], NT) + pick_lanes(near, tn_ref[at : at + rows, :], NT)
        ref[...] = have_ref[...] + back
        at += rows


def collect_slab_kernel(v_ref, rf_ref, rn_ref, tf_ref, tn_ref, o_ref):
    back = pick_lanes(rf_ref[...], tf_ref[...], NT) + pick_lanes(rn_ref[...], tn_ref[...], NT)
    forces = -(v_ref[...] + back)
    for k in range(3):
        o_ref[0, k] = forces[k : k + 1]


def swap_slab_far(value):
    count = lax.axis_size("slab")
    pairs = [(i, i + 1) for i in range(1, count - 1, 2)]
    return lax.ppermute(value, "slab", pairs + [(b, a) for a, b in pairs])


def swap_slab_near(value):
    count = lax.axis_size("slab")
    return lax.ppermute(value, "slab", [(i, i ^ 1) for i in range(count)])


def swap_plane_far(value):
    count = lax.axis_size("plane")
    pairs = [(i, (i + 1) % count) for i in range(1, count, 2)]
    return lax.ppermute(value, "plane", pairs + [(b, a) for a, b in pairs])


def swap_plane_near(value):
    count = lax.axis_size("plane")
    return lax.all_gather(value, "plane", axis_index_groups=[[i, i + 1] for i in range(0, count, 2)])


def both(swap_far, swap_near, far, near):
    return swap_far(far), swap_near(near)


def body(
    positions,
    species,
    slab_sends,
    plane_sends,
    edges,
    edge_count,
    embed_table,
    atom_ref,
    radial_one,
    radial_two,
    radial_three,
    radial_four,
    up_weight,
    skip_weight,
    out_weight,
    prod_weight,
    read_one,
    read_hidden,
    read_out,
):
    edge_mat = ((EDGES, C), f32)
    message_mat = ((3, EDGES, 2 * C), bf16)
    by_degree = ((EDGES, 3 * C), f32)
    edge_rows = ((8, EDGES), f32)
    amp_mat = ((9, OWN, C), f32)
    slab_rows = ((32, C), f32)
    plane_rows = ((64, C), f32)
    own_lanes = ((8, OWN), f32)
    slab_lanes = ((8, 32), f32)
    plane_lanes = ((8, 64), f32)

    with jax.named_scope("atoms_slab"):
        *arguments, values, slab_t_far, slab_t_near, plane_t_far, plane_t_near, far, near = call(
            atoms_slab_kernel,
            [own_lanes, ((OWN, 32), bf16), ((OWN, 32), bf16), ((128, 64), bf16), ((128, 64), bf16), slab_lanes, slab_lanes],
            (jnp.transpose(positions, (0, 2, 1, 3)), species[0], slab_sends[0, 0], plane_sends[0, 0]),
            carried=(
                edges[0, 0], radial_one, radial_two, radial_three, radial_four, embed_table, up_weight, skip_weight,
                atom_ref[None, :], jnp.transpose(read_hidden), read_out[None, :], out_weight, prod_weight, read_one[None, :],
            ),
            name="atoms_slab",
        )
        far, near = both(swap_slab_far, swap_slab_near, far, near)
    with jax.named_scope("prepare"):
        sender_n, sender_t, edge_t, mask, *prepared = call(
            prepare_kernel,
            [((EDGES, EXT), bf16), ((EXT, EDGES), bf16), ((EXT, EDGES), bf16), ((GROUP, EDGES), f32),
             ((2, 64, 32), bf16), ((2, 64, 192), bf16), ((2, 64, 192), bf16), ((2, 192, 3 * C), bf16),
             ((KINDS, 2 * C), bf16), ((KINDS, 3 * C), bf16), ((KINDS, 3 * C), bf16), ((8, KINDS), f32),
             *[((16, C), f32)] * 4, ((C, C), f32), ((C, C), f32), ((2, 4, C), f32), ((1, C), f32), ((8, 16), f32)],
            arguments,
            flops=1_000_000_000,
            name="prepare",
        )
        weights = tuple(prepared[:4])
        (table, skip_table, skip_up_table, ref_row, from_first, from_mix, from_first_ro, from_mix_ro, out_up, out_first,
         gains, read_row, read_last) = prepared[4:]
    with jax.named_scope("atoms_plane"):
        far, near, edge_t = lax.optimization_barrier((far, near, edge_t))
        slab_far, slab_near, far, near = call(
            atoms_plane_kernel,
            [slab_lanes, slab_lanes, plane_lanes, plane_lanes],
            (values, far, near, plane_t_far, plane_t_near),
            name="atoms_plane",
        )
        far, near = both(swap_plane_far, swap_plane_near, far, near)

    hidden_mat = ((16, OWN), f32)
    with jax.named_scope("first_layer"):
        (first, s_far, s_near, mix, amp_first, lift_first, message_first, angular, basis, basis_slope, geo) = call(
            first_kernel,
            [plane_rows, slab_rows, slab_rows, plane_rows, amp_mat, edge_mat, message_mat,
             ((BLOCKS * STACK, SPAN), bf16), edge_rows, edge_rows, edge_rows],
            (values, slab_far, slab_near, far, near, edge_t, sender_n, mask, table, skip_up_table, *weights,
             gains, out_up, slab_t_far, slab_t_near),
            name="first_layer",
        )
    with jax.named_scope("features_slab"):
        slab_far, slab_near = both(swap_slab_far, swap_slab_near, s_far, s_near)
    radial_second, slope_second, slope_first, hidden, energies, turned = call(
        beside_features_kernel,
        [by_degree, ((192, EDGES), bf16), ((192, EDGES), bf16), hidden_mat, own_lanes, ((EDGES, TURNED), bf16)],
        (basis, basis_slope, geo, *weights, values, mix, skip_table, out_first, ref_row, read_row, from_first,
         angular),
        flops=1_000_000_000, name="beside_features",
    )
    with jax.named_scope("features_plane"):
        slab_far, slab_near, radial_second = lax.optimization_barrier((slab_far, slab_near, radial_second))
        far, near = call(
            middle_kernel, [plane_rows] * 2, (first, slab_far, slab_near, plane_t_far, plane_t_near), name="middle"
        )
        far, near = both(swap_plane_far, swap_plane_near, far, near)
    with jax.named_scope("second_layer"):
        act, slope, gmid, far, near, lift_second, message_second, ga = call(
            second_kernel,
            [hidden_mat, hidden_mat, ((128, C), f32), plane_rows, plane_rows, edge_mat, message_mat, amp_mat],
            (first, slab_far, slab_near, far, near, sender_n, sender_t, angular, turned, radial_second, gains, hidden, from_mix,
             from_mix_ro),
            scratch=[pltpu.VMEM((9, OWN, C), f32), pltpu.VMEM((EDGES, 2 * C), bf16)],
            name="second_layer",
        )
    with jax.named_scope("feature_grads_plane"):
        far, near = both(swap_plane_far, swap_plane_near, far, near)
    with jax.named_scope("feature_grads_slab"):
        own, far, near = call(
            back_middle_kernel, [plane_rows, slab_rows, slab_rows], (gmid, far, near, plane_t_far, plane_t_near),
            name="back_middle",
        )
        far, near, ga = lax.optimization_barrier((far, near, ga))
        far, near = both(swap_slab_far, swap_slab_near, far, near)
    early, slope_first, energies, own_grads = call(
        beside_grads_kernel,
        [edge_rows, by_degree, ((1, OWN), f32), plane_rows],
        (turned, slope_second, weights[3], lift_second, message_second, ga, geo, mask, slope_first,
         act, slope, energies, read_last, from_first_ro, read_row, out_first),
        scratch=[pltpu.VMEM((EDGES, 2 * C), bf16), pltpu.VMEM((8, EDGES), f32)],
        flops=1_000_000_000, name="beside_grads",
    )
    with jax.named_scope("late_forces"):
        own, slab_far, slab_near, far, near = call(
            late_kernel,
            [own_lanes, slab_lanes, slab_lanes, plane_lanes, plane_lanes],
            (own, far, near, slab_t_far, slab_t_near, own_grads, out_up, gains, amp_first, turned, slope_first,
             lift_first, message_first, geo, mask, edge_t, early),
            scratch=[pltpu.VMEM((9, OWN, C), f32), pltpu.VMEM((8, EDGES), f32), pltpu.VMEM((EDGES, 2 * C), bf16),
                     pltpu.VMEM((8, EDGES), f32)],
            name="late_forces",
        )
    with jax.named_scope("position_grads_plane"):
        far, near = both(swap_plane_far, swap_plane_near, far, near)
        own, far, near = call(
            collect_plane_kernel, [own_lanes, slab_lanes, slab_lanes],
            (own, slab_far, slab_near, far, near, plane_t_far, plane_t_near), name="collect_plane",
        )
    with jax.named_scope("position_grads_slab"):
        far, near = both(swap_slab_far, swap_slab_near, far, near)
        forces, = call(
            collect_slab_kernel, [((1, 3, 1, OWN), f32)], (own, far, near, slab_t_far, slab_t_near), name="collect_slab",
        )
    return (energies[None], jnp.transpose(forces, (0, 2, 1, 3)))


def solution(mesh):
    in_specs = (
        P("slab", "plane", None, None),
        P("slab", "plane", None),
        P("slab", "plane", None, None),
        P("slab", "plane", None, None),
        P("slab", "plane", None, None),
        P("slab", "plane"),
    ) + (P(),) * 13
    out_specs = (P("slab", "plane", None), P("slab", "plane", None, None))
    return jax.shard_map(body, mesh=mesh, in_specs=in_specs, out_specs=out_specs, check_vma=False)
```

```python
import functools

import jax
import jax.numpy as jnp
from jax import lax
from jax.experimental import pallas as pl
from jax.experimental.pallas import tpu as pltpu
from jax.sharding import PartitionSpec as P

CELLS_Y = 2
CELLS_Z = 2

cutoff_radius = 5.0
cell_side = 3.0
inverse_neighbours = 0.2
highest = lax.Precision.HIGHEST
f32 = jnp.float32
bf16 = jnp.bfloat16

C = 128
OWN = 64
EXT = 256
EDGES = 1536
BLOCKS = 4
GROUP = 16
SPAN = EDGES // BLOCKS
KINDS = 96
LMS = (1, 3, 5)
FIRST_LM = (0, 1, 4)
STACK_AT = (0, 48, 192)
STACK = 432
PAIR_ROWS = 192
TURNED_AT = 256
TURNED = 512
R3, R5, R15 = 3.0**0.5, 5.0**0.5, 15.0**0.5

NN = (((1,), (0,)), ((), ()))
TN = (((0,), (0,)), ((), ()))
NT = (((1,), (1,)), ((), ()))


def dot(a, b, dims=NN):
    return lax.dot_general(a, b, dims, preferred_element_type=f32)


def dot3(a, b, dims=NN):
    return lax.dot_general(a, b, dims, precision=lax.Precision.HIGH, preferred_element_type=f32)


def exact(a, b, dims=NN):
    return lax.dot_general(a, b, dims, precision=highest, preferred_element_type=f32)


def split(x):
    hi = x.astype(bf16)
    return hi, (x - hi.astype(f32)).astype(bf16)


def pair_lanes(x):
    hi, lo = split(x)
    return jnp.concatenate([hi, lo], axis=1)


def halves(o):
    return o[:, :C] + o[:, C:]


def stack_rows(x):
    hi, lo = split(x)
    return jnp.concatenate([hi, lo, hi], axis=0)


def three(x):
    hi = x.astype(bf16).astype(f32)
    rest = x - hi
    mid = rest.astype(bf16).astype(f32)
    return hi, mid, rest - mid


def pick_lanes(values, chooser, dims=NN):
    hi, mid, lo = three(values)
    o = dot(jnp.concatenate([hi, mid, lo, jnp.zeros_like(lo)], axis=0).astype(bf16), chooser, dims)
    return (o[0:8] + o[8:16]) + o[16:24]


def pick_rows(chooser, values, dims=NN):
    hi, mid, lo = three(values)
    o = dot(chooser, jnp.concatenate([hi, mid, lo], axis=1).astype(bf16), dims)
    return (o[:, :C] + o[:, C : 2 * C]) + o[:, 2 * C :]


def sigmoid(x):
    return 0.5 + 0.5 * jnp.tanh(0.5 * x)


def silu(x):
    return x * sigmoid(x)


def silu_pair(x):
    s = sigmoid(x)
    return x * s, s * (1.0 + x * (1.0 - s))


def span(b):
    return pl.ds(b * SPAN, SPAN)


def fetched(kernel, count, carried):
    def run(*refs):
        given, rest = refs[: count + carried], refs[count + carried :]
        sems, held = rest[-1], rest[-1 - count : -1]
        targets = held + rest[:carried]
        copies = [pltpu.make_async_copy(src, dst, sems.at[k]) for k, (src, dst) in enumerate(zip(given, targets))]
        for copy in copies:
            copy.start()
        for copy in copies[:count]:
            copy.wait()
        kernel(*held, *rest[carried : -1 - count])
        for copy in copies[count:]:
            copy.wait()

    return run


def call(kernel, outs, args, scratch=(), flops=0, name=None, limit=8, carried=None):
    spec = pl.BlockSpec(memory_space=pltpu.VMEM)
    scratch = list(scratch)
    if carried is not None:
        scratch += [pltpu.VMEM(a.shape, a.dtype) for a in args]
        scratch.append(pltpu.SemaphoreType.DMA((len(args) + len(carried),)))
        kernel = fetched(kernel, len(args), len(carried))
        outs = [(a.shape, a.dtype) for a in carried] + list(outs)
        args = [pltpu.with_memory_space_constraint(a, pltpu.HBM) for a in [*args, *carried]]
        in_specs = [pl.BlockSpec(memory_space=pltpu.HBM)] * len(args)
    else:
        args = [pltpu.with_memory_space_constraint(a, pltpu.VMEM) for a in args]
        in_specs = [spec] * len(args)
    out_shape = tuple(pltpu.VMEM(shape, dtype) for shape, dtype in outs)
    moved = sum(a.size * a.dtype.itemsize for a in args)
    return pl.pallas_call(
        kernel,
        out_shape=out_shape,
        in_specs=in_specs,
        out_specs=tuple(spec for _ in out_shape),
        scratch_shapes=scratch,
        compiler_params=pltpu.CompilerParams(vmem_limit_bytes=limit * 1024 * 1024),
        cost_estimate=pl.CostEstimate(flops=flops, bytes_accessed=moved, transcendentals=0),
        name=name,
    )(*args)


def odd(axis):
    return lax.rem(lax.axis_index(axis), 2)


def partner_of(ref):
    return jnp.where(jnp.full(ref.shape[1:], odd("plane")) == 1, ref[0], ref[1])


def by_parity(flag, rows):
    swap = jnp.full(rows[0:1].shape, flag) == 1
    return jnp.where(swap, rows[0:1], rows[1:2]), jnp.where(swap, rows[1:2], rows[0:1])


def moved_slab(slot):
    swap = (jnp.full(slot.shape, odd("slab")) == 1) & (slot >= 64) & (slot < 128)
    return jnp.where(swap, slot ^ 32, slot)


def chooser(slots, picked):
    rows = lax.broadcasted_iota(jnp.int32, (slots, picked.shape[1]), 0)
    return (rows == picked).astype(f32).astype(bf16)


def shifted(values, row, step):
    rows = lax.broadcasted_iota(jnp.int32, values.shape, 0)
    return values + jnp.where(rows == row, step, 0.0)


def atoms_slab_kernel(
    pos_ref, kind_ref, list_ref, plane_ref, v_ref, tf_ref, tn_ref, pf_ref, pn_ref, far_ref, near_ref
):
    for k in range(3):
        v_ref[k : k + 1, :] = pos_ref[0, k]
    v_ref[3:4, :] = kind_ref[...].astype(f32)
    v_ref[4:8, :] = jnp.zeros((4, OWN), f32)
    far, near = by_parity(odd("slab"), list_ref[...])
    far, near = chooser(OWN, far), chooser(OWN, near)
    tf_ref[...] = far
    tn_ref[...] = near
    v = v_ref[...]
    far_ref[...] = pick_lanes(v, far)
    near_ref[...] = pick_lanes(v, near)
    for picked, t_ref in zip(by_parity(odd("plane"), plane_ref[...]), (pf_ref, pn_ref)):
        t_ref[...] = chooser(128, moved_slab(picked))


def atoms_plane_kernel(v_ref, far_ref, near_ref, tf_ref, tn_ref, pf_ref, pn_ref, sf_ref, sn_ref):
    step = (2 * odd("slab") - 1).astype(f32) * (CELLS_Z * cell_side)
    far = shifted(far_ref[...], 2, step)
    near = shifted(near_ref[...], 2, -step)
    pf_ref[...] = far
    pn_ref[...] = near
    own = v_ref[...]
    for t_ref, s_ref in ((tf_ref, sf_ref), (tn_ref, sn_ref)):
        s_ref[...] = pick_lanes(own, t_ref[0:64, :]) + (
            pick_lanes(far, t_ref[64:96, :]) + pick_lanes(near, t_ref[96:128, :])
        )


def prepare_kernel(
    edge_ref, one_ref, two_ref, three_ref, four_ref, embed_ref, up_ref, skip_ref, atom_ref, hid_ref, ro_ref,
    out_ref, gain_ref, read_ref,
    g_ref, gt_ref, dd_ref, mask_ref, w1_ref, w2_ref, w3_ref, w4_ref, table_ref, skips_ref, skipups_ref, refs_ref,
    from_first_ref, from_mix_ref, from_first_ro_ref, from_mix_ro_ref, outup_ref, out0_ref, gains_ref, reads_ref, ros_ref,
):
    per_atom = jnp.sum((edge_ref[1:2, :] == OWN - 1).astype(f32)).astype(jnp.int32)
    senders = jnp.broadcast_to(edge_ref[0:1, :], (8, EDGES))
    swap_plane = jnp.full((1, SPAN), odd("plane")) == 1
    place = lax.broadcasted_iota(jnp.int32, (GROUP, SPAN), 1)
    first_place = lax.broadcasted_iota(jnp.int32, (GROUP, SPAN), 0) * per_atom
    mask = ((place >= first_place) & (place < first_place + per_atom)).astype(f32)
    lanes = lax.broadcasted_iota(jnp.int32, (128, 128), 1).astype(f32)
    for b in range(BLOCKS):
        start = b * GROUP * per_atom
        rows = senders if b == 0 else pltpu.roll(senders, lax.rem(EDGES - start, EDGES), 1)
        row = rows[0:1, :SPAN]
        row = moved_slab(row)
        row = jnp.where(swap_plane & (row >= 128), row ^ 64, row)
        row = jnp.where(place[0:1] < GROUP * per_atom, row, -1)
        t = (lax.broadcasted_iota(jnp.int32, (EXT, SPAN), 0) == row).astype(f32)
        gt_ref[:, span(b)] = t.astype(bf16)
        dd_ref[:, span(b)] = t.astype(bf16)
        mine = pl.ds(b * GROUP, GROUP)
        dd_ref[mine, span(b)] = (t[b * GROUP : (b + 1) * GROUP] - mask).astype(bf16)
        mask_ref[:, span(b)] = mask
        for chunk in range(SPAN // 128):
            part = row[:, chunk * 128 : (chunk + 1) * 128].astype(f32)
            column = jnp.transpose(jnp.broadcast_to(part, (128, 128)))
            here = pl.ds(b * SPAN + chunk * 128, 128)
            g_ref[here, 0:128] = (column == lanes).astype(f32).astype(bf16)
            g_ref[here, 128:256] = (column == lanes + 128.0).astype(f32).astype(bf16)
    for t in range(2):
        hi, mid, lo = three(one_ref[t])
        stacked = jnp.concatenate([hi, hi, mid + lo, jnp.zeros_like(hi)], axis=0)
        w1_ref[t] = jnp.transpose(stacked).astype(bf16)
        for ref, to_ref in ((two_ref, w2_ref), (three_ref, w3_ref)):
            hi, mid, lo = three(ref[t])
            to_ref[t] = jnp.transpose(jnp.concatenate([hi, hi, mid + lo], axis=0)).astype(bf16)
        hi, lo = split(four_ref[t])
        w4_ref[t] = jnp.concatenate([hi, hi, lo], axis=0)
    embed = embed_ref[...]
    kinds = embed.shape[0]
    for ref in (table_ref, skips_ref, skipups_ref):
        ref[...] = jnp.zeros(ref.shape, bf16)
    table_ref[0:kinds, :] = pair_lanes(exact(embed, up_ref[0]))
    skipped = exact(embed, skip_ref[0])
    for ref, values in ((skips_ref, skipped), (skipups_ref, exact(skipped, up_ref[1]))):
        hi, mid, lo = three(values)
        ref[0:kinds, :] = jnp.concatenate([hi, mid, lo], axis=1).astype(bf16)
    refs_ref[...] = jnp.zeros(refs_ref.shape, f32)
    refs_ref[0:1, 0:kinds] = atom_ref[...]
    last = jnp.transpose(jnp.broadcast_to(ro_ref[...], (C, ro_ref.shape[1])))
    from_first = exact(hid_ref[...], skip_ref[1], NT)
    from_mix = exact(hid_ref[...], out_ref[1], NT)
    from_first_ref[...] = from_first
    from_mix_ref[...] = from_mix
    from_first_ro_ref[...] = from_first * last
    from_mix_ro_ref[...] = from_mix * last
    outup_ref[...] = exact(out_ref[0], up_ref[1])
    out0_ref[...] = out_ref[0]
    gains_ref[...] = gain_ref[...]
    reads_ref[...] = read_ref[...]
    ros_ref[...] = jnp.broadcast_to(ro_ref[...], ros_ref.shape)


def kinds_of(row):
    kinds = lax.broadcasted_iota(jnp.int32, (KINDS, row.shape[1]), 0).astype(f32) == row
    return kinds.astype(f32)


def geometry(v, valid, b_ref, db_ref, geo_ref):
    vx = jnp.where(valid, v[0:1], 2.0 * cutoff_radius)
    vy = jnp.where(valid, v[1:2], 0.0)
    vz = jnp.where(valid, v[2:3], 0.0)
    d = jnp.sqrt(vx * vx + vy * vy + vz * vz)
    inv = 1.0 / d
    geo_ref[0:1, :] = vx * inv
    geo_ref[1:2, :] = vy * inv
    geo_ref[2:3, :] = vz * inv
    geo_ref[3:4, :] = inv
    s = d / cutoff_radius
    s2 = s * s
    s4 = s2 * s2
    s5 = s4 * s
    s6 = s4 * s2
    s7 = s6 * s
    inside = (s < 1.0) & valid
    u = 1.0 - 28.0 * s6 + 48.0 * s7 - 21.0 * s4 * s4
    du = (-168.0 * s5 + 336.0 * s6 - 168.0 * s7) / cutoff_radius
    geo_ref[4:5, :] = jnp.where(inside, u * inverse_neighbours, 0.0)
    geo_ref[5:6, :] = jnp.where(inside, du * inverse_neighbours, 0.0)
    geo_ref[6:8, :] = jnp.zeros_like(geo_ref[6:8, :])
    t = (jnp.minimum(s, 1.0) - 0.5) * jnp.pi
    z = t * t
    cs = 1.0 - z * (1 / 2 - z * (1 / 24 - z * (1 / 720 - z * (1 / 40320 - z * (1 / 3628800 - z * (1 / 479001600 - z * (1 / 87178291200)))))))
    sn = 1.0 - z * (1 / 6 - z * (1 / 120 - z * (1 / 5040 - z * (1 / 362880 - z * (1 / 39916800 - z * (1 / 6227020800))))))
    s1, c1 = cs, -t * sn

    def plus(a, b):
        return a[0] * b[1] + a[1] * b[0], a[1] * b[1] - a[0] * b[0]

    w1 = (s1, c1)
    w2 = plus(w1, w1)
    w3 = plus(w2, w1)
    w4 = plus(w2, w2)
    waves = (w1, w2, w3, w4, plus(w4, w1), plus(w4, w2), plus(w4, w3), plus(w4, w4))
    gain = (2.0 / cutoff_radius) ** 0.5 * inv
    for n, (sine, cosine) in enumerate(waves):
        b_ref[n : n + 1, :] = gain * sine
        db_ref[n : n + 1, :] = gain * (cosine * ((n + 1) * jnp.pi / cutoff_radius) - sine * inv)


def basis_stack(x):
    hi, mid, _ = three(x)
    lo = x - hi
    return jnp.concatenate([hi, lo, hi, jnp.zeros_like(hi)], axis=0).astype(bf16)


def radial_hidden(b, w1, w2, w3):
    h = silu(dot(w1, basis_stack(b)))
    h = silu(dot(w2, stack_rows(h)))
    return silu(dot(w3, stack_rows(h)))


def radial_hidden_pair(b, db, w1, w2, w3):
    h, g = silu_pair(dot(w1, basis_stack(b)))
    t = g * dot(w1, basis_stack(db))
    h, g = silu_pair(dot(w2, stack_rows(h)))
    t = g * dot(w2, stack_rows(t))
    h, g = silu_pair(dot(w3, stack_rows(h)))
    t = g * dot(w3, stack_rows(t))
    return h, t


def angular_rows(geo):
    x, y, z = geo[0:1], geo[1:2], geo[2:3]
    return (
        jnp.ones_like(x),
        R3 * x,
        R3 * y,
        R3 * z,
        R15 * x * y,
        R15 * y * z,
        0.5 * R5 * (3.0 * z * z - 1.0),
        R15 * x * z,
        0.5 * R15 * (x * x - y * y),
    )


def messages(g_ref, lifted, radial_of, l_ref, m_ref):
    for b in range(BLOCKS):
        lift = halves(dot(g_ref[span(b), :], lifted))
        l_ref[span(b), :] = lift
        radial = radial_of(b)
        for l in range(3):
            m_ref[l, span(b), :] = pair_lanes(radial[:, l * C : (l + 1) * C] * lift)


def amplitudes(ast_ref, m_ref, amp_ref):
    for b in range(BLOCKS):
        for l in range(3):
            n = LMS[l]
            o = dot(ast_ref[pl.ds(b * STACK + STACK_AT[l], 32 * n), :], m_ref[l, span(b), :])
            amp = halves(o[: 16 * n]) + o[16 * n :, :C]
            for k in range(n):
                amp_ref[FIRST_LM[l] + k, pl.ds(b * GROUP, GROUP), :] = amp[16 * k : 16 * (k + 1)]


def invariants(amp_ref, gain):
    b0 = amp_ref[0]
    b1 = sum(amp_ref[k] * amp_ref[k] for k in range(1, 4))
    b2 = sum(amp_ref[k] * amp_ref[k] for k in range(4, 9))
    return gain[0:1] * b0 + gain[1:2] * b1 + gain[2:3] * b2 + gain[3:4] * b0 * b0


def amp_grads(amp_ref, gain, gm, ga_ref):
    ga_ref[0] = gm * (gain[0:1] + 2.0 * gain[3:4] * amp_ref[0])
    one = gm * (2.0 * gain[1:2])
    two = gm * (2.0 * gain[2:3])
    for k in range(1, 4):
        ga_ref[k] = one * amp_ref[k]
    for k in range(4, 9):
        ga_ref[k] = two * amp_ref[k]


def group_grads(ga_ref, b, l):
    return jnp.concatenate(
        [ga_ref[FIRST_LM[l] + k, pl.ds(b * GROUP, GROUP), :] for k in range(LMS[l])], axis=0
    )


def spread(turned_ref, ga_ref, b):
    pieces = [split(group_grads(ga_ref, b, l)) for l in range(3)]
    rows = []
    for l in range(2):
        hi, lo = pieces[l]
        none = jnp.zeros_like(hi)
        for part in (hi, hi, lo):
            rows.append(jnp.concatenate([part, none] if l == 0 else [none, part], axis=1))
    first = dot(turned_ref[span(b), 0:PAIR_ROWS], jnp.concatenate(rows, axis=0))
    hi, lo = pieces[2]
    last = turned_ref[span(b), TURNED_AT : TURNED_AT + STACK - PAIR_ROWS]
    return first[:, :C], first[:, C:], dot(last, jnp.concatenate([hi, hi, lo], axis=0))


def angular_grads(m_ref, ga_ref, mask_ref, gy_ref):
    for b in range(BLOCKS):
        mask = mask_ref[:, span(b)]
        for l in (1, 2):
            n = LMS[l]
            hi, lo = split(group_grads(ga_ref, b, l))
            left = jnp.concatenate(
                [jnp.concatenate([hi, hi], axis=1), jnp.concatenate([lo, jnp.zeros_like(lo)], axis=1)],
                axis=0,
            )
            w = dot(left, m_ref[l, span(b), :], NT)
            w = w[: 16 * n] + w[16 * n :]
            for k in range(n):
                row = FIRST_LM[l] + k - 1
                gy_ref[row : row + 1, span(b)] = jnp.sum(mask * w[16 * k : 16 * (k + 1)], axis=0, keepdims=True)


def edge_forces(x_ref, gy_ref, geo_ref, gv_ref):
    gd = dot(jnp.ones((16, 2 * C), bf16), x_ref[...], NT)[0:1]
    gy = [None] + [gy_ref[k : k + 1, :] for k in range(8)]
    x, y, z, inv = (geo_ref[k : k + 1, :] for k in range(4))
    gx = R3 * gy[1] + R15 * (y * gy[4] + z * gy[7] + x * gy[8])
    gyy = R3 * gy[2] + R15 * (x * gy[4] + z * gy[5] - y * gy[8])
    gz = R3 * gy[3] + R15 * (y * gy[5] + x * gy[7]) + (3.0 * R5) * z * gy[6]
    along = x * gx + y * gyy + z * gz
    core = gd - along * inv
    gv_ref[0:1, :] = core * x + gx * inv
    gv_ref[1:2, :] = core * y + gyy * inv
    gv_ref[2:3, :] = core * z + gz * inv
    gv_ref[3:8, :] = jnp.zeros((5, EDGES), f32)


def first_kernel(
    v_ref, pf_ref, pn_ref, qf_ref, qn_ref, dd_ref, g_ref, mask_ref, table_ref, skip_ref, w1_ref, w2_ref, w3_ref, w4_ref,
    gain_ref, outup_ref, tf_ref, tn_ref,
    f_ref, sf_ref, sn_ref, mix_ref, amp_ref, l_ref, m_ref, ast_ref, b_ref, db_ref, geo_ref,
):
    step = (2 * odd("plane") - 1).astype(f32) * (CELLS_Y * cell_side)
    far, near = shifted(qf_ref[...], 1, step), shifted(partner_of(qn_ref), 1, -step)
    valid = jnp.sum(mask_ref[...], axis=0, keepdims=True) > 0.5
    vector, lifted, at = None, [], 0
    for part in (v_ref[...], pf_ref[...], pn_ref[...], far, near):
        rows = part.shape[1]
        piece = pick_lanes(part, dd_ref[at : at + rows, :])
        vector = piece if vector is None else vector + piece
        lifted.append(dot(kinds_of(part[3:4]).astype(bf16), table_ref[...], TN).astype(bf16))
        at += rows
    lifted = jnp.concatenate(lifted, axis=0)
    o = dot(kinds_of(v_ref[3:4, :]).astype(bf16), skip_ref[...], TN)
    skipped = (o[:, :C] + o[:, C : 2 * C]) + o[:, 2 * C :]
    geometry(vector, valid, b_ref, db_ref, geo_ref)
    h = stack_rows(radial_hidden(b_ref[...], w1_ref[0], w2_ref[0], w3_ref[0]) * geo_ref[4:5, :])
    rows = angular_rows(geo_ref[0:3, :])
    for b in range(BLOCKS):
        mask = mask_ref[:, span(b)]
        for l in range(3):
            a = jnp.concatenate(
                [mask * rows[FIRST_LM[l] + k][:, b * SPAN : (b + 1) * SPAN] for k in range(LMS[l])], axis=0
            )
            ast_ref[pl.ds(b * STACK + STACK_AT[l], 48 * LMS[l]), :] = stack_rows(a)
    messages(g_ref, lifted, lambda b: dot(h[:, b * SPAN : (b + 1) * SPAN], w4_ref[0], TN), l_ref, m_ref)
    amplitudes(ast_ref, m_ref, amp_ref)
    mix = invariants(amp_ref, gain_ref[0])
    mix_ref[...] = mix
    lifted = skipped + dot3(mix, outup_ref[...])
    f_ref[...] = lifted
    sf_ref[...] = pick_rows(tf_ref[...], lifted, TN)
    sn_ref[...] = pick_rows(tn_ref[...], lifted, TN)


def own_terms_kernel(v_ref, mix_ref, skip_ref, out0_ref, ref_ref, one_ref, from_first_ref, hid_ref, e_ref):
    kinds = kinds_of(v_ref[3:4, :])
    o = dot(kinds.astype(bf16), skip_ref[...], TN)
    first = ((o[:, :C] + o[:, C : 2 * C]) + o[:, 2 * C :]) + dot3(mix_ref[...], out0_ref[...])
    hid_ref[...] = dot3(from_first_ref[...], first, NT)
    e_ref[...] = exact(ref_ref[...], kinds) + exact(jnp.broadcast_to(one_ref[...], (8, C)), first, NT)


def middle_kernel(f_ref, rf_ref, rn_ref, pf_ref, pn_ref, a_ref, b_ref):
    rows = jnp.concatenate([f_ref[...], rf_ref[...], rn_ref[...]], axis=0)
    a_ref[...] = pick_rows(pf_ref[...], rows, TN)
    b_ref[...] = pick_rows(pn_ref[...], rows, TN)


def slope_kernel(b_ref, db_ref, geo_ref, w1_ref, w2_ref, w3_ref, q_ref, *, layer):
    h, t = radial_hidden_pair(b_ref[...], db_ref[...], w1_ref[layer], w2_ref[layer], w3_ref[layer])
    q_ref[...] = stack_rows(t * geo_ref[4:5, :] + h * geo_ref[5:6, :])


def radial_kernel(b_ref, db_ref, geo_ref, w1_ref, w2_ref, w3_ref, w4_ref, r_ref, q_ref, *, layer):
    h, t = radial_hidden_pair(b_ref[...], db_ref[...], w1_ref[layer], w2_ref[layer], w3_ref[layer])
    q_ref[...] = stack_rows(t * geo_ref[4:5, :] + h * geo_ref[5:6, :])
    h = stack_rows(h * geo_ref[4:5, :])
    for b in range(BLOCKS):
        r_ref[span(b), :] = dot(h[:, b * SPAN : (b + 1) * SPAN], w4_ref[layer], TN)


def expand_kernel(q_ref, w4_ref, r_ref, *, layer):
    for b in range(BLOCKS):
        r_ref[span(b), :] = dot(q_ref[:, span(b)], w4_ref[layer], TN)


def beside_features_kernel(
    b_ref, db_ref, geo_ref, w1_ref, w2_ref, w3_ref, w4_ref, v_ref, mix_ref, skip_ref, out0_ref, ref_ref, one_ref, from_first_ref,
    ast_ref, r_ref, second_q_ref, first_q_ref, hid_ref, e_ref, turned_ref,
):
    for b in range(BLOCKS):
        turned_ref[span(b), 0:PAIR_ROWS] = jnp.transpose(ast_ref[pl.ds(b * STACK, PAIR_ROWS), :])
        rest = ast_ref[pl.ds(b * STACK + PAIR_ROWS, STACK - PAIR_ROWS), :]
        turned_ref[span(b), TURNED_AT : TURNED_AT + STACK - PAIR_ROWS] = jnp.transpose(rest)
    slope_kernel(b_ref, db_ref, geo_ref, w1_ref, w2_ref, w3_ref, first_q_ref, layer=0)
    radial_kernel(b_ref, db_ref, geo_ref, w1_ref, w2_ref, w3_ref, w4_ref, r_ref, second_q_ref, layer=1)
    own_terms_kernel(v_ref, mix_ref, skip_ref, out0_ref, ref_ref, one_ref, from_first_ref, hid_ref, e_ref)


def second_kernel(
    f_ref, rf_ref, rn_ref, pf_ref, pn_ref, g_ref, gt_ref, ast_ref, turned_ref, r_ref, gain_ref, hid_ref, from_mix_ref, from_mix_ro_ref,
    act_ref, slope_ref, gmid_ref, gf_ref, gn_ref, l_ref, m_ref, ga_ref,
    amp_ref, glift_ref,
):
    lifted = pair_lanes(
        jnp.concatenate([f_ref[...], rf_ref[...], rn_ref[...], pf_ref[...], partner_of(pn_ref)], axis=0)
    )
    messages(g_ref, lifted, lambda b: r_ref[span(b), :], l_ref, m_ref)
    amplitudes(ast_ref, m_ref, amp_ref)
    gain = gain_ref[1]
    act, slope = silu_pair(hid_ref[...] + dot3(from_mix_ref[...], invariants(amp_ref, gain), NT))
    act_ref[...] = act
    slope_ref[...] = slope
    amp_grads(amp_ref, gain, dot3(slope, from_mix_ro_ref[...], TN), ga_ref)
    for b in range(BLOCKS):
        grad = None
        for l, z in enumerate(spread(turned_ref, ga_ref, b)):
            term = r_ref[span(b), l * C : (l + 1) * C] * z
            grad = term if grad is None else grad + term
        glift_ref[span(b), :] = pair_lanes(grad)
    glift = halves(dot(gt_ref[...], glift_ref[...]))
    gmid_ref[...] = glift[0:128]
    gf_ref[...] = glift[128:192]
    gn_ref[...] = glift[192:256]


def own_grads_kernel(act_ref, slope_ref, e0_ref, ro_ref, from_first_ro_ref, one_ref, out0_ref, e_ref, gm_ref):
    e_ref[...] = (e0_ref[...] + exact(ro_ref[...], act_ref[...]))[0:1]
    grad = dot3(slope_ref[...], from_first_ro_ref[...], TN) + one_ref[...]
    gm_ref[...] = dot3(grad, out0_ref[...], NT)


def early_kernel(turned_ref, q_ref, w4_ref, l_ref, m_ref, ga_ref, geo_ref, mask_ref, gv_ref, x_ref, gy_ref):
    for b in range(BLOCKS):
        slope = dot(q_ref[:, span(b)], w4_ref[1], TN)
        x = sum(z * slope[:, l * C : (l + 1) * C] for l, z in enumerate(spread(turned_ref, ga_ref, b)))
        x_ref[span(b), :] = pair_lanes(x * l_ref[span(b), :])
    angular_grads(m_ref, ga_ref, mask_ref, gy_ref)
    edge_forces(x_ref, gy_ref, geo_ref, gv_ref)


def beside_grads_kernel(
    turned_ref, second_q_ref, w4_ref, l_ref, m_ref, ga_ref, geo_ref, mask_ref, first_q_ref,
    act_ref, slope_ref, e0_ref, ro_ref, from_first_ro_ref, one_ref, out0_ref,
    gv_ref, dr_ref, e_ref, gm_ref, x_ref, gy_ref,
):
    early_kernel(turned_ref, second_q_ref, w4_ref, l_ref, m_ref, ga_ref, geo_ref, mask_ref, gv_ref, x_ref, gy_ref)
    expand_kernel(first_q_ref, w4_ref, dr_ref, layer=0)
    own_grads_kernel(act_ref, slope_ref, e0_ref, ro_ref, from_first_ro_ref, one_ref, out0_ref, e_ref, gm_ref)


def back_middle_kernel(gmid_ref, rf_ref, rn_ref, pf_ref, pn_ref, own_ref, f_ref, n_ref):
    mid = gmid_ref[...] + (pick_rows(pf_ref[...], rf_ref[...]) + pick_rows(pn_ref[...], partner_of(rn_ref)))
    own_ref[...] = mid[:64]
    f_ref[...] = mid[64:96]
    n_ref[...] = mid[96:128]


def late_kernel(
    own_ref, rf_ref, rn_ref, tf_ref, tn_ref, gm_ref, outup_ref, gain_ref, amp_ref, turned_ref, dr_ref, l_ref, m_ref, geo_ref,
    mask_ref, dd_ref, early_ref, of_ref, pf_ref, pn_ref, qf_ref, qn_ref, ga_ref, gv_ref, x_ref, gy_ref,
):
    grad = own_ref[...] + (pick_rows(tf_ref[...], rf_ref[...]) + pick_rows(tn_ref[...], rn_ref[...]))
    amp_grads(amp_ref, gain_ref[0], gm_ref[...] + dot3(grad, outup_ref[...], NT), ga_ref)
    for b in range(BLOCKS):
        x = None
        for l, z in enumerate(spread(turned_ref, ga_ref, b)):
            term = z * dr_ref[span(b), l * C : (l + 1) * C]
            x = term if x is None else x + term
        x_ref[span(b), :] = pair_lanes(x * l_ref[span(b), :])
    angular_grads(m_ref, ga_ref, mask_ref, gy_ref)
    edge_forces(x_ref, gy_ref, geo_ref, gv_ref)
    total = gv_ref[...] + early_ref[...]
    at = 0
    for ref in (of_ref, pf_ref, pn_ref, qf_ref, qn_ref):
        rows = ref.shape[1]
        ref[...] = pick_lanes(total, dd_ref[at : at + rows, :], NT)
        at += rows


def collect_plane_kernel(of_ref, pf_ref, pn_ref, rf_ref, rn_ref, tf_ref, tn_ref, o_ref, f_ref, n_ref):
    far, near, at = rf_ref[...], partner_of(rn_ref), 0
    for have_ref, ref in ((of_ref, o_ref), (pf_ref, f_ref), (pn_ref, n_ref)):
        rows = ref.shape[1]
        back = pick_lanes(far, tf_ref[at : at + rows, :], NT) + pick_lanes(near, tn_ref[at : at + rows, :], NT)
        ref[...] = have_ref[...] + back
        at += rows


def collect_slab_kernel(v_ref, rf_ref, rn_ref, tf_ref, tn_ref, o_ref):
    back = pick_lanes(rf_ref[...], tf_ref[...], NT) + pick_lanes(rn_ref[...], tn_ref[...], NT)
    forces = -(v_ref[...] + back)
    for k in range(3):
        o_ref[0, k] = forces[k : k + 1]


def swap_slab_far(value):
    count = lax.axis_size("slab")
    pairs = [(i, i + 1) for i in range(1, count - 1, 2)]
    return lax.ppermute(value, "slab", pairs + [(b, a) for a, b in pairs])


def swap_slab_near(value):
    count = lax.axis_size("slab")
    return lax.ppermute(value, "slab", [(i, i ^ 1) for i in range(count)])


def swap_plane_far(value):
    count = lax.axis_size("plane")
    pairs = [(i, (i + 1) % count) for i in range(1, count, 2)]
    return lax.ppermute(value, "plane", pairs + [(b, a) for a, b in pairs])


def swap_plane_near(value):
    count = lax.axis_size("plane")
    return lax.all_gather(value, "plane", axis_index_groups=[[i, i + 1] for i in range(0, count, 2)])


def both(swap_far, swap_near, far, near):
    return swap_far(far), swap_near(near)


def body(
    positions,
    species,
    slab_sends,
    plane_sends,
    edges,
    edge_count,
    embed_table,
    atom_ref,
    radial_one,
    radial_two,
    radial_three,
    radial_four,
    up_weight,
    skip_weight,
    out_weight,
    prod_weight,
    read_one,
    read_hidden,
    read_out,
):
    edge_mat = ((EDGES, C), f32)
    message_mat = ((3, EDGES, 2 * C), bf16)
    by_degree = ((EDGES, 3 * C), f32)
    edge_rows = ((8, EDGES), f32)
    amp_mat = ((9, OWN, C), f32)
    slab_rows = ((32, C), f32)
    plane_rows = ((64, C), f32)
    own_lanes = ((8, OWN), f32)
    slab_lanes = ((8, 32), f32)
    plane_lanes = ((8, 64), f32)

    with jax.named_scope("atoms_slab"):
        *arguments, values, slab_t_far, slab_t_near, plane_t_far, plane_t_near, far, near = call(
            atoms_slab_kernel,
            [own_lanes, ((OWN, 32), bf16), ((OWN, 32), bf16), ((128, 64), bf16), ((128, 64), bf16), slab_lanes, slab_lanes],
            (jnp.transpose(positions, (0, 2, 1, 3)), species[0], slab_sends[0, 0], plane_sends[0, 0]),
            carried=(
                edges[0, 0], radial_one, radial_two, radial_three, radial_four, embed_table, up_weight, skip_weight,
                atom_ref[None, :], jnp.transpose(read_hidden), read_out[None, :], out_weight, prod_weight, read_one[None, :],
            ),
            name="atoms_slab",
        )
        far, near = both(swap_slab_far, swap_slab_near, far, near)
    with jax.named_scope("prepare"):
        sender_n, sender_t, edge_t, mask, *prepared = call(
            prepare_kernel,
            [((EDGES, EXT), bf16), ((EXT, EDGES), bf16), ((EXT, EDGES), bf16), ((GROUP, EDGES), f32),
             ((2, 64, 32), bf16), ((2, 64, 192), bf16), ((2, 64, 192), bf16), ((2, 192, 3 * C), bf16),
             ((KINDS, 2 * C), bf16), ((KINDS, 3 * C), bf16), ((KINDS, 3 * C), bf16), ((8, KINDS), f32),
             *[((16, C), f32)] * 4, ((C, C), f32), ((C, C), f32), ((2, 4, C), f32), ((1, C), f32), ((8, 16), f32)],
            arguments,
            flops=1_000_000_000,
            name="prepare",
        )
        weights = tuple(prepared[:4])
        (table, skip_table, skip_up_table, ref_row, from_first, from_mix, from_first_ro, from_mix_ro, out_up, out_first,
         gains, read_row, read_last) = prepared[4:]
    with jax.named_scope("atoms_plane"):
        far, near, edge_t = lax.optimization_barrier((far, near, edge_t))
        slab_far, slab_near, far, near = call(
            atoms_plane_kernel,
            [slab_lanes, slab_lanes, plane_lanes, plane_lanes],
            (values, far, near, plane_t_far, plane_t_near),
            name="atoms_plane",
        )
        far, near = both(swap_plane_far, swap_plane_near, far, near)

    hidden_mat = ((16, OWN), f32)
    with jax.named_scope("first_layer"):
        (first, s_far, s_near, mix, amp_first, lift_first, message_first, angular, basis, basis_slope, geo) = call(
            first_kernel,
            [plane_rows, slab_rows, slab_rows, plane_rows, amp_mat, edge_mat, message_mat,
             ((BLOCKS * STACK, SPAN), bf16), edge_rows, edge_rows, edge_rows],
            (values, slab_far, slab_near, far, near, edge_t, sender_n, mask, table, skip_up_table, *weights,
             gains, out_up, slab_t_far, slab_t_near),
            name="first_layer",
        )
    with jax.named_scope("features_slab"):
        slab_far, slab_near = both(swap_slab_far, swap_slab_near, s_far, s_near)
    radial_second, slope_second, slope_first, hidden, energies, turned = call(
        beside_features_kernel,
        [by_degree, ((192, EDGES), bf16), ((192, EDGES), bf16), hidden_mat, own_lanes, ((EDGES, TURNED), bf16)],
        (basis, basis_slope, geo, *weights, values, mix, skip_table, out_first, ref_row, read_row, from_first,
         angular),
        flops=1_000_000_000, name="beside_features",
    )
    with jax.named_scope("features_plane"):
        slab_far, slab_near, radial_second = lax.optimization_barrier((slab_far, slab_near, radial_second))
        far, near = call(
            middle_kernel, [plane_rows] * 2, (first, slab_far, slab_near, plane_t_far, plane_t_near), name="middle"
        )
        far, near = both(swap_plane_far, swap_plane_near, far, near)
    with jax.named_scope("second_layer"):
        act, slope, gmid, far, near, lift_second, message_second, ga = call(
            second_kernel,
            [hidden_mat, hidden_mat, ((128, C), f32), plane_rows, plane_rows, edge_mat, message_mat, amp_mat],
            (first, slab_far, slab_near, far, near, sender_n, sender_t, angular, turned, radial_second, gains, hidden, from_mix,
             from_mix_ro),
            scratch=[pltpu.VMEM((9, OWN, C), f32), pltpu.VMEM((EDGES, 2 * C), bf16)],
            name="second_layer",
        )
    with jax.named_scope("feature_grads_plane"):
        far, near = both(swap_plane_far, swap_plane_near, far, near)
    with jax.named_scope("feature_grads_slab"):
        own, far, near = call(
            back_middle_kernel, [plane_rows, slab_rows, slab_rows], (gmid, far, near, plane_t_far, plane_t_near),
            name="back_middle",
        )
        far, near, ga = lax.optimization_barrier((far, near, ga))
        far, near = both(swap_slab_far, swap_slab_near, far, near)
    early, slope_first, energies, own_grads = call(
        beside_grads_kernel,
        [edge_rows, by_degree, ((1, OWN), f32), plane_rows],
        (turned, slope_second, weights[3], lift_second, message_second, ga, geo, mask, slope_first,
         act, slope, energies, read_last, from_first_ro, read_row, out_first),
        scratch=[pltpu.VMEM((EDGES, 2 * C), bf16), pltpu.VMEM((8, EDGES), f32)],
        flops=1_000_000_000, name="beside_grads",
    )
    with jax.named_scope("late_forces"):
        own, slab_far, slab_near, far, near = call(
            late_kernel,
            [own_lanes, slab_lanes, slab_lanes, plane_lanes, plane_lanes],
            (own, far, near, slab_t_far, slab_t_near, own_grads, out_up, gains, amp_first, turned, slope_first,
             lift_first, message_first, geo, mask, edge_t, early),
            scratch=[pltpu.VMEM((9, OWN, C), f32), pltpu.VMEM((8, EDGES), f32), pltpu.VMEM((EDGES, 2 * C), bf16),
                     pltpu.VMEM((8, EDGES), f32)],
            name="late_forces",
        )
    with jax.named_scope("position_grads_plane"):
        far, near = both(swap_plane_far, swap_plane_near, far, near)
        own, far, near = call(
            collect_plane_kernel, [own_lanes, slab_lanes, slab_lanes],
            (own, slab_far, slab_near, far, near, plane_t_far, plane_t_near), name="collect_plane",
        )
    with jax.named_scope("position_grads_slab"):
        far, near = both(swap_slab_far, swap_slab_near, far, near)
        forces, = call(
            collect_slab_kernel, [((1, 3, 1, OWN), f32)], (own, far, near, slab_t_far, slab_t_near), name="collect_slab",
        )
    return (energies[None], jnp.transpose(forces, (0, 2, 1, 3)))


def solution(mesh):
    in_specs = (
        P("slab", "plane", None, None),
        P("slab", "plane", None),
        P("slab", "plane", None, None),
        P("slab", "plane", None, None),
        P("slab", "plane", None, None),
        P("slab", "plane"),
    ) + (P(),) * 13
    out_specs = (P("slab", "plane", None), P("slab", "plane", None, None))
    return jax.shard_map(body, mesh=mesh, in_specs=in_specs, out_specs=out_specs, check_vma=False)
```
